32 devices in a mesh: gy: 4 (over x, core), gx: 2 (over y), rep: 4 (over z).
Axes of the slice: x: 2, y: 2, z: 4, core: 2. Of those that a mesh axis runs over, the one named last changes fastest.
Arguments:
- pages: bfloat16 [4, 128, 64, 384], P('rep', 'gy', 'gx'), may hold values from -6 to 6
- cotangent: bfloat16 [4, 128, 64, 384], P('rep', 'gy', 'gx'), may hold values from -6 to 6
- conv_kernel: float32 [7, 7, 384], replicated, may hold values from -0.875 to 0.875
- conv_bias: float32 [384], replicated, may hold values from -3 to 3
- norm_gain: float32 [384], replicated, may hold values from 0.1 to 1.9
- norm_bias: float32 [384], replicated, may hold values from -3 to 3
- w_in: bfloat16 [1536, 384], replicated, may hold values from -0.3125 to 0.3125
- b_in: float32 [1536], replicated, may hold values from -3 to 3
- w_out: bfloat16 [384, 1536], replicated, may hold values from -0.15625 to 0.15625
- b_out: float32 [384], replicated, may hold values from -3 to 3
- layer_scale: float32 [384], replicated, may hold values from 0.2 to 2
Outputs:
- result: bfloat16 [4, 128, 64, 384], P('rep', 'gy', 'gx')
- grad_pages: bfloat16 [4, 128, 64, 384], P('rep', 'gy', 'gx')
- grad_kernel: float32 [7, 7, 384], replicated
- grad_conv_bias: float32 [384], replicated
- grad_gain: float32 [384], replicated
- grad_norm_bias: float32 [384], replicated
- grad_w_in: float32 [1536, 384], replicated
- grad_b_in: float32 [1536], replicated
- grad_w_out: float32 [384, 1536], replicated
- grad_b_out: float32 [384], replicated
- grad_scale: float32 [384], replicated
The draws below stay inside these ranges and needn't reach their ends.
All inputs are finite; a program needn't handle non-finite values.
Results may differ from the reference program's by a relative error of at most 0.0095.
Values may be sent and summed in bfloat16 or wider, within the bound.
No kernel may reach another device: no remote copies, remote signals or barrier semaphores. Data moves between devices by JAX's collectives and lax.ppermute only.
A program may use at most 128 MiB of HBM per device.

```python
import math
import jax
import jax.numpy as jnp
from jax import lax

C = 384
HID = 1536
H = 128
W = 64
PAGES = 4
PIXELS = 32768


def shard_levels(rng, shape, pieces, low, top_value):
    loudness = 1.0
    for axis_at, parts in pieces:
        heights = jax.random.uniform(jax.random.fold_in(jax.random.fold_in(rng, 6), axis_at), (parts,), jnp.float32, low / len(pieces), top_value / len(pieces))
        loudness = loudness * jnp.repeat(jnp.exp(heights), shape[axis_at] // parts).reshape((-1,) + (1,) * (len(shape) - 1 - axis_at))
    return loudness


def noise(key, shape, deviation, bound, pieces=(), dtype=jnp.bfloat16):
    values = deviation * jax.random.normal(key, shape, jnp.float32)
    if pieces:
        values = values * shard_levels(key, shape, pieces, -0.22, 0.18)
    return jnp.clip(values, -bound, bound).astype(dtype)


def setup_inputs(seed: int = 0) -> dict:
    splits = jax.random.split(jax.random.key(seed), 12)
    return {
        "pages": noise(splits[0], (PAGES, H, W, C), 1.0, 6.0, ((0, 4), (1, 4), (2, 2))),
        "cotangent": noise(splits[1], (PAGES, H, W, C), 1.0, 6.0, ((0, 4), (1, 4), (2, 2))),
        "conv_kernel": noise(splits[2], (7, 7, C), 49 ** -0.5, 0.875, (), jnp.float32),
        "conv_bias": noise(splits[3], (C,), 0.5, 3.0, (), jnp.float32),
        "norm_gain": jnp.clip(1.0 + 0.18 * jax.random.normal(splits[4], (C,), jnp.float32), 0.1, 1.9),
        "norm_bias": noise(splits[5], (C,), 0.5, 3.0, (), jnp.float32),
        "w_in": noise(splits[6], (HID, C), C ** -0.5, 0.3125),
        "b_in": noise(splits[7], (HID,), 0.5, 3.0, (), jnp.float32),
        "w_out": noise(splits[8], (C, HID), HID ** -0.5, 0.15625),
        "b_out": noise(splits[9], (C,), 0.5, 3.0, (), jnp.float32),
        "layer_scale": jnp.clip(jnp.exp(jax.random.uniform(splits[10], (C,), jnp.float32, math.log(0.2), math.log(2.0))), 0.2, 2.0),
    }


norm_epsilon = 1e-06
inv_root_two = 0.7071067811865476
inv_root_tau = 0.3989422804014327

def gelu_grad(values):
    cdf = 0.5 * (1.0 + lax.erf(values * inv_root_two))
    pdf = jnp.exp(-0.5 * values * values) * inv_root_tau
    return cdf + values * pdf

def reference(pages, cotangent, conv_kernel, conv_bias, norm_gain, norm_bias, w_in, b_in, w_out, b_out, layer_scale):
    channels = pages.shape[3]

    def one_page(inputs):
        page, cot = inputs
        padded = jnp.pad(page, ((3, 3), (3, 3), (0, 0)))
        accum = jnp.zeros(page.shape, jnp.float32)
        for row_off in range(7):
            for col_off in range(7):
                accum = accum + padded[row_off:row_off + H, col_off:col_off + W, :].astype(jnp.float32) * conv_kernel[row_off, col_off]
        depth_out = accum + conv_bias
        average = lax.optimization_barrier(jnp.mean(depth_out, axis=-1, keepdims=True))
        centred = depth_out - average
        inv_std = lax.rsqrt(lax.optimization_barrier(jnp.mean(centred * centred, axis=-1, keepdims=True)) + norm_epsilon)
        normed = (centred * inv_std).reshape(-1, channels)
        inv_rows = inv_std.reshape(-1, 1)
        ln_out = (normed * norm_gain + norm_bias).astype(jnp.bfloat16)
        pre_act = lax.dot_general(ln_out, w_in, (((1,), (1,)), ((), ())), preferred_element_type=jnp.float32) + b_in
        hidden = jax.nn.gelu(pre_act, approximate=False).astype(jnp.bfloat16)
        branch = lax.dot_general(hidden, w_out, (((1,), (1,)), ((), ())), preferred_element_type=jnp.float32) + b_out
        page_rows = page.reshape(-1, channels).astype(jnp.float32)
        result = (page_rows + layer_scale * branch).astype(jnp.bfloat16).reshape(page.shape)
        cot_rows = cot.reshape(-1, channels).astype(jnp.float32)
        g_scale = lax.optimization_barrier(jnp.sum(cot_rows * branch, axis=0))
        d_branch32 = layer_scale * cot_rows
        g_bout = lax.optimization_barrier(jnp.sum(d_branch32, axis=0))
        d_branch = d_branch32.astype(jnp.bfloat16)
        g_wout = lax.dot_general(d_branch, hidden, (((0,), (0,)), ((), ())), preferred_element_type=jnp.float32)
        d_hidden = jnp.dot(d_branch, w_out, preferred_element_type=jnp.float32)
        d_pre32 = d_hidden * gelu_grad(pre_act)
        g_bin = lax.optimization_barrier(jnp.sum(d_pre32, axis=0))
        d_pre = d_pre32.astype(jnp.bfloat16)
        g_win = lax.dot_general(d_pre, ln_out, (((0,), (0,)), ((), ())), preferred_element_type=jnp.float32)
        d_norm = jnp.dot(d_pre, w_in, preferred_element_type=jnp.float32)
        g_gain = lax.optimization_barrier(jnp.sum(d_norm * normed, axis=0))
        g_nbias = lax.optimization_barrier(jnp.sum(d_norm, axis=0))
        d_scaled = d_norm * norm_gain
        d_depth32 = inv_rows * (d_scaled - lax.optimization_barrier(jnp.mean(d_scaled, axis=-1, keepdims=True)) - normed * lax.optimization_barrier(jnp.mean(d_scaled * normed, axis=-1, keepdims=True)))
        d_depth = d_depth32.astype(jnp.bfloat16).reshape(page.shape)
        depth_f = d_depth.astype(jnp.float32)
        g_cbias = lax.optimization_barrier(jnp.sum(depth_f, axis=(0, 1)))
        kernel_terms = []
        for row_off in range(7):
            for col_off in range(7):
                piece = padded[row_off:row_off + H, col_off:col_off + W, :].astype(jnp.float32)
                kernel_terms.append(lax.optimization_barrier(jnp.sum(depth_f * piece, axis=(0, 1))))
        g_kernel = jnp.stack(kernel_terms).reshape(7, 7, channels)
        grad_pad = jnp.pad(d_depth, ((3, 3), (3, 3), (0, 0)))
        back = jnp.zeros(page.shape, jnp.float32)
        for row_off in range(7):
            for col_off in range(7):
                back = back + grad_pad[6 - row_off:6 - row_off + H, 6 - col_off:6 - col_off + W, :].astype(jnp.float32) * conv_kernel[row_off, col_off]
        grad_page = (cot.astype(jnp.float32) + back).astype(jnp.bfloat16)
        return (result, grad_page, (g_kernel, g_cbias, g_gain, g_nbias, g_win, g_bin, g_wout, g_bout, g_scale))
    result, grad_pages, partials = lax.map(one_page, (pages, cotangent))
    factor = float(PIXELS) ** (-0.5)
    totals = [lax.optimization_barrier(jnp.sum(term, axis=0)) * factor for term in partials]
    return (result, grad_pages, totals[0], totals[1], totals[2], totals[3], totals[4], totals[5], totals[6], totals[7], totals[8])
```

```python
import functools

import jax
import jax.numpy as jnp
from jax import lax
from jax.experimental import pallas as pl
from jax.experimental.pallas import tpu as pltpu
from jax.sharding import PartitionSpec as P

norm_epsilon = 1e-06
inv_root_two = 0.7071067811865476
inv_root_tau = 0.3989422804014327

LANES = 128
EDGE = 8
BAND = 16
AXES = ("gy", "gx", "rep")
f32 = jnp.float32
bf16 = jnp.bfloat16


def dot(a, b, dims):
    return lax.dot_general(a, b, (dims, ((), ())), preferred_element_type=f32)


NN = ((1,), (0,))
NT = ((1,), (1,))
TN = ((0,), (0,))


def pair_rounds(count):
    first = [(i, i + 1) for i in range(0, count - 1, 2)]
    second = [(i, i + 1) for i in range(1, count - 1, 2)]
    return [pairs + [(b, a) for a, b in pairs] for pairs in (first, second)]


def edges(block, axis, dim, width):
    size = block.shape[dim]
    even = lax.axis_index(axis) % 2 == 0
    low = lax.slice_in_dim(block, 0, width, axis=dim)
    high = lax.slice_in_dim(block, size - width, size, axis=dim)
    out = []
    for pairs, is_high in zip(pair_rounds(lax.axis_size(axis)), (even, ~even)):
        if pairs:
            out.append(lax.ppermute(jnp.where(is_high, high, low), axis, pairs))
        else:
            out.append(jnp.zeros_like(low))
    return out


def halo(tile):
    rows = edges(tile, "gy", 0, 3)
    even = lax.axis_index("gy") % 2 == 0
    top = jnp.where(even, rows[1], rows[0])
    bottom = jnp.where(even, rows[0], rows[1])
    even_x = lax.axis_index("gx") % 2 == 0
    size = tile.shape[1]
    column = [jnp.concatenate([part[:, :3], part[:, size - 3 :]], axis=1) for part in (top, tile, bottom)]
    column = jnp.concatenate(column, axis=0)
    out = []
    for pairs, is_high in zip(pair_rounds(lax.axis_size("gx")), (even_x, ~even_x)):
        if pairs:
            out.append(lax.ppermute(jnp.where(is_high, column[:, 3:], column[:, :3]), "gx", pairs))
        else:
            out.append(jnp.zeros_like(column[:, :3]))
    left = jnp.where(even_x, out[1], out[0])
    right = jnp.where(even_x, out[0], out[1])
    return top, bottom, left, right


def fill(pad, tile, top, bottom, left, right):
    rows, cols, channels = tile.shape
    for slab in range(channels // LANES):
        at = slice(slab * LANES, (slab + 1) * LANES)
        pad[slab, 0:3, EDGE : EDGE + cols, :] = top[:, :, at].astype(f32)
        pad[slab, 3 + rows :, EDGE : EDGE + cols, :] = bottom[:, :, at].astype(f32)
        pad[slab, :, EDGE - 3 : EDGE, :] = left[:, :, at].astype(f32)
        pad[slab, :, EDGE + cols : EDGE + cols + 3, :] = right[:, :, at].astype(f32)

        def body(row, _):
            pad[slab, row + 3, EDGE : EDGE + cols, :] = tile[row, :, at].astype(f32)
            return _

        lax.fori_loop(0, rows, body, 0, unroll=4)


def steps(rows, cols, channels, body):
    slabs, tiles, bands = channels // LANES, cols // 8, rows // BAND

    def step(i, _):
        slab = i // (tiles * bands)
        rest = i % (tiles * bands)
        body(slab, pl.multiple_of(rest // bands * 8, 8), rest % bands * BAND)
        return _

    lax.fori_loop(0, slabs * tiles * bands, step, 0)


def lanes(slab):
    return pl.ds(pl.multiple_of(slab * LANES, LANES), LANES)


def taps(pad, kernel, slab, col, row, flip):
    acc = [None] * BAND
    for b in range(7):
        scale = []
        for a in range(7):
            tap = (6 - a) * 7 + 6 - b if flip else a * 7 + b
            scale.append(jnp.broadcast_to(kernel[pl.ds(tap, 1), lanes(slab)], (8, LANES)))
        for r in range(BAND + 6):
            x = pad[slab, row + r, pl.ds(col + EDGE - 3 + b, 8), :]
            for a in range(7):
                i = r - a
                if 0 <= i < BAND:
                    acc[i] = x * scale[a] if acc[i] is None else acc[i] + x * scale[a]
    return acc


def conv_norm_kernel(
    tile, top, bottom, left, right, kernel, bias, gain, shift, normed_ref, inv_ref, ln_ref, pad, depth
):
    rows, cols, channels = tile.shape
    fill(pad, tile, top, bottom, left, right)

    def piece(slab, col, row):
        acc = taps(pad, kernel, slab, col, row, False)
        add = jnp.broadcast_to(bias[:, lanes(slab)], (8, LANES))
        for i in range(BAND):
            at = pl.ds(pl.multiple_of((row + i) * cols + col, 8), 8)
            depth[at, lanes(slab)] = acc[i] + add

    steps(rows, cols, channels, piece)
    block = 128

    def norm(i, _):
        at = pl.ds(pl.multiple_of(i * block, block), block)
        x = depth[at, :]
        centred = x - jnp.mean(x, axis=-1, keepdims=True)
        inv = lax.rsqrt(jnp.mean(centred * centred, axis=-1, keepdims=True) + norm_epsilon)
        normed = centred * inv
        normed_ref[at, :] = normed
        inv_ref[at, :] = jnp.broadcast_to(inv, (block, LANES))
        ln_ref[at, :] = (normed * gain[...] + shift[...]).astype(bf16)
        return _

    lax.fori_loop(0, rows * cols // block, norm, 0)


def gelu_pair(u):
    cdf = 0.5 * (1.0 + lax.erf(u * inv_root_two))
    pdf = jnp.exp(-0.5 * u * u) * inv_root_tau
    return u * cdf, cdf + u * pdf


def fold(x):
    return jnp.sum(x.reshape(-1, 8, x.shape[1]), axis=0)


def mlp_block(ln, d_branch, w_in, w_out, b_in, base, width, hid_ref, dpre_ref, gbin):
    sub = 256
    count = width // sub

    def products(s):
        at = pl.ds(base + s * sub, sub)
        return dot(ln, w_in[at, :], NT), dot(d_branch, w_out[:, at], NN)

    ahead = products(0)
    for s in range(count):
        pre, d_hidden = ahead
        if s + 1 < count:
            ahead = products(s + 1)
        act, slope = gelu_pair(pre + b_in[:, base + s * sub : base + (s + 1) * sub])
        d_pre = d_hidden * slope
        gbin[:, s * sub : (s + 1) * sub] += fold(d_pre)
        hid_ref[:, s * sub : (s + 1) * sub] = act.astype(bf16)
        dpre_ref[:, s * sub : (s + 1) * sub] = d_pre.astype(bf16)
    at = pl.ds(base, width)
    hidden, d_pre = hid_ref[...], dpre_ref[...]
    branch = dot(hidden, w_out[:, at], NT)
    d_norm = dot(d_pre, w_in[at, :], NN)
    return hidden, d_pre, branch, d_norm


def pack_grads(pack, gwin, gwout, gbin_ref, gbin):
    width, channels = gwin.shape
    pack[0:width, :] = gwin[...].astype(bf16)
    for j in range(width // channels):
        pack[width + j * channels : width + (j + 1) * channels, :] = gwout[
            :, j * channels : (j + 1) * channels
        ].astype(bf16)
    gbin_ref[...] = jnp.sum(gbin[...], axis=0, keepdims=True)


MLP_BLOCK = 256


def mlp_first_kernel(
    base, width, ln_ref, cot, w_in, w_out, b_in, scale, branch_ref, dnorm_ref, pack, gbin_ref,
    hid_ref, dpre_ref, gwin, gwout, gbin,
):
    gwin[...] = jnp.zeros_like(gwin)
    gwout[...] = jnp.zeros_like(gwout)
    gbin[...] = jnp.zeros_like(gbin)

    def step(i, _):
        at = pl.ds(pl.multiple_of(i * MLP_BLOCK, MLP_BLOCK), MLP_BLOCK)
        ln = ln_ref[at, :]
        d_branch = (scale[...] * cot[at, :].astype(f32)).astype(bf16)
        hidden, d_pre, branch, d_norm = mlp_block(
            ln, d_branch, w_in, w_out, b_in, base, width, hid_ref, dpre_ref, gbin
        )
        branch_ref[at, :] = branch
        dnorm_ref[at, :] = d_norm
        gwin[...] += dot(d_pre, ln, TN)
        gwout[...] += dot(d_branch, hidden, TN)
        return _

    lax.fori_loop(0, ln_ref.shape[0] // MLP_BLOCK, step, 0)
    pack_grads(pack, gwin, gwout, gbin_ref, gbin)


def mlp_second_kernel(
    base, width, ln_ref, cot, w_in, w_out, b_in, scale, b_out, gain, page, normed_ref, inv_ref,
    branch_ref, dnorm_ref,
    result, d_depth_ref, pack, gbin_ref, sums_ref,
    hid_ref, dpre_ref, gwin, gwout, gbin, sums,
):
    gwin[...] = jnp.zeros_like(gwin)
    gwout[...] = jnp.zeros_like(gwout)
    gbin[...] = jnp.zeros_like(gbin)
    sums[...] = jnp.zeros_like(sums)

    def step(i, _):
        at = pl.ds(pl.multiple_of(i * MLP_BLOCK, MLP_BLOCK), MLP_BLOCK)
        ln = ln_ref[at, :]
        cot32 = cot[at, :].astype(f32)
        d_branch32 = scale[...] * cot32
        d_branch = d_branch32.astype(bf16)
        hidden, d_pre, branch, d_norm = mlp_block(
            ln, d_branch, w_in, w_out, b_in, base, width, hid_ref, dpre_ref, gbin
        )
        gwin[...] += dot(d_pre, ln, TN)
        gwout[...] += dot(d_branch, hidden, TN)
        branch = branch + branch_ref[at, :] + b_out[...]
        result[at, :] = (page[at, :].astype(f32) + scale[...] * branch).astype(bf16)
        d_norm = d_norm + dnorm_ref[at, :]
        normed = normed_ref[at, :]
        inv = inv_ref[at, 0:1]
        weighted = d_norm * normed
        s = d_norm * gain[...]
        mean_s = jnp.mean(s, axis=-1, keepdims=True)
        mean_sn = jnp.mean(s * normed, axis=-1, keepdims=True)
        d_depth = (inv * (s - mean_s - normed * mean_sn)).astype(bf16)
        d_depth_ref[at, :] = d_depth
        sums[0] += fold(cot32 * branch)
        sums[1] += fold(d_branch32)
        sums[2] += fold(weighted)
        sums[3] += fold(d_norm)
        sums[4] += fold(d_depth.astype(f32))
        return _

    lax.fori_loop(0, ln_ref.shape[0] // MLP_BLOCK, step, 0)
    pack_grads(pack, gwin, gwout, gbin_ref, gbin)
    for j in range(5):
        sums_ref[j : j + 1, :] = jnp.sum(sums[j], axis=0, keepdims=True)


def kernel_grad_kernel(tile, top, bottom, left, right, d_depth, out, pad, d32, acc_ref):
    rows, cols, channels = tile.shape
    fill(pad, tile, top, bottom, left, right)
    d32[...] = d_depth[...].astype(f32)
    acc_ref[...] = jnp.zeros_like(acc_ref)

    def piece(slab, col, row):
        grads = []
        for i in range(BAND):
            at = pl.ds(pl.multiple_of((row + i) * cols + col, 8), 8)
            grads.append(d32[at, lanes(slab)])
        for b in range(7):
            acc = [None] * 7
            for r in range(BAND + 6):
                x = pad[slab, row + r, pl.ds(col + EDGE - 3 + b, 8), :]
                for a in range(7):
                    i = r - a
                    if 0 <= i < BAND:
                        acc[a] = x * grads[i] if acc[a] is None else acc[a] + x * grads[i]
            for a in range(7):
                acc_ref[slab, a * 7 + b] += acc[a]

    steps(rows, cols, channels, piece)
    for slab in range(channels // LANES):
        out[:, slab * LANES : (slab + 1) * LANES] = jnp.sum(acc_ref[slab], axis=1)


def conv_grad_kernel(tile, top, bottom, left, right, kernel, cot, out, pad, total):
    rows, cols, channels = tile.shape
    fill(pad, tile, top, bottom, left, right)

    def piece(slab, col, row):
        acc = taps(pad, kernel, slab, col, row, True)
        for i in range(BAND):
            at = pl.ds(pl.multiple_of((row + i) * cols + col, 8), 8)
            total[at, lanes(slab)] = acc[i]

    steps(rows, cols, channels, piece)
    block = 128

    def finish(i, _):
        at = pl.ds(pl.multiple_of(i * block, block), block)
        out[at, :] = (cot[at, :].astype(f32) + total[at, :]).astype(bf16)
        return _

    lax.fori_loop(0, rows * cols // block, finish, 0)


def call(body, outs, scratch, args, flops, size=24 << 20):
    vmem = pl.BlockSpec(memory_space=pltpu.VMEM)
    return pl.pallas_call(
        body,
        out_shape=[jax.ShapeDtypeStruct(shape, dtype) for shape, dtype in outs],
        in_specs=[vmem] * len(args),
        out_specs=[vmem] * len(outs),
        scratch_shapes=[pltpu.VMEM(shape, dtype) for shape, dtype in scratch],
        compiler_params=pltpu.CompilerParams(vmem_limit_bytes=size),
        cost_estimate=pl.CostEstimate(flops=flops, bytes_accessed=1 << 20, transcendentals=0),
    )(*args)


def bits(count):
    return max(count.bit_length() - 1, 0)


def sum_plan():
    plan = [("gy", 0)]
    rest = [("gy", j) for j in range(1, bits(lax.axis_size("gy")))]
    wide = [("gx", j) for j in range(bits(lax.axis_size("gx")))]
    deep = [("rep", j) for j in range(bits(lax.axis_size("rep")))]
    first = rest + wide + deep
    second = wide + rest + deep
    return [(plan[0], plan[0])] + list(zip(first, second))


def exchange(x, choice):
    sizes = [lax.axis_size(axis) for axis in AXES]
    perm = []
    for i in range(sizes[0] * sizes[1] * sizes[2]):
        at = {"gy": i // (sizes[1] * sizes[2]), "gx": i // sizes[2] % sizes[1], "rep": i % sizes[2]}
        axis, bit = choice[at["gy"] % 2]
        at[axis] ^= 1 << bit
        perm.append((i, (at["gy"] * sizes[1] + at["gx"]) * sizes[2] + at["rep"]))
    return lax.ppermute(x, AXES, perm)


def own_bit(choice):
    core = lax.axis_index("gy") % 2
    values = [lax.axis_index(axis) // (1 << bit) % 2 for axis, bit in choice]
    return jnp.where(core == 0, values[0], values[1])


def sum_scatter(x):
    for choice in sum_plan():
        bit = own_bit(choice)
        halves = x.reshape(2, x.shape[0] // 2, x.shape[1])
        keep = lax.dynamic_index_in_dim(halves, bit, 0, keepdims=False)
        send = lax.dynamic_index_in_dim(halves, 1 - bit, 0, keepdims=False)
        x = (keep.astype(f32) + exchange(send, choice).astype(f32)).astype(bf16)
    return x


def gather_back(x):
    for choice in reversed(sum_plan()):
        bit = own_bit(choice)
        other = exchange(x, choice)
        x = jnp.where(bit == 0, jnp.concatenate([x, other]), jnp.concatenate([other, x]))
    return x


def gather_call(x):
    plan = sum_plan()
    sizes = [lax.axis_size(axis) for axis in AXES]
    got = lax.all_gather(x, AXES)
    dims, place = [], {}
    for axis, size in zip(AXES, sizes):
        for j in reversed(range(bits(size))):
            place[(axis, j)] = len(dims)
            dims.append(2)
    got = got.reshape(*dims, *x.shape)
    parts = []
    for core in range(2):
        half = lax.index_in_dim(got, core, place[("gy", 0)], keepdims=True)
        order = [place[choice[core]] for choice in plan]
        parts.append(half.transpose(*order, len(dims), len(dims) + 1))
    return jnp.concatenate(parts).reshape(-1, x.shape[1])


def shards(
    pages,
    cotangent,
    conv_kernel,
    conv_bias,
    norm_gain,
    norm_bias,
    w_in,
    b_in,
    w_out,
    b_out,
    layer_scale,
):
    _, rows, cols, channels = pages.shape
    hid = w_in.shape[0]
    width = hid // 2
    pixels = rows * cols
    tile = pages.reshape(rows, cols, channels)
    page = pages.reshape(pixels, channels)
    cot = cotangent.reshape(pixels, channels)
    kernel = conv_kernel.reshape(49, channels)
    row = lambda v: v.reshape(1, -1)
    gain, shift, scale = row(norm_gain), row(norm_bias), row(layer_scale)
    pad = ((channels // LANES, rows + 6, EDGE + cols + 8, LANES), f32)
    full = (pixels, channels)

    around = halo(tile)
    conv_flops = 2 * 49 * pixels * channels * 60
    normed, inv, ln_out = call(
        conv_norm_kernel,
        [(full, f32), ((pixels, LANES), f32), (full, bf16)],
        [pad, (full, f32)],
        (tile, *around, kernel, row(conv_bias), gain, shift),
        conv_flops,
    )
    grads = [
        ((MLP_BLOCK, width), bf16),
        ((MLP_BLOCK, width), bf16),
        ((width, channels), f32),
        ((channels, width), f32),
        ((8, width), f32),
    ]
    packed = ((2 * width, channels), bf16)
    mlp_flops = 6 * pixels * channels * hid * 2
    weights = (w_in, w_out, row(b_in), scale)
    branch, d_norm, pack_a, gbin_a = call(
        functools.partial(mlp_first_kernel, 0, width),
        [(full, f32), (full, f32), packed, ((1, width), f32)],
        grads,
        (ln_out, cot, *weights),
        mlp_flops,
    )
    piece_a = sum_scatter(pack_a)
    result, d_depth, pack_b, gbin_b, sums = call(
        functools.partial(mlp_second_kernel, width, width),
        [(full, bf16), (full, bf16), packed, ((1, width), f32), ((8, channels), f32)],
        grads + [((8, 8, channels), f32)],
        (ln_out, cot, *weights, row(b_out), gain, page, normed, inv, branch, d_norm),
        mlp_flops,
    )
    piece_b = sum_scatter(pack_b)
    d_tile = d_depth.reshape(tile.shape)
    d_around = halo(d_tile)
    (g_kernel,) = call(
        kernel_grad_kernel,
        [((49, channels), f32)],
        [pad, (full, f32), ((channels // LANES, 49, 8, LANES), f32)],
        (tile, *around, d_depth),
        conv_flops,
    )
    small = jnp.concatenate(
        [g_kernel, sums[:5], gbin_a.reshape(-1, channels), gbin_b.reshape(-1, channels)]
    )
    (grad_pages,) = call(
        conv_grad_kernel,
        [(full, bf16)],
        [pad, (full, f32)],
        (d_tile, *d_around, kernel, cot),
        conv_flops,
    )
    factor = float(pixels * lax.axis_size("gy") * lax.axis_size("gx") * lax.axis_size("rep")) ** (-0.5)
    small = lax.psum(small, AXES) * factor
    both = [gather_back(piece_a), gather_call(piece_b)]
    sum_win = jnp.concatenate([g[:width] for g in both]).astype(f32) * factor
    blocks = [g[width + j * channels : width + (j + 1) * channels] for g in both for j in range(width // channels)]
    sum_wout = jnp.concatenate(blocks, axis=1).astype(f32) * factor
    return (
        result.reshape(pages.shape),
        grad_pages.reshape(pages.shape),
        small[:49].reshape(7, 7, channels),
        small[53],
        small[51],
        small[52],
        sum_win,
        small[54:].reshape(-1),
        sum_wout,
        small[50],
        small[49],
    )


def solution(mesh):
    split = P("rep", "gy", "gx", None)
    return jax.shard_map(
        shards,
        mesh=mesh,
        in_specs=(split, split) + (P(),) * 9,
        out_specs=(split, split) + (P(),) * 9,
        check_vma=False,
    )
```

```python
import functools
import math

import jax
import jax.numpy as jnp
from jax import lax
from jax.experimental import pallas as pl
from jax.experimental.pallas import tpu as pltpu
from jax.sharding import PartitionSpec as P

norm_epsilon = 1e-06
inv_root_two = 0.7071067811865476
inv_root_tau = 0.3989422804014327

LANES = 128
EDGE = 8
BAND = 16
AXES = ("gy", "gx", "rep")
f32 = jnp.float32
bf16 = jnp.bfloat16


def dot(a, b, dims):
    return lax.dot_general(a, b, (dims, ((), ())), preferred_element_type=f32)


NN = ((1,), (0,))
NT = ((1,), (1,))
TN = ((0,), (0,))


def pair_rounds(count):
    first = [(i, i + 1) for i in range(0, count - 1, 2)]
    second = [(i, i + 1) for i in range(1, count - 1, 2)]
    return [pairs + [(b, a) for a, b in pairs] for pairs in (first, second)]


def edges(block, axis, dim, width):
    size = block.shape[dim]
    even = lax.axis_index(axis) % 2 == 0
    low = lax.slice_in_dim(block, 0, width, axis=dim)
    high = lax.slice_in_dim(block, size - width, size, axis=dim)
    out = []
    for pairs, is_high in zip(pair_rounds(lax.axis_size(axis)), (even, ~even)):
        if pairs:
            out.append(lax.ppermute(jnp.where(is_high, high, low), axis, pairs))
        else:
            out.append(jnp.zeros_like(low))
    return out


def halo(tile):
    rows = edges(tile, "gy", 0, 3)
    even = lax.axis_index("gy") % 2 == 0
    top = jnp.where(even, rows[1], rows[0])
    bottom = jnp.where(even, rows[0], rows[1])
    even_x = lax.axis_index("gx") % 2 == 0
    size = tile.shape[1]
    column = [jnp.concatenate([part[:, :3], part[:, size - 3 :]], axis=1) for part in (top, tile, bottom)]
    column = jnp.concatenate(column, axis=0)
    out = []
    for pairs, is_high in zip(pair_rounds(lax.axis_size("gx")), (even_x, ~even_x)):
        if pairs:
            out.append(lax.ppermute(jnp.where(is_high, column[:, 3:], column[:, :3]), "gx", pairs))
        else:
            out.append(jnp.zeros_like(column[:, :3]))
    left = jnp.where(even_x, out[1], out[0])
    right = jnp.where(even_x, out[0], out[1])
    return top, bottom, left, right


def fill(pad, tile, top, bottom, left, right):
    rows, cols, channels = tile.shape
    for slab in range(channels // LANES):
        at = slice(slab * LANES, (slab + 1) * LANES)
        pad[slab, 0:3, EDGE : EDGE + cols, :] = top[:, :, at].astype(f32)
        pad[slab, 3 + rows :, EDGE : EDGE + cols, :] = bottom[:, :, at].astype(f32)
        pad[slab, :, EDGE - 3 : EDGE, :] = left[:, :, at].astype(f32)
        pad[slab, :, EDGE + cols : EDGE + cols + 3, :] = right[:, :, at].astype(f32)

        def body(row, _):
            pad[slab, row + 3, EDGE : EDGE + cols, :] = tile[row, :, at].astype(f32)
            return _

        lax.fori_loop(0, rows, body, 0, unroll=4)


def steps(rows, cols, channels, body):
    slabs, tiles, bands = channels // LANES, cols // 8, rows // BAND

    def step(i, _):
        slab = i // (tiles * bands)
        rest = i % (tiles * bands)
        body(slab, pl.multiple_of(rest // bands * 8, 8), rest % bands * BAND)
        return _

    lax.fori_loop(0, slabs * tiles * bands, step, 0)


def lanes(slab):
    return pl.ds(pl.multiple_of(slab * LANES, LANES), LANES)


def taps(pad, kernel, slab, col, row, flip):
    acc = [None] * BAND
    for b in range(7):
        scale = []
        for a in range(7):
            tap = (6 - a) * 7 + 6 - b if flip else a * 7 + b
            scale.append(jnp.broadcast_to(kernel[pl.ds(tap, 1), lanes(slab)], (8, LANES)))
        for r in range(BAND + 6):
            x = pad[slab, row + r, pl.ds(col + EDGE - 3 + b, 8), :]
            for a in range(7):
                i = r - a
                if 0 <= i < BAND:
                    acc[i] = x * scale[a] if acc[i] is None else acc[i] + x * scale[a]
    return acc


def conv_norm_kernel(
    tile, top, bottom, left, right, kernel, bias, gain, shift, normed_ref, inv_ref, ln_ref, pad, depth
):
    rows, cols, channels = tile.shape
    fill(pad, tile, top, bottom, left, right)

    def piece(slab, col, row):
        acc = taps(pad, kernel, slab, col, row, False)
        add = jnp.broadcast_to(bias[:, lanes(slab)], (8, LANES))
        for i in range(BAND):
            at = pl.ds(pl.multiple_of((row + i) * cols + col, 8), 8)
            depth[at, lanes(slab)] = acc[i] + add

    steps(rows, cols, channels, piece)
    block = 128

    def norm(i, _):
        at = pl.ds(pl.multiple_of(i * block, block), block)
        x = depth[at, :]
        centred = x - jnp.mean(x, axis=-1, keepdims=True)
        inv = lax.rsqrt(jnp.mean(centred * centred, axis=-1, keepdims=True) + norm_epsilon)
        normed = centred * inv
        normed_ref[at, :] = normed
        inv_ref[at, :] = jnp.broadcast_to(inv, (block, LANES))
        ln_ref[at, :] = (normed * gain[...] + shift[...]).astype(bf16)
        return _

    lax.fori_loop(0, rows * cols // block, norm, 0)


def gelu_pair(u):
    cdf = 0.5 * (1.0 + lax.erf(u * inv_root_two))
    pdf = jnp.exp(-0.5 * u * u) * inv_root_tau
    return u * cdf, cdf + u * pdf


def fold(x):
    return jnp.sum(x.reshape(-1, 8, x.shape[1]), axis=0)


def mlp_block(ln, d_branch, w_in, w_out, b_in, base, width, hid_ref, dpre_ref, gbin):
    sub = 256
    count = width // sub

    def products(s):
        at = pl.ds(base + s * sub, sub)
        return dot(ln, w_in[at, :], NT), dot(d_branch, w_out[:, at], NN)

    ahead = products(0)
    for s in range(count):
        pre, d_hidden = ahead
        if s + 1 < count:
            ahead = products(s + 1)
        act, slope = gelu_pair(pre + b_in[:, base + s * sub : base + (s + 1) * sub])
        d_pre = d_hidden * slope
        gbin[:, s * sub : (s + 1) * sub] += fold(d_pre)
        hid_ref[:, s * sub : (s + 1) * sub] = act.astype(bf16)
        dpre_ref[:, s * sub : (s + 1) * sub] = d_pre.astype(bf16)
    at = pl.ds(base, width)
    hidden, d_pre = hid_ref[...], dpre_ref[...]
    branch = dot(hidden, w_out[:, at], NT)
    d_norm = dot(d_pre, w_in[at, :], NN)
    return hidden, d_pre, branch, d_norm


def pack_grads(core, keep, send, gwin, gwout, gbin_ref, gbin):
    width, channels = gwin.shape

    def store(first, second):
        first[...] = gwin[...].astype(bf16)
        for j in range(width // channels):
            at = slice(j * channels, (j + 1) * channels)
            second[at, :] = gwout[:, at].astype(bf16)

    pl.when(core[0] == 0)(lambda: store(keep, send))
    pl.when(core[0] != 0)(lambda: store(send, keep))
    gbin_ref[...] = jnp.sum(gbin[...], axis=0, keepdims=True)


MLP_BLOCK = 256


def mlp_first_kernel(
    base, width, core, ln_ref, cot, w_in, w_out, b_in, scale, branch_ref, dnorm_ref, keep, send, gbin_ref,
    hid_ref, dpre_ref, gwin, gwout, gbin,
):
    gwin[...] = jnp.zeros_like(gwin)
    gwout[...] = jnp.zeros_like(gwout)
    gbin[...] = jnp.zeros_like(gbin)

    def step(i, _):
        at = pl.ds(pl.multiple_of(i * MLP_BLOCK, MLP_BLOCK), MLP_BLOCK)
        ln = ln_ref[at, :]
        d_branch = (scale[...] * cot[at, :].astype(f32)).astype(bf16)
        hidden, d_pre, branch, d_norm = mlp_block(
            ln, d_branch, w_in, w_out, b_in, base, width, hid_ref, dpre_ref, gbin
        )
        branch_ref[at, :] = branch
        dnorm_ref[at, :] = d_norm
        gwin[...] += dot(d_pre, ln, TN)
        gwout[...] += dot(d_branch, hidden, TN)
        return _

    lax.fori_loop(0, ln_ref.shape[0] // MLP_BLOCK, step, 0)
    pack_grads(core, keep, send, gwin, gwout, gbin_ref, gbin)


def mlp_second_kernel(
    base, width, core, ln_ref, cot, w_in, w_out, b_in, scale, b_out, gain, page, normed_ref, inv_ref,
    branch_ref, dnorm_ref,
    result, d_depth_ref, keep, send, gbin_ref, sums_ref,
    hid_ref, dpre_ref, gwin, gwout, gbin, sums,
):
    gwin[...] = jnp.zeros_like(gwin)
    gwout[...] = jnp.zeros_like(gwout)
    gbin[...] = jnp.zeros_like(gbin)
    sums[...] = jnp.zeros_like(sums)

    def step(i, _):
        at = pl.ds(pl.multiple_of(i * MLP_BLOCK, MLP_BLOCK), MLP_BLOCK)
        ln = ln_ref[at, :]
        cot32 = cot[at, :].astype(f32)
        d_branch32 = scale[...] * cot32
        d_branch = d_branch32.astype(bf16)
        hidden, d_pre, branch, d_norm = mlp_block(
            ln, d_branch, w_in, w_out, b_in, base, width, hid_ref, dpre_ref, gbin
        )
        gwin[...] += dot(d_pre, ln, TN)
        gwout[...] += dot(d_branch, hidden, TN)
        branch = branch + branch_ref[at, :] + b_out[...]
        result[at, :] = (page[at, :].astype(f32) + scale[...] * branch).astype(bf16)
        d_norm = d_norm + dnorm_ref[at, :]
        normed = normed_ref[at, :]
        inv = inv_ref[at, 0:1]
        weighted = d_norm * normed
        s = d_norm * gain[...]
        mean_s = jnp.mean(s, axis=-1, keepdims=True)
        mean_sn = jnp.mean(s * normed, axis=-1, keepdims=True)
        d_depth = (inv * (s - mean_s - normed * mean_sn)).astype(bf16)
        d_depth_ref[at, :] = d_depth
        sums[0] += fold(cot32 * branch)
        sums[1] += fold(d_branch32)
        sums[2] += fold(weighted)
        sums[3] += fold(d_norm)
        sums[4] += fold(d_depth.astype(f32))
        return _

    lax.fori_loop(0, ln_ref.shape[0] // MLP_BLOCK, step, 0)
    pack_grads(core, keep, send, gwin, gwout, gbin_ref, gbin)
    for j in range(5):
        sums_ref[j : j + 1, :] = jnp.sum(sums[j], axis=0, keepdims=True)


def kernel_grad_kernel(tile, top, bottom, left, right, d_depth, out, pad, d32, acc_ref):
    rows, cols, channels = tile.shape
    fill(pad, tile, top, bottom, left, right)
    d32[...] = d_depth[...].astype(f32)
    acc_ref[...] = jnp.zeros_like(acc_ref)

    def piece(slab, col, row):
        grads = []
        for i in range(BAND):
            at = pl.ds(pl.multiple_of((row + i) * cols + col, 8), 8)
            grads.append(d32[at, lanes(slab)])
        for b in range(7):
            acc = [None] * 7
            for r in range(BAND + 6):
                x = pad[slab, row + r, pl.ds(col + EDGE - 3 + b, 8), :]
                for a in range(7):
                    i = r - a
                    if 0 <= i < BAND:
                        acc[a] = x * grads[i] if acc[a] is None else acc[a] + x * grads[i]
            for a in range(7):
                acc_ref[slab, a * 7 + b] += acc[a]

    steps(rows, cols, channels, piece)
    for slab in range(channels // LANES):
        out[:, slab * LANES : (slab + 1) * LANES] = jnp.sum(acc_ref[slab], axis=1)


def conv_grad_kernel(tile, top, bottom, left, right, kernel, cot, out, pad, total):
    rows, cols, channels = tile.shape
    fill(pad, tile, top, bottom, left, right)

    def piece(slab, col, row):
        acc = taps(pad, kernel, slab, col, row, True)
        for i in range(BAND):
            at = pl.ds(pl.multiple_of((row + i) * cols + col, 8), 8)
            total[at, lanes(slab)] = acc[i]

    steps(rows, cols, channels, piece)
    block = 128

    def finish(i, _):
        at = pl.ds(pl.multiple_of(i * block, block), block)
        out[at, :] = (cot[at, :].astype(f32) + total[at, :]).astype(bf16)
        return _

    lax.fori_loop(0, rows * cols // block, finish, 0)


def call(body, outs, scratch, args, flops, scalars=0, size=24 << 20):
    vmem = pl.BlockSpec(memory_space=pltpu.VMEM)
    smem = pl.BlockSpec(memory_space=pltpu.SMEM)
    return pl.pallas_call(
        body,
        out_shape=[jax.ShapeDtypeStruct(shape, dtype) for shape, dtype in outs],
        in_specs=[smem] * scalars + [vmem] * (len(args) - scalars),
        out_specs=[vmem] * len(outs),
        scratch_shapes=[pltpu.VMEM(shape, dtype) for shape, dtype in scratch],
        compiler_params=pltpu.CompilerParams(vmem_limit_bytes=size),
        cost_estimate=pl.CostEstimate(flops=flops, bytes_accessed=1 << 20, transcendentals=0),
    )(*args)


def bits(count):
    return max(count.bit_length() - 1, 0)


def sum_plan():
    plan = [("gy", 0)]
    rest = [("gy", j) for j in range(1, bits(lax.axis_size("gy")))]
    wide = [("gx", j) for j in range(bits(lax.axis_size("gx")))]
    deep = [("rep", j) for j in range(bits(lax.axis_size("rep")))]
    first = rest + wide + deep
    second = wide + rest + deep
    return [(plan[0], plan[0])] + list(zip(first, second))


def exchange(x, choice):
    sizes = [lax.axis_size(axis) for axis in AXES]
    perm = []
    for i in range(sizes[0] * sizes[1] * sizes[2]):
        at = {"gy": i // (sizes[1] * sizes[2]), "gx": i // sizes[2] % sizes[1], "rep": i % sizes[2]}
        axis, bit = choice[at["gy"] % 2]
        at[axis] ^= 1 << bit
        perm.append((i, (at["gy"] * sizes[1] + at["gx"]) * sizes[2] + at["rep"]))
    return lax.ppermute(x, AXES, perm)


def own_bit(choice):
    core = lax.axis_index("gy") % 2
    values = [lax.axis_index(axis) // (1 << bit) % 2 for axis, bit in choice]
    return jnp.where(core == 0, values[0], values[1])


def sum_scatter(keep, send):
    plan = sum_plan()
    x = (keep.astype(f32) + exchange(send, plan[0]).astype(f32)).astype(bf16)
    for choice in plan[1:]:
        bit = own_bit(choice)
        halves = x.reshape(2, x.shape[0] // 2, x.shape[1])
        keep = lax.dynamic_index_in_dim(halves, bit, 0, keepdims=False)
        send = lax.dynamic_index_in_dim(halves, 1 - bit, 0, keepdims=False)
        x = (keep.astype(f32) + exchange(send, choice).astype(f32)).astype(bf16)
    return x


def gather_back(x):
    for choice in reversed(sum_plan()):
        bit = own_bit(choice)
        other = exchange(x, choice)
        x = jnp.where(bit == 0, jnp.concatenate([x, other]), jnp.concatenate([other, x]))
    return x


def sum_small(x):
    rows, channels = x.shape
    groups = (("gy", "gx"), ("rep",))
    counts = [math.prod(lax.axis_size(axis) for axis in group) for group in groups]
    whole = -(-rows // math.prod(counts)) * math.prod(counts)
    x = jnp.pad(x, ((0, whole - rows), (0, 0)))
    for group, count in zip(groups, counts):
        got = lax.all_to_all(x, group, 0, 0, tiled=True)
        x = jnp.sum(got.reshape(count, -1, channels), axis=0)
    for group, count in reversed(list(zip(groups, counts))):
        x = lax.all_to_all(jnp.tile(x, (count, 1)), group, 0, 0, tiled=True)
    return x[:rows]


def shards(
    pages,
    cotangent,
    conv_kernel,
    conv_bias,
    norm_gain,
    norm_bias,
    w_in,
    b_in,
    w_out,
    b_out,
    layer_scale,
):
    _, rows, cols, channels = pages.shape
    hid = w_in.shape[0]
    width = hid // 2
    pixels = rows * cols
    tile = pages.reshape(rows, cols, channels)
    page = pages.reshape(pixels, channels)
    cot = cotangent.reshape(pixels, channels)
    kernel = conv_kernel.reshape(49, channels)
    row = lambda v: v.reshape(1, -1)
    gain, shift, scale = row(norm_gain), row(norm_bias), row(layer_scale)
    pad = ((channels // LANES, rows + 6, EDGE + cols + 8, LANES), f32)
    full = (pixels, channels)

    around = halo(tile)
    conv_flops = 2 * 49 * pixels * channels * 60
    normed, inv, ln_out = call(
        conv_norm_kernel,
        [(full, f32), ((pixels, LANES), f32), (full, bf16)],
        [pad, (full, f32)],
        (tile, *around, kernel, row(conv_bias), gain, shift),
        conv_flops,
    )
    grads = [
        ((MLP_BLOCK, width), bf16),
        ((MLP_BLOCK, width), bf16),
        ((width, channels), f32),
        ((channels, width), f32),
        ((8, width), f32),
    ]
    packed = ((width, channels), bf16)
    core = (lax.axis_index("gy") % 2).astype(jnp.int32).reshape(1)
    mlp_flops = 6 * pixels * channels * hid * 2
    weights = (w_in, w_out, row(b_in), scale)
    branch, d_norm, keep_a, send_a, gbin_a = call(
        functools.partial(mlp_first_kernel, 0, width),
        [(full, f32), (full, f32), packed, packed, ((1, width), f32)],
        grads,
        (core, ln_out, cot, *weights),
        mlp_flops,
        1,
    )
    piece_a = sum_scatter(keep_a, send_a)
    result, d_depth, keep_b, send_b, gbin_b, sums = call(
        functools.partial(mlp_second_kernel, width, width),
        [(full, bf16), (full, bf16), packed, packed, ((1, width), f32), ((8, channels), f32)],
        grads + [((8, 8, channels), f32)],
        (core, ln_out, cot, *weights, row(b_out), gain, page, normed, inv, branch, d_norm),
        mlp_flops,
        1,
    )
    piece_b = sum_scatter(keep_b, send_b)
    d_tile = d_depth.reshape(tile.shape)
    d_around = halo(d_tile)
    (g_kernel,) = call(
        kernel_grad_kernel,
        [((49, channels), f32)],
        [pad, (full, f32), ((channels // LANES, 49, 8, LANES), f32)],
        (tile, *around, d_depth),
        conv_flops,
    )
    small = jnp.concatenate(
        [g_kernel, sums[:5], gbin_a.reshape(-1, channels), gbin_b.reshape(-1, channels)]
    )
    (grad_pages,) = call(
        conv_grad_kernel,
        [(full, bf16)],
        [pad, (full, f32)],
        (d_tile, *d_around, kernel, cot),
        conv_flops,
    )
    factor = float(pixels * lax.axis_size("gy") * lax.axis_size("gx") * lax.axis_size("rep")) ** (-0.5)
    small = sum_small(small) * factor
    both = [gather_back(piece_a), gather_back(piece_b)]
    sum_win = jnp.concatenate([g[:width] for g in both]).astype(f32) * factor
    blocks = [g[width + j * channels : width + (j + 1) * channels] for g in both for j in range(width // channels)]
    sum_wout = jnp.concatenate(blocks, axis=1).astype(f32) * factor
    return (
        result.reshape(pages.shape),
        grad_pages.reshape(pages.shape),
        small[:49].reshape(7, 7, channels),
        small[53],
        small[51],
        small[52],
        sum_win,
        small[54:].reshape(-1),
        sum_wout,
        small[50],
        small[49],
    )


def solution(mesh):
    split = P("rep", "gy", "gx", None)
    return jax.shard_map(
        shards,
        mesh=mesh,
        in_specs=(split, split) + (P(),) * 9,
        out_specs=(split, split) + (P(),) * 9,
        check_vma=False,
    )
```

```python
import functools
import math

import jax
import jax.numpy as jnp
from jax import lax
from jax.experimental import pallas as pl
from jax.experimental.pallas import tpu as pltpu
from jax.sharding import PartitionSpec as P

norm_epsilon = 1e-06
inv_root_two = 0.7071067811865476
inv_root_tau = 0.3989422804014327

LANES = 128
EDGE = 8
BAND = 16
AXES = ("gy", "gx", "rep")
f32 = jnp.float32
bf16 = jnp.bfloat16


def dot(a, b, dims):
    return lax.dot_general(a, b, (dims, ((), ())), preferred_element_type=f32)


NN = ((1,), (0,))
NT = ((1,), (1,))
TN = ((0,), (0,))


def pair_rounds(count):
    first = [(i, i + 1) for i in range(0, count - 1, 2)]
    second = [(i, i + 1) for i in range(1, count - 1, 2)]
    return [pairs + [(b, a) for a, b in pairs] for pairs in (first, second)]


def edges(block, axis, dim, width):
    size = block.shape[dim]
    even = lax.axis_index(axis) % 2 == 0
    low = lax.slice_in_dim(block, 0, width, axis=dim)
    high = lax.slice_in_dim(block, size - width, size, axis=dim)
    out = []
    for pairs, is_high in zip(pair_rounds(lax.axis_size(axis)), (even, ~even)):
        if pairs:
            out.append(lax.ppermute(jnp.where(is_high, high, low), axis, pairs))
        else:
            out.append(jnp.zeros_like(low))
    return out


def halo(tile):
    rows = edges(tile, "gy", 0, 3)
    even = lax.axis_index("gy") % 2 == 0
    top = jnp.where(even, rows[1], rows[0])
    bottom = jnp.where(even, rows[0], rows[1])
    even_x = lax.axis_index("gx") % 2 == 0
    size = tile.shape[1]
    column = [jnp.concatenate([part[:, :3], part[:, size - 3 :]], axis=1) for part in (top, tile, bottom)]
    column = jnp.concatenate(column, axis=0)
    out = []
    for pairs, is_high in zip(pair_rounds(lax.axis_size("gx")), (even_x, ~even_x)):
        if pairs:
            out.append(lax.ppermute(jnp.where(is_high, column[:, 3:], column[:, :3]), "gx", pairs))
        else:
            out.append(jnp.zeros_like(column[:, :3]))
    left = jnp.where(even_x, out[1], out[0])
    right = jnp.where(even_x, out[0], out[1])
    return top, bottom, left, right


def fill(pad, tile, top, bottom, left, right):
    rows, cols, channels = tile.shape
    for slab in range(channels // LANES):
        at = slice(slab * LANES, (slab + 1) * LANES)
        pad[slab, 0:3, EDGE : EDGE + cols, :] = top[:, :, at].astype(f32)
        pad[slab, 3 + rows :, EDGE : EDGE + cols, :] = bottom[:, :, at].astype(f32)
        pad[slab, :, EDGE - 3 : EDGE, :] = left[:, :, at].astype(f32)
        pad[slab, :, EDGE + cols : EDGE + cols + 3, :] = right[:, :, at].astype(f32)

        def body(row, _):
            pad[slab, row + 3, EDGE : EDGE + cols, :] = tile[row, :, at].astype(f32)
            return _

        lax.fori_loop(0, rows, body, 0, unroll=4)


def steps(rows, cols, channels, body):
    slabs, tiles, bands = channels // LANES, cols // 8, rows // BAND

    def step(i, _):
        slab = i // (tiles * bands)
        rest = i % (tiles * bands)
        body(slab, pl.multiple_of(rest // bands * 8, 8), rest % bands * BAND)
        return _

    lax.fori_loop(0, slabs * tiles * bands, step, 0)


def lanes(slab):
    return pl.ds(pl.multiple_of(slab * LANES, LANES), LANES)


def taps(pad, kernel, slab, col, row, flip):
    acc = [None] * BAND
    for b in range(7):
        scale = []
        for a in range(7):
            tap = (6 - a) * 7 + 6 - b if flip else a * 7 + b
            scale.append(jnp.broadcast_to(kernel[pl.ds(tap, 1), lanes(slab)], (8, LANES)))
        for r in range(BAND + 6):
            x = pad[slab, row + r, pl.ds(col + EDGE - 3 + b, 8), :]
            for a in range(7):
                i = r - a
                if 0 <= i < BAND:
                    acc[i] = x * scale[a] if acc[i] is None else acc[i] + x * scale[a]
    return acc


def conv_norm_kernel(
    tile, top, bottom, left, right, kernel, bias, gain, shift, normed_ref, inv_ref, ln_ref, pad, depth
):
    rows, cols, channels = tile.shape
    fill(pad, tile, top, bottom, left, right)

    def piece(slab, col, row):
        acc = taps(pad, kernel, slab, col, row, False)
        add = jnp.broadcast_to(bias[:, lanes(slab)], (8, LANES))
        for i in range(BAND):
            at = pl.ds(pl.multiple_of((row + i) * cols + col, 8), 8)
            depth[at, lanes(slab)] = acc[i] + add

    steps(rows, cols, channels, piece)
    block = 128

    def norm(i, _):
        at = pl.ds(pl.multiple_of(i * block, block), block)
        x = depth[at, :]
        centred = x - jnp.mean(x, axis=-1, keepdims=True)
        inv = lax.rsqrt(jnp.mean(centred * centred, axis=-1, keepdims=True) + norm_epsilon)
        normed = centred * inv
        normed_ref[at, :] = normed
        inv_ref[at, :] = jnp.broadcast_to(inv, (block, LANES))
        ln_ref[at, :] = (normed * gain[...] + shift[...]).astype(bf16)
        return _

    lax.fori_loop(0, rows * cols // block, norm, 0)


def gelu_pair(u):
    cdf = 0.5 * (1.0 + lax.erf(u * inv_root_two))
    pdf = jnp.exp(-0.5 * u * u) * inv_root_tau
    return u * cdf, cdf + u * pdf


def fold(x):
    return jnp.sum(x.reshape(-1, 8, x.shape[1]), axis=0)


def mlp_block(ln, d_branch, w_in, w_out, b_in, base, width, hid_ref, dpre_ref, gbin):
    sub = 256
    count = width // sub

    def products(s):
        at = pl.ds(base + s * sub, sub)
        return dot(ln, w_in[at, :], NT), dot(d_branch, w_out[:, at], NN)

    ahead = products(0)
    for s in range(count):
        pre, d_hidden = ahead
        if s + 1 < count:
            ahead = products(s + 1)
        act, slope = gelu_pair(pre + b_in[:, base + s * sub : base + (s + 1) * sub])
        d_pre = d_hidden * slope
        gbin[:, s * sub : (s + 1) * sub] += fold(d_pre)
        hid_ref[:, s * sub : (s + 1) * sub] = act.astype(bf16)
        dpre_ref[:, s * sub : (s + 1) * sub] = d_pre.astype(bf16)
    at = pl.ds(base, width)
    hidden, d_pre = hid_ref[...], dpre_ref[...]
    branch = dot(hidden, w_out[:, at], NT)
    d_norm = dot(d_pre, w_in[at, :], NN)
    return hidden, d_pre, branch, d_norm


def pack_grads(core, keep, send, gwin, gwout, gbin_ref, gbin):
    width, channels = gwin.shape

    def store(first, second):
        for j in range(channels // LANES):
            first[j * width : (j + 1) * width, :] = gwin[:, j * LANES : (j + 1) * LANES].astype(bf16)
        for j in range(width // LANES):
            second[j * channels : (j + 1) * channels, :] = gwout[
                :, j * LANES : (j + 1) * LANES
            ].astype(bf16)

    pl.when(core[0] == 0)(lambda: store(keep, send))
    pl.when(core[0] != 0)(lambda: store(send, keep))
    gbin_ref[...] = jnp.sum(gbin[...], axis=0, keepdims=True)


MLP_BLOCK = 256


def mlp_first_kernel(
    base, width, core, ln_ref, cot, w_in, w_out, b_in, scale, branch_ref, dnorm_ref, keep, send, gbin_ref,
    hid_ref, dpre_ref, gwin, gwout, gbin,
):
    gwin[...] = jnp.zeros_like(gwin)
    gwout[...] = jnp.zeros_like(gwout)
    gbin[...] = jnp.zeros_like(gbin)

    def step(i, _):
        at = pl.ds(pl.multiple_of(i * MLP_BLOCK, MLP_BLOCK), MLP_BLOCK)
        ln = ln_ref[at, :]
        d_branch = (scale[...] * cot[at, :].astype(f32)).astype(bf16)
        hidden, d_pre, branch, d_norm = mlp_block(
            ln, d_branch, w_in, w_out, b_in, base, width, hid_ref, dpre_ref, gbin
        )
        branch_ref[at, :] = branch
        dnorm_ref[at, :] = d_norm
        gwin[...] += dot(d_pre, ln, TN)
        gwout[...] += dot(d_branch, hidden, TN)
        return _

    lax.fori_loop(0, ln_ref.shape[0] // MLP_BLOCK, step, 0)
    pack_grads(core, keep, send, gwin, gwout, gbin_ref, gbin)


def mlp_second_kernel(
    base, width, core, ln_ref, cot, w_in, w_out, b_in, scale, b_out, gain, page, normed_ref, inv_ref,
    branch_ref, dnorm_ref,
    result, d_depth_ref, keep, send, gbin_ref, sums_ref,
    hid_ref, dpre_ref, gwin, gwout, gbin, sums,
):
    gwin[...] = jnp.zeros_like(gwin)
    gwout[...] = jnp.zeros_like(gwout)
    gbin[...] = jnp.zeros_like(gbin)
    sums[...] = jnp.zeros_like(sums)

    def step(i, _):
        at = pl.ds(pl.multiple_of(i * MLP_BLOCK, MLP_BLOCK), MLP_BLOCK)
        ln = ln_ref[at, :]
        cot32 = cot[at, :].astype(f32)
        d_branch32 = scale[...] * cot32
        d_branch = d_branch32.astype(bf16)
        hidden, d_pre, branch, d_norm = mlp_block(
            ln, d_branch, w_in, w_out, b_in, base, width, hid_ref, dpre_ref, gbin
        )
        gwin[...] += dot(d_pre, ln, TN)
        gwout[...] += dot(d_branch, hidden, TN)
        branch = branch + branch_ref[at, :] + b_out[...]
        result[at, :] = (page[at, :].astype(f32) + scale[...] * branch).astype(bf16)
        d_norm = d_norm + dnorm_ref[at, :]
        normed = normed_ref[at, :]
        inv = inv_ref[at, 0:1]
        weighted = d_norm * normed
        s = d_norm * gain[...]
        mean_s = jnp.mean(s, axis=-1, keepdims=True)
        mean_sn = jnp.mean(s * normed, axis=-1, keepdims=True)
        d_depth = (inv * (s - mean_s - normed * mean_sn)).astype(bf16)
        d_depth_ref[at, :] = d_depth
        sums[0] += fold(cot32 * branch)
        sums[1] += fold(d_branch32)
        sums[2] += fold(weighted)
        sums[3] += fold(d_norm)
        sums[4] += fold(d_depth.astype(f32))
        return _

    lax.fori_loop(0, ln_ref.shape[0] // MLP_BLOCK, step, 0)
    pack_grads(core, keep, send, gwin, gwout, gbin_ref, gbin)
    for j in range(5):
        sums_ref[j : j + 1, :] = jnp.sum(sums[j], axis=0, keepdims=True)


SMALL = 64


def kernel_grad_kernel(
    core, tile, top, bottom, left, right, d_depth, sums, gbin_a, gbin_b, keep, send, pad, d32, acc_ref
):
    rows, cols, channels = tile.shape
    fill(pad, tile, top, bottom, left, right)
    d32[...] = d_depth[...].astype(f32)
    acc_ref[...] = jnp.zeros_like(acc_ref)

    def piece(slab, col, row):
        grads = []
        for i in range(BAND):
            at = pl.ds(pl.multiple_of((row + i) * cols + col, 8), 8)
            grads.append(d32[at, lanes(slab)])
        for b in range(7):
            acc = [None] * 7
            for r in range(BAND + 6):
                x = pad[slab, row + r, pl.ds(col + EDGE - 3 + b, 8), :]
                for a in range(7):
                    i = r - a
                    if 0 <= i < BAND:
                        acc[a] = x * grads[i] if acc[a] is None else acc[a] + x * grads[i]
            for a in range(7):
                acc_ref[slab, a * 7 + b] += acc[a]

    steps(rows, cols, channels, piece)

    def store(first, second):
        second[...] = jnp.zeros_like(second)
        slabs = channels // LANES
        for slab in range(slabs):
            at = slice(slab * LANES, (slab + 1) * LANES)
            part = [jnp.sum(acc_ref[slab], axis=1), sums[:5, at]]
            for j in range((gbin_a.shape[1] + gbin_b.shape[1]) // channels):
                lane = (j * slabs + slab) * LANES
                source = gbin_a if lane < gbin_a.shape[1] else gbin_b
                lane = lane if lane < gbin_a.shape[1] else lane - gbin_a.shape[1]
                part.append(source[:, lane : lane + LANES])
            part = jnp.concatenate(part)
            part = jnp.concatenate([part, jnp.zeros((SMALL - part.shape[0], LANES), f32)])
            first[slab * SMALL : (slab + 1) * SMALL, :] = part.astype(bf16)
        rest = first.shape[0] - slabs * SMALL
        first[slabs * SMALL :, :] = jnp.zeros((rest, LANES), bf16)

    pl.when(core[0] == 0)(lambda: store(keep, send))
    pl.when(core[0] != 0)(lambda: store(send, keep))


def conv_grad_kernel(tile, top, bottom, left, right, kernel, cot, out, pad, total):
    rows, cols, channels = tile.shape
    fill(pad, tile, top, bottom, left, right)

    def piece(slab, col, row):
        acc = taps(pad, kernel, slab, col, row, True)
        for i in range(BAND):
            at = pl.ds(pl.multiple_of((row + i) * cols + col, 8), 8)
            total[at, lanes(slab)] = acc[i]

    steps(rows, cols, channels, piece)
    block = 128

    def finish(i, _):
        at = pl.ds(pl.multiple_of(i * block, block), block)
        out[at, :] = (cot[at, :].astype(f32) + total[at, :]).astype(bf16)
        return _

    lax.fori_loop(0, rows * cols // block, finish, 0)


def call(body, outs, scratch, args, flops, scalars=0, after=(), size=24 << 20):
    held = len(args)

    def kernel(*refs):
        body(*refs[:held], *refs[held + len(after) :])

    vmem = pl.BlockSpec(memory_space=pltpu.VMEM)
    smem = pl.BlockSpec(memory_space=pltpu.SMEM)
    return pl.pallas_call(
        kernel,
        out_shape=[jax.ShapeDtypeStruct(shape, dtype) for shape, dtype in outs],
        in_specs=[smem] * scalars
        + [vmem] * (held - scalars)
        + [pl.BlockSpec(memory_space=pl.ANY)] * len(after),
        out_specs=[vmem] * len(outs),
        scratch_shapes=[pltpu.VMEM(shape, dtype) for shape, dtype in scratch],
        compiler_params=pltpu.CompilerParams(vmem_limit_bytes=size),
        cost_estimate=pl.CostEstimate(flops=flops, bytes_accessed=flops >> 10, transcendentals=0),
    )(*args, *after)


def bits(axis):
    return [(axis, j) for j in range(max(lax.axis_size(axis).bit_length() - 1, 0))]


def rounds():
    rest = bits("gy")[2:] + bits("gx")[1:] + bits("rep")
    return [[("gy", 1), ("gx", 0)]] + [rest[i : i + 2] for i in range(0, len(rest), 2)]


def exchange(x, flips):
    sizes = [lax.axis_size(axis) for axis in AXES]
    perm = []
    for i in range(math.prod(sizes)):
        at = {"gy": i // (sizes[1] * sizes[2]), "gx": i // sizes[2] % sizes[1], "rep": i % sizes[2]}
        for axis, bit in flips:
            at[axis] ^= 1 << bit
        perm.append((i, (at["gy"] * sizes[1] + at["gx"]) * sizes[2] + at["rep"]))
    return lax.ppermute(x, AXES, perm)


def others(group):
    return [[g for j, g in enumerate(group) if delta >> j & 1] for delta in range(1, 1 << len(group))]


def place(group):
    value = 0
    for j, (axis, bit) in enumerate(group):
        value = value + (lax.axis_index(axis) // (1 << bit) % 2 << j)
    return jnp.asarray(value, jnp.int32).reshape(1)


def hold(arrays):
    return lax.optimization_barrier(arrays)


def chunks(rows, body):
    size = max(n for n in (128, 64, 32, 16) if rows % n == 0)

    def step(i, _):
        body(pl.multiple_of(i * size, size), size)
        return _

    lax.fori_loop(0, rows // size, step, 0, unroll=2 if rows // size > 1 else 1)


def first_sum_kernel(has_small, mine, *refs):
    wide, outs = refs[:2], refs[4 if has_small else 2 :]
    rows = wide[0].shape[0] // len(outs)
    for delta, out in enumerate(outs):
        to = mine[0] ^ delta

        def add(at, size):
            part = pl.ds(pl.multiple_of(to * rows + at, 16), size)
            out[pl.ds(at, size), :] = (wide[0][part, :].astype(f32) + wide[1][part, :].astype(f32)).astype(bf16)

        chunks(rows, add)
        end = rows
        if has_small:
            small = refs[2:4]
            size = small[0].shape[0] // len(outs)
            part = pl.ds(pl.multiple_of(to * size, 16), size)
            out[end : end + size, :] = (small[0][part, :].astype(f32) + small[1][part, :].astype(f32)).astype(bf16)
            end += size
        if end < out.shape[0]:
            out[end:, :] = jnp.zeros((out.shape[0] - end, LANES), bf16)


def next_sum_kernel(count, mine, *refs):
    ins, outs = refs[:count], refs[count:]
    rows = outs[0].shape[0]
    for delta, out in enumerate(outs):
        start = (mine[0] ^ delta) * rows if len(outs) > 1 else 0

        def add(at, size):
            part = pl.ds(pl.multiple_of(start + at, 16), size)
            out[pl.ds(at, size), :] = sum(r[part, :].astype(f32) for r in ins).astype(bf16)

        chunks(rows, add)


def join_kernel(count, mine, *refs):
    out = refs[count]
    rows = refs[0].shape[0]
    for delta, ref in enumerate(refs[:count]):
        out[pl.ds(pl.multiple_of((mine[0] ^ delta) * rows, 16), rows), :] = ref[...]


def part_rows(weights, small):
    step = 16 * math.prod(1 << len(group) for group in rounds()[1:])
    return -(-(weights + small) // step) * step


SUM_FLOPS = 1 << 20


def scatter_start(keep, other, small=(), after=()):
    plan = rounds()
    count = 1 << len(plan[0])
    rows = part_rows(keep.shape[0] // count, small[0].shape[0] // count if small else 0)
    return call(
        functools.partial(first_sum_kernel, bool(small)),
        [((rows, LANES), bf16)] * count,
        [],
        (place(plan[0]), keep, other, *small),
        SUM_FLOPS,
        1,
        after,
    )


def transfers():
    plan = rounds()
    return [(group, True) for group in plan] + [(group, False) for group in reversed(plan)]


def send_parts(parts, step):
    group, scatters = transfers()[step]
    if not scatters:
        parts = [parts[0]] * (1 << len(group))
    return [parts[0]] + [exchange(x, flips) for x, flips in zip(parts[1:], others(group))]


def combine(got, step):
    steps = transfers()
    group, scatters = steps[step]
    rows = got[0].shape[0]
    if not scatters:
        shapes = [((len(got) * rows, LANES), bf16)]
        body, mine = join_kernel, place(group)
    else:
        following = steps[step + 1][0] if steps[step + 1][1] else []
        count = 1 << len(following)
        shapes = [((rows // count, LANES), bf16)] * count
        body, mine = next_sum_kernel, place(following)
    return call(functools.partial(body, len(got)), shapes, [], (mine, *got), SUM_FLOPS, 1)


def finish_kernel(
    factor, widths, core, own_a, other_a, own_b, other_b,
    win, wout, gk, scale, b_out, gain, shift, bias, b_in,
):
    channels = wout.shape[0]

    def store(firsts, seconds):
        base = 0
        for width, first, second in zip(widths, firsts, seconds):
            part = first.shape[0] // 4
            block = width * channels // LANES // 4

            def rows(ref, at):
                start = at // block * part + at % block
                return ref[start : start + LANES, :].astype(f32) * factor

            for j in range(channels // LANES):
                for i in range(0, width, LANES):
                    win[base + i : base + i + LANES, j * LANES : (j + 1) * LANES] = rows(first, j * width + i)
            for j in range(width // LANES):
                for i in range(0, channels, LANES):
                    wout[i : i + LANES, base + j * LANES : base + (j + 1) * LANES] = rows(
                        second, j * channels + i
                    )
            base += width
        slabs = channels // LANES
        for slab in range(slabs):
            at = slice(slab * LANES, (slab + 1) * LANES)
            start = slab * part + block
            values = firsts[1][start : start + SMALL, :].astype(f32) * factor
            gk[:, at] = values[:49]
            for j, ref in enumerate((scale, b_out, gain, shift, bias)):
                ref[:, at] = values[49 + j : 50 + j]
            for j in range(b_in.shape[1] // channels):
                lane = (j * slabs + slab) * LANES
                b_in[:, lane : lane + LANES] = values[54 + j : 55 + j]

    pl.when(core[0] == 0)(lambda: store((own_a, own_b), (other_a, other_b)))
    pl.when(core[0] != 0)(lambda: store((other_a, other_b), (own_a, own_b)))


def shards(
    pages,
    cotangent,
    conv_kernel,
    conv_bias,
    norm_gain,
    norm_bias,
    w_in,
    b_in,
    w_out,
    b_out,
    layer_scale,
):
    _, rows, cols, channels = pages.shape
    hid = w_in.shape[0]
    pixels = rows * cols
    tile = pages.reshape(rows, cols, channels)
    page = pages.reshape(pixels, channels)
    cot = cotangent.reshape(pixels, channels)
    kernel = conv_kernel.reshape(49, channels)
    row = lambda v: v.reshape(1, -1)
    gain, shift, scale = row(norm_gain), row(norm_bias), row(layer_scale)
    pad = ((channels // LANES, rows + 6, EDGE + cols + 8, LANES), f32)
    full = (pixels, channels)

    around = halo(tile)
    conv_flops = 2 * 49 * pixels * channels * 60
    normed, inv, ln_out = call(
        conv_norm_kernel,
        [(full, f32), ((pixels, LANES), f32), (full, bf16)],
        [pad, (full, f32)],
        (tile, *around, kernel, row(conv_bias), gain, shift),
        conv_flops,
    )
    grads = lambda width: [
        ((MLP_BLOCK, width), bf16),
        ((MLP_BLOCK, width), bf16),
        ((width, channels), f32),
        ((channels, width), f32),
        ((8, width), f32),
    ]
    packed = lambda width: [((width * channels // LANES, LANES), bf16)] * 2 + [((1, width), f32)]
    core_flip = [("gy", 0)]
    core = place(core_flip)
    mlp_flops = 12 * pixels * channels * hid
    weights = (w_in, w_out, row(b_in), scale)
    first, second = hid * 2 // 3, hid // 3
    branch, d_norm, keep_a, send_a, gbin_a = call(
        functools.partial(mlp_first_kernel, 0, first),
        [(full, f32), (full, f32)] + packed(first),
        grads(first),
        (core, ln_out, cot, *weights),
        mlp_flops,
        1,
    )
    other_a = exchange(send_a, core_flip)
    result, d_depth, keep_b, send_b, gbin_b, sums = call(
        functools.partial(mlp_second_kernel, first, second),
        [(full, bf16), (full, bf16)] + packed(second) + [((8, channels), f32)],
        grads(second) + [((8, 8, channels), f32)],
        (core, ln_out, cot, *weights, row(b_out), gain, page, normed, inv, branch, d_norm),
        mlp_flops,
        1,
    )
    d_tile = d_depth.reshape(tile.shape)
    parts_a = scatter_start(keep_a, other_a, after=(d_depth,))
    d_edge, parts_a, keep_b, send_b = hold((d_tile, parts_a, keep_b, send_b))
    got_a = send_parts(parts_a, 0)
    other_b = exchange(send_b, core_flip)
    d_around = halo(d_edge)
    small_rows = ((4 * SMALL, LANES), bf16)
    keep_s, send_s = call(
        kernel_grad_kernel,
        [small_rows, small_rows],
        [pad, (full, f32), ((channels // LANES, 49, 8, LANES), f32)],
        (core, tile, *around, d_depth, sums, gbin_a, gbin_b),
        conv_flops,
        1,
        (parts_a[1],),
    )
    got_a, keep_s, send_s, other_b = hold((got_a, keep_s, send_s, other_b))
    other_s = exchange(send_s, core_flip)
    parts_a = combine(got_a, 0)
    parts_b = scatter_start(keep_b, other_b, (keep_s, other_s))
    got_a, got_b = send_parts(parts_a, 1), send_parts(parts_b, 0)
    (grad_pages,) = call(
        conv_grad_kernel,
        [(full, bf16)],
        [pad, (full, f32)],
        (d_tile, *d_around, kernel, cot),
        conv_flops,
        0,
        (parts_a[1], parts_b[1]),
    )
    got_a, got_b, grad_pages = hold((got_a, got_b, grad_pages))
    last = len(transfers()) - 1
    for step in range(1, last):
        parts_a, parts_b = combine(got_a, step), combine(got_b, step - 1)
        got_a, got_b = hold((send_parts(parts_a, step + 1), send_parts(parts_b, step)))
    (half_a,), parts_b = combine(got_a, last), combine(got_b, last - 1)
    got_a, got_b = hold(([half_a, exchange(half_a, core_flip)], send_parts(parts_b, last)))
    (half_b,) = combine(got_b, last)
    got_b = [half_b, exchange(half_b, core_flip)]
    factor = float(pixels * lax.axis_size("gy") * lax.axis_size("gx") * lax.axis_size("rep")) ** (-0.5)
    line = ((1, channels), f32)
    win, wout, gk, g_scale, g_bout, g_gain, g_shift, g_bias, g_bin = call(
        functools.partial(finish_kernel, factor, (first, second)),
        [((hid, channels), f32), ((channels, hid), f32), ((49, channels), f32)] + [line] * 5 + [((1, hid), f32)],
        [],
        (core, *got_a, *got_b),
        SUM_FLOPS,
        1,
    )
    flat = lambda v: v.reshape(-1)
    return (
        result.reshape(pages.shape),
        grad_pages.reshape(pages.shape),
        gk.reshape(7, 7, channels),
        flat(g_bias),
        flat(g_gain),
        flat(g_shift),
        win,
        flat(g_bin),
        wout,
        flat(g_bout),
        flat(g_scale),
    )


def solution(mesh):
    split = P("rep", "gy", "gx", None)
    return jax.shard_map(
        shards,
        mesh=mesh,
        in_specs=(split, split) + (P(),) * 9,
        out_specs=(split, split) + (P(),) * 9,
        check_vma=False,
    )
```

```python
import functools
import math

import jax
import jax.numpy as jnp
from jax import lax
from jax.experimental import pallas as pl
from jax.experimental.pallas import tpu as pltpu
from jax.sharding import PartitionSpec as P

norm_epsilon = 1e-06
inv_root_two = 0.7071067811865476
inv_root_tau = 0.3989422804014327

LANES = 128
EDGE = 8
BAND = 16
AXES = ("gy", "gx", "rep")
f32 = jnp.float32
bf16 = jnp.bfloat16


def dot(a, b, dims):
    return lax.dot_general(a, b, (dims, ((), ())), preferred_element_type=f32)


NN = ((1,), (0,))
NT = ((1,), (1,))
TN = ((0,), (0,))


def pair_rounds(count):
    first = [(i, i + 1) for i in range(0, count - 1, 2)]
    second = [(i, i + 1) for i in range(1, count - 1, 2)]
    return [pairs + [(b, a) for a, b in pairs] for pairs in (first, second)]


def halo(tile, even_y, even_x):
    rows, cols, _ = tile.shape

    def swap_edges(low, high, axis, even):
        got = []
        for pairs, is_high in zip(pair_rounds(lax.axis_size(axis)), (even, ~even)):
            if pairs:
                got.append(lax.ppermute(jnp.where(is_high, high, low), axis, pairs))
            else:
                got.append(jnp.zeros_like(low))
        return jnp.where(even, got[1], got[0]), jnp.where(even, got[0], got[1])

    top, bottom = swap_edges(tile[:3], tile[rows - 3 :], "gy", even_y)
    column = [
        jnp.concatenate([part[:, at : at + 3] for part in (top, tile, bottom)], axis=0) for at in (0, cols - 3)
    ]
    left, right = swap_edges(*column, "gx", even_x)
    return top, bottom, left, right


def fill(pad, tile, top, bottom, left, right):
    rows, cols, channels = tile.shape
    for slab in range(channels // LANES):
        at = slice(slab * LANES, (slab + 1) * LANES)
        pad[slab, 0:3, EDGE : EDGE + cols, :] = top[:, :, at].astype(f32)
        pad[slab, 3 + rows :, EDGE : EDGE + cols, :] = bottom[:, :, at].astype(f32)
        pad[slab, :, EDGE - 3 : EDGE, :] = left[:, :, at].astype(f32)
        pad[slab, :, EDGE + cols : EDGE + cols + 3, :] = right[:, :, at].astype(f32)

        def body(row, _):
            pad[slab, row + 3, EDGE : EDGE + cols, :] = tile[row, :, at].astype(f32)
            return _

        lax.fori_loop(0, rows, body, 0, unroll=4)


def steps(rows, cols, channels, body):
    slabs, tiles, bands = channels // LANES, cols // 8, rows // BAND

    def step(i, _):
        slab = i // (tiles * bands)
        rest = i % (tiles * bands)
        body(slab, pl.multiple_of(rest // bands * 8, 8), rest % bands * BAND)
        return _

    lax.fori_loop(0, slabs * tiles * bands, step, 0)


def lanes(slab):
    return pl.ds(pl.multiple_of(slab * LANES, LANES), LANES)


def taps(pad, kernel, slab, col, row, flip):
    acc = [None] * BAND
    for b in range(7):
        scale = []
        for a in range(7):
            tap = (6 - a) * 7 + 6 - b if flip else a * 7 + b
            scale.append(jnp.broadcast_to(kernel[pl.ds(tap, 1), lanes(slab)], (8, LANES)))
        for r in range(BAND + 6):
            x = pad[slab, row + r, pl.ds(col + EDGE - 3 + b, 8), :]
            for a in range(7):
                i = r - a
                if 0 <= i < BAND:
                    acc[i] = x * scale[a] if acc[i] is None else acc[i] + x * scale[a]
    return acc


def conv_norm_kernel(
    tile, top, bottom, left, right, kernel, bias, gain, shift, normed_ref, inv_ref, ln_ref, pad, depth
):
    rows, cols, channels = tile.shape
    fill(pad, tile, top, bottom, left, right)

    def piece(slab, col, row):
        acc = taps(pad, kernel, slab, col, row, False)
        add = jnp.broadcast_to(bias[:, lanes(slab)], (8, LANES))
        for i in range(BAND):
            at = pl.ds(pl.multiple_of((row + i) * cols + col, 8), 8)
            depth[at, lanes(slab)] = acc[i] + add

    steps(rows, cols, channels, piece)
    block = 128

    def norm(i, _):
        at = pl.ds(pl.multiple_of(i * block, block), block)
        x = depth[at, :]
        centred = x - jnp.mean(x, axis=-1, keepdims=True)
        inv = lax.rsqrt(jnp.mean(centred * centred, axis=-1, keepdims=True) + norm_epsilon)
        normed = centred * inv
        normed_ref[at, :] = normed
        inv_ref[at, :] = jnp.broadcast_to(inv, (block, LANES))
        ln_ref[at, :] = (normed * gain[...] + shift[...]).astype(bf16)
        return _

    lax.fori_loop(0, rows * cols // block, norm, 0)


def gelu_pair(u):
    cdf = 0.5 * (1.0 + lax.erf(u * inv_root_two))
    pdf = jnp.exp(-0.5 * u * u) * inv_root_tau
    return u * cdf, cdf + u * pdf


def fold(x):
    return jnp.sum(x.reshape(-1, 8, x.shape[1]), axis=0)


def mlp_block(ln, d_branch, w_in, w_out, b_in, base, width, hid_ref, dpre_ref, gbin):
    sub = 256
    count = width // sub

    def products(s):
        at = pl.ds(base + s * sub, sub)
        return dot(ln, w_in[at, :], NT), dot(d_branch, w_out[:, at], NN)

    ahead = products(0)
    for s in range(count):
        pre, d_hidden = ahead
        if s + 1 < count:
            ahead = products(s + 1)
        act, slope = gelu_pair(pre + b_in[:, base + s * sub : base + (s + 1) * sub])
        d_pre = d_hidden * slope
        gbin[:, s * sub : (s + 1) * sub] += fold(d_pre)
        hid_ref[:, s * sub : (s + 1) * sub] = act.astype(bf16)
        dpre_ref[:, s * sub : (s + 1) * sub] = d_pre.astype(bf16)
    at = pl.ds(base, width)
    hidden, d_pre = hid_ref[...], dpre_ref[...]
    branch = dot(hidden, w_out[:, at], NT)
    d_norm = dot(d_pre, w_in[at, :], NN)
    return hidden, d_pre, branch, d_norm


def pack_grads(core, keep, send, gwin, gwout, gbin_ref, gbin):
    width, channels = gwin.shape

    def store(first, second):
        for j in range(channels // LANES):
            first[j * width : (j + 1) * width, :] = gwin[:, j * LANES : (j + 1) * LANES].astype(bf16)
        for j in range(width // LANES):
            second[j * channels : (j + 1) * channels, :] = gwout[
                :, j * LANES : (j + 1) * LANES
            ].astype(bf16)

    pl.when(core[0] == 0)(lambda: store(keep, send))
    pl.when(core[0] != 0)(lambda: store(send, keep))
    gbin_ref[...] = jnp.sum(gbin[...], axis=0, keepdims=True)


MLP_BLOCK = 256


def mlp_first_kernel(
    base, width, core, ln_ref, cot, w_in, w_out, b_in, scale, branch_ref, dnorm_ref, keep, send, gbin_ref,
    hid_ref, dpre_ref, gwin, gwout, gbin,
):
    gwin[...] = jnp.zeros_like(gwin)
    gwout[...] = jnp.zeros_like(gwout)
    gbin[...] = jnp.zeros_like(gbin)

    def step(i, _):
        at = pl.ds(pl.multiple_of(i * MLP_BLOCK, MLP_BLOCK), MLP_BLOCK)
        ln = ln_ref[at, :]
        d_branch = (scale[...] * cot[at, :].astype(f32)).astype(bf16)
        hidden, d_pre, branch, d_norm = mlp_block(
            ln, d_branch, w_in, w_out, b_in, base, width, hid_ref, dpre_ref, gbin
        )
        branch_ref[at, :] = branch
        dnorm_ref[at, :] = d_norm
        gwin[...] += dot(d_pre, ln, TN)
        gwout[...] += dot(d_branch, hidden, TN)
        return _

    lax.fori_loop(0, ln_ref.shape[0] // MLP_BLOCK, step, 0)
    pack_grads(core, keep, send, gwin, gwout, gbin_ref, gbin)


def mlp_second_kernel(
    base, width, core, ln_ref, cot, w_in, w_out, b_in, scale, b_out, gain, page, normed_ref, inv_ref,
    branch_ref, dnorm_ref,
    result, d_depth_ref, keep, send, gbin_ref, sums_ref,
    hid_ref, dpre_ref, gwin, gwout, gbin, sums,
):
    gwin[...] = jnp.zeros_like(gwin)
    gwout[...] = jnp.zeros_like(gwout)
    gbin[...] = jnp.zeros_like(gbin)
    sums[...] = jnp.zeros_like(sums)

    def step(i, _):
        at = pl.ds(pl.multiple_of(i * MLP_BLOCK, MLP_BLOCK), MLP_BLOCK)
        ln = ln_ref[at, :]
        cot32 = cot[at, :].astype(f32)
        d_branch32 = scale[...] * cot32
        d_branch = d_branch32.astype(bf16)
        hidden, d_pre, branch, d_norm = mlp_block(
            ln, d_branch, w_in, w_out, b_in, base, width, hid_ref, dpre_ref, gbin
        )
        gwin[...] += dot(d_pre, ln, TN)
        gwout[...] += dot(d_branch, hidden, TN)
        branch = branch + branch_ref[at, :] + b_out[...]
        result[at, :] = (page[at, :].astype(f32) + scale[...] * branch).astype(bf16)
        d_norm = d_norm + dnorm_ref[at, :]
        normed = normed_ref[at, :]
        inv = inv_ref[at, 0:1]
        weighted = d_norm * normed
        s = d_norm * gain[...]
        mean_s = jnp.mean(s, axis=-1, keepdims=True)
        mean_sn = jnp.mean(s * normed, axis=-1, keepdims=True)
        d_depth = (inv * (s - mean_s - normed * mean_sn)).astype(bf16)
        d_depth_ref[at, :] = d_depth
        sums[0] += fold(cot32 * branch)
        sums[1] += fold(d_branch32)
        sums[2] += fold(weighted)
        sums[3] += fold(d_norm)
        sums[4] += fold(d_depth.astype(f32))
        return _

    lax.fori_loop(0, ln_ref.shape[0] // MLP_BLOCK, step, 0)
    pack_grads(core, keep, send, gwin, gwout, gbin_ref, gbin)
    for j in range(5):
        sums_ref[j : j + 1, :] = jnp.sum(sums[j], axis=0, keepdims=True)


SMALL = 64


def kernel_grad_kernel(
    core, tile, top, bottom, left, right, d_depth, sums, gbin_a, gbin_b, keep, send, pad, d32, acc_ref
):
    rows, cols, channels = tile.shape
    fill(pad, tile, top, bottom, left, right)
    d32[...] = d_depth[...].astype(f32)
    acc_ref[...] = jnp.zeros_like(acc_ref)

    def piece(slab, col, row):
        grads = []
        for i in range(BAND):
            at = pl.ds(pl.multiple_of((row + i) * cols + col, 8), 8)
            grads.append(d32[at, lanes(slab)])
        for b in range(7):
            acc = [None] * 7
            for r in range(BAND + 6):
                x = pad[slab, row + r, pl.ds(col + EDGE - 3 + b, 8), :]
                for a in range(7):
                    i = r - a
                    if 0 <= i < BAND:
                        acc[a] = x * grads[i] if acc[a] is None else acc[a] + x * grads[i]
            for a in range(7):
                acc_ref[slab, a * 7 + b] += acc[a]

    steps(rows, cols, channels, piece)

    def store(first, second):
        second[...] = jnp.zeros_like(second)
        slabs = channels // LANES
        for slab in range(slabs):
            at = slice(slab * LANES, (slab + 1) * LANES)
            part = [jnp.sum(acc_ref[slab], axis=1), sums[:5, at]]
            for j in range((gbin_a.shape[1] + gbin_b.shape[1]) // channels):
                lane = (j * slabs + slab) * LANES
                source = gbin_a if lane < gbin_a.shape[1] else gbin_b
                lane = lane if lane < gbin_a.shape[1] else lane - gbin_a.shape[1]
                part.append(source[:, lane : lane + LANES])
            part = jnp.concatenate(part)
            part = jnp.concatenate([part, jnp.zeros((SMALL - part.shape[0], LANES), f32)])
            first[slab * SMALL : (slab + 1) * SMALL, :] = part.astype(bf16)
        rest = first.shape[0] - slabs * SMALL
        first[slabs * SMALL :, :] = jnp.zeros((rest, LANES), bf16)

    pl.when(core[0] == 0)(lambda: store(keep, send))
    pl.when(core[0] != 0)(lambda: store(send, keep))


def conv_grad_kernel(tile, top, bottom, left, right, kernel, cot, out, pad, total):
    rows, cols, channels = tile.shape
    fill(pad, tile, top, bottom, left, right)

    def piece(slab, col, row):
        acc = taps(pad, kernel, slab, col, row, True)
        for i in range(BAND):
            at = pl.ds(pl.multiple_of((row + i) * cols + col, 8), 8)
            total[at, lanes(slab)] = acc[i]

    steps(rows, cols, channels, piece)
    block = 128

    def finish(i, _):
        at = pl.ds(pl.multiple_of(i * block, block), block)
        out[at, :] = (cot[at, :].astype(f32) + total[at, :]).astype(bf16)
        return _

    lax.fori_loop(0, rows * cols // block, finish, 0)


def call(body, outs, scratch, args, flops, scalars=0, after=(), size=24 << 20):
    held = len(args)

    def kernel(*refs):
        body(*refs[:held], *refs[held + len(after) :])

    vmem = pl.BlockSpec(memory_space=pltpu.VMEM)
    smem = pl.BlockSpec(memory_space=pltpu.SMEM)
    return pl.pallas_call(
        kernel,
        out_shape=[jax.ShapeDtypeStruct(shape, dtype) for shape, dtype in outs],
        in_specs=[smem] * scalars
        + [vmem] * (held - scalars)
        + [pl.BlockSpec(memory_space=pl.ANY)] * len(after),
        out_specs=[vmem] * len(outs),
        scratch_shapes=[pltpu.VMEM(shape, dtype) for shape, dtype in scratch],
        compiler_params=pltpu.CompilerParams(vmem_limit_bytes=size),
        cost_estimate=pl.CostEstimate(flops=flops, bytes_accessed=flops >> 10, transcendentals=0),
    )(*args, *after)


def groups():
    sizes = [lax.axis_size(axis) for axis in AXES]
    near = sizes[1] * sizes[2]
    return [[i for i in range(math.prod(sizes)) if i // near % 2 == core] for core in range(2)]


def exchange(x, flips):
    sizes = [lax.axis_size(axis) for axis in AXES]
    perm = []
    for i in range(math.prod(sizes)):
        at = {"gy": i // (sizes[1] * sizes[2]), "gx": i // sizes[2] % sizes[1], "rep": i % sizes[2]}
        for axis, bit in flips:
            at[axis] ^= 1 << bit
        perm.append((i, (at["gy"] * sizes[1] + at["gx"]) * sizes[2] + at["rep"]))
    return lax.ppermute(x, AXES, perm)


def swap(x):
    return lax.all_to_all(x, AXES, 0, 0, axis_index_groups=groups(), tiled=True)


def hold(arrays):
    return lax.optimization_barrier(arrays)


def chunks(rows, body):
    size = max(n for n in (128, 64, 32, 16) if rows % n == 0)

    def step(i, _):
        body(pl.multiple_of(i * size, size), size)
        return _

    lax.fori_loop(0, rows // size, step, 0, unroll=2 if rows // size > 1 else 1)


def first_sum_kernel(*refs):
    out = refs[-1]
    start = 0
    for one, two in zip(refs[:-1:2], refs[1:-1:2]):

        def add(at, size):
            part = pl.ds(at, size)
            to = pl.ds(pl.multiple_of(start + at, 16), size)
            out[to, :] = (one[part, :].astype(f32) + two[part, :].astype(f32)).astype(bf16)

        chunks(one.shape[0], add)
        start += one.shape[0]
    if start < out.shape[0]:
        out[start:, :] = jnp.zeros((out.shape[0] - start, LANES), bf16)


def sum_kernel(got, out):
    count, rows, _ = got.shape

    def add(at, size):
        total = got[0, pl.ds(at, size), :].astype(f32)
        for j in range(1, count):
            total = total + got[j, pl.ds(at, size), :].astype(f32)
        total = total.astype(bf16)
        for j in range(count):
            out[j, pl.ds(at, size), :] = total

    chunks(rows, add)


SUM_FLOPS = 1 << 20


def add_halves(*halves):
    count = len(groups()[0])
    rows = sum(x.shape[0] for x in halves[::2])
    rows = -(-rows // (16 * count)) * 16 * count
    (x,) = call(first_sum_kernel, [((rows, LANES), bf16)], [], halves, SUM_FLOPS)
    return x


def add_parts(x, after=()):
    parts = x.reshape(len(groups()[0]), -1, LANES)
    (y,) = call(sum_kernel, [(parts.shape, bf16)], [], (parts,), SUM_FLOPS, 0, after)
    return y.reshape(x.shape)


def finish_kernel(
    factor, widths, core, own_a, other_a, own_b, other_b,
    win, wout, gk, scale, b_out, gain, shift, bias, b_in,
):
    channels = wout.shape[0]

    def store(firsts, seconds):
        base = 0
        for width, first, second in zip(widths, firsts, seconds):
            for j in range(channels // LANES):
                win[base : base + width, j * LANES : (j + 1) * LANES] = (
                    first[j * width : (j + 1) * width, :].astype(f32) * factor
                )
            for j in range(width // LANES):
                wout[:, base + j * LANES : base + (j + 1) * LANES] = (
                    second[j * channels : (j + 1) * channels, :].astype(f32) * factor
                )
            base += width
        slabs = channels // LANES
        for slab in range(slabs):
            at = slice(slab * LANES, (slab + 1) * LANES)
            start = widths[1] * channels // LANES + slab * SMALL
            values = firsts[1][start : start + SMALL, :].astype(f32) * factor
            for j in range(7):
                gk[j, :, at] = values[7 * j : 7 * j + 7]
            for j, ref in enumerate((scale, b_out, gain, shift, bias)):
                ref[at] = values[49 + j]
            for j in range(b_in.shape[0] // channels):
                lane = (j * slabs + slab) * LANES
                b_in[lane : lane + LANES] = values[54 + j]

    pl.when(core[0] == 0)(lambda: store((own_a, own_b), (other_a, other_b)))
    pl.when(core[0] != 0)(lambda: store((other_a, other_b), (own_a, own_b)))


def shards(
    pages,
    cotangent,
    conv_kernel,
    conv_bias,
    norm_gain,
    norm_bias,
    w_in,
    b_in,
    w_out,
    b_out,
    layer_scale,
):
    _, rows, cols, channels = pages.shape
    hid = w_in.shape[0]
    pixels = rows * cols
    tile = pages.reshape(rows, cols, channels)
    page = pages.reshape(pixels, channels)
    cot = cotangent.reshape(pixels, channels)
    kernel = conv_kernel.reshape(49, channels)
    row = lambda v: v.reshape(1, -1)
    gain, shift, scale = row(norm_gain), row(norm_bias), row(layer_scale)
    pad = ((channels // LANES, rows + 6, EDGE + cols + 8, LANES), f32)
    full = (pixels, channels)

    even_y = lax.axis_index("gy") % 2 == 0
    even_x = lax.axis_index("gx") % 2 == 0
    core = (lax.axis_index("gy") % 2).astype(jnp.int32).reshape(1)
    even_y, even_x, core, tile = hold((even_y, even_x, core, tile))
    around = halo(tile, even_y, even_x)
    conv_flops = 2 * 49 * pixels * channels * 60
    normed, inv, ln_out = call(
        conv_norm_kernel,
        [(full, f32), ((pixels, LANES), f32), (full, bf16)],
        [pad, (full, f32)],
        (tile, *around, kernel, row(conv_bias), gain, shift),
        conv_flops,
    )
    grads = lambda width: [
        ((MLP_BLOCK, width), bf16),
        ((MLP_BLOCK, width), bf16),
        ((width, channels), f32),
        ((channels, width), f32),
        ((8, width), f32),
    ]
    packed = lambda width: [((width * channels // LANES, LANES), bf16)] * 2 + [((1, width), f32)]
    core_flip = [("gy", 0)]
    mlp_flops = 12 * pixels * channels * hid
    weights = (w_in, w_out, row(b_in), scale)
    first, second = hid * 2 // 3, hid // 3
    branch, d_norm, keep_a, send_a, gbin_a = call(
        functools.partial(mlp_first_kernel, 0, first),
        [(full, f32), (full, f32)] + packed(first),
        grads(first),
        (core, ln_out, cot, *weights),
        mlp_flops,
        1,
    )
    other_a = exchange(send_a, core_flip)
    result, d_depth, keep_b, send_b, gbin_b, sums = call(
        functools.partial(mlp_second_kernel, first, second),
        [(full, bf16), (full, bf16)] + packed(second) + [((8, channels), f32)],
        grads(second) + [((8, 8, channels), f32)],
        (core, ln_out, cot, *weights, row(b_out), gain, page, normed, inv, branch, d_norm),
        mlp_flops,
        1,
    )
    d_tile = d_depth.reshape(tile.shape)
    other_a, d_tile, keep_b, send_b = hold((other_a, d_tile, keep_b, send_b))
    parts_a = add_halves(keep_a, other_a)
    got_a = swap(parts_a)
    other_b = exchange(send_b, core_flip)
    d_around = halo(d_tile, even_y, even_x)
    small_rows = ((4 * SMALL, LANES), bf16)
    keep_s, send_s = call(
        kernel_grad_kernel,
        [small_rows, small_rows],
        [pad, (full, f32), ((channels // LANES, 49, 8, LANES), f32)],
        (core, tile, *around, d_tile.reshape(full), sums, gbin_a, gbin_b),
        conv_flops,
        1,
        (parts_a,),
    )
    keep_s, send_s, other_b = hold((keep_s, send_s, other_b))
    other_s = exchange(send_s, core_flip)
    parts_b = add_halves(keep_b, other_b, keep_s, other_s)
    got_b = swap(parts_b)
    (grad_pages,) = call(
        conv_grad_kernel,
        [(full, bf16)],
        [pad, (full, f32)],
        (d_tile, *d_around, kernel, cot),
        conv_flops,
        0,
        (parts_b,),
    )
    got_a, grad_pages = hold((got_a, grad_pages))
    sum_a = add_parts(got_a)
    half_a = swap(sum_a)
    half_b = swap(add_parts(got_b, (sum_a,)))
    got_a = [half_a, exchange(half_a, core_flip)]
    got_b = [half_b, exchange(half_b, core_flip)]
    factor = float(pixels * lax.axis_size("gy") * lax.axis_size("gx") * lax.axis_size("rep")) ** (-0.5)
    line = ((channels,), f32)
    win, wout, gk, g_scale, g_bout, g_gain, g_shift, g_bias, g_bin = call(
        functools.partial(finish_kernel, factor, (first, second)),
        [((hid, channels), f32), ((channels, hid), f32), ((7, 7, channels), f32)] + [line] * 5 + [((hid,), f32)],
        [],
        (core, *got_a, *got_b),
        SUM_FLOPS,
        1,
    )
    return (
        result.reshape(pages.shape),
        grad_pages.reshape(pages.shape),
        gk,
        g_bias,
        g_gain,
        g_shift,
        win,
        g_bin,
        wout,
        g_bout,
        g_scale,
    )


def solution(mesh):
    split = P("rep", "gy", "gx", None)
    return jax.shard_map(
        shards,
        mesh=mesh,
        in_specs=(split, split) + (P(),) * 9,
        out_specs=(split, split) + (P(),) * 9,
        check_vma=False,
    )
```

```python
import functools
import math

import jax
import jax.numpy as jnp
from jax import lax
from jax.experimental import pallas as pl
from jax.experimental.pallas import tpu as pltpu
from jax.sharding import PartitionSpec as P

norm_epsilon = 1e-06
inv_root_two = 0.7071067811865476
inv_root_tau = 0.3989422804014327

LANES = 128
EDGE = 8
BAND = 16
AXES = ("gy", "gx", "rep")
f32 = jnp.float32
bf16 = jnp.bfloat16


def dot(a, b, dims):
    return lax.dot_general(a, b, (dims, ((), ())), preferred_element_type=f32)


NN = ((1,), (0,))
NT = ((1,), (1,))
TN = ((0,), (0,))


def pair_rounds(count):
    first = [(i, i + 1) for i in range(0, count - 1, 2)]
    second = [(i, i + 1) for i in range(1, count - 1, 2)]
    return [pairs + [(b, a) for a, b in pairs] for pairs in (first, second)]


def halo(tile, even_y, even_x):
    rows, cols, _ = tile.shape

    def swap_edges(low, high, axis, even):
        got = []
        for pairs, is_high in zip(pair_rounds(lax.axis_size(axis)), (even, ~even)):
            if pairs:
                got.append(lax.ppermute(jnp.where(is_high, high, low), axis, pairs))
            else:
                got.append(jnp.zeros_like(low))
        return jnp.where(even, got[1], got[0]), jnp.where(even, got[0], got[1])

    top, bottom = swap_edges(tile[:3], tile[rows - 3 :], "gy", even_y)
    column = [
        jnp.concatenate([part[:, at : at + 3] for part in (top, tile, bottom)], axis=0) for at in (0, cols - 3)
    ]
    left, right = swap_edges(*column, "gx", even_x)
    return top, bottom, left, right


def fill(pad, tile, top, bottom, left, right):
    rows, cols, channels = tile.shape
    for slab in range(channels // LANES):
        at = slice(slab * LANES, (slab + 1) * LANES)
        pad[slab, 0:3, EDGE : EDGE + cols, :] = top[:, :, at].astype(f32)
        pad[slab, 3 + rows :, EDGE : EDGE + cols, :] = bottom[:, :, at].astype(f32)
        pad[slab, :, EDGE - 3 : EDGE, :] = left[:, :, at].astype(f32)
        pad[slab, :, EDGE + cols : EDGE + cols + 3, :] = right[:, :, at].astype(f32)

        def body(row, _):
            pad[slab, row + 3, EDGE : EDGE + cols, :] = tile[row, :, at].astype(f32)
            return _

        lax.fori_loop(0, rows, body, 0, unroll=4)


def steps(rows, cols, channels, body):
    slabs, tiles, bands = channels // LANES, cols // 8, rows // BAND

    def step(i, _):
        slab = i // (tiles * bands)
        rest = i % (tiles * bands)
        body(slab, pl.multiple_of(rest // bands * 8, 8), rest % bands * BAND)
        return _

    lax.fori_loop(0, slabs * tiles * bands, step, 0)


def lanes(slab):
    return pl.ds(pl.multiple_of(slab * LANES, LANES), LANES)


def taps(pad, kernel, slab, col, row, flip):
    acc = [None] * BAND
    for b in range(7):
        scale = []
        for a in range(7):
            tap = (6 - a) * 7 + 6 - b if flip else a * 7 + b
            scale.append(jnp.broadcast_to(kernel[pl.ds(tap, 1), lanes(slab)], (8, LANES)))
        for r in range(BAND + 6):
            x = pad[slab, row + r, pl.ds(col + EDGE - 3 + b, 8), :]
            for a in range(7):
                i = r - a
                if 0 <= i < BAND:
                    acc[i] = x * scale[a] if acc[i] is None else acc[i] + x * scale[a]
    return acc


def conv_norm_kernel(
    tile, top, bottom, left, right, kernel, bias, gain, shift, normed_ref, inv_ref, ln_ref, pad, depth
):
    rows, cols, channels = tile.shape
    fill(pad, tile, top, bottom, left, right)

    def piece(slab, col, row):
        acc = taps(pad, kernel, slab, col, row, False)
        add = jnp.broadcast_to(bias[:, lanes(slab)], (8, LANES))
        for i in range(BAND):
            at = pl.ds(pl.multiple_of((row + i) * cols + col, 8), 8)
            depth[at, lanes(slab)] = acc[i] + add

    steps(rows, cols, channels, piece)
    block = 128

    def norm(i, _):
        at = pl.ds(pl.multiple_of(i * block, block), block)
        x = depth[at, :]
        centred = x - jnp.mean(x, axis=-1, keepdims=True)
        inv = lax.rsqrt(jnp.mean(centred * centred, axis=-1, keepdims=True) + norm_epsilon)
        normed = centred * inv
        normed_ref[at, :] = normed
        inv_ref[at, :] = jnp.broadcast_to(inv, (block, LANES))
        ln_ref[at, :] = (normed * gain[...] + shift[...]).astype(bf16)
        return _

    lax.fori_loop(0, rows * cols // block, norm, 0)


def gelu_pair(u):
    cdf = 0.5 * (1.0 + lax.erf(u * inv_root_two))
    pdf = jnp.exp(-0.5 * u * u) * inv_root_tau
    return u * cdf, cdf + u * pdf


def fold(x):
    return jnp.sum(x.reshape(-1, 8, x.shape[1]), axis=0)


def mlp_block(ln, d_branch, w_in, w_out, b_in, base, width, hid_ref, dpre_ref, gbin):
    sub = 256
    count = width // sub

    def products(s):
        at = pl.ds(base + s * sub, sub)
        return dot(ln, w_in[at, :], NT), dot(d_branch, w_out[:, at], NN)

    ahead = products(0)
    for s in range(count):
        pre, d_hidden = ahead
        if s + 1 < count:
            ahead = products(s + 1)
        act, slope = gelu_pair(pre + b_in[:, base + s * sub : base + (s + 1) * sub])
        d_pre = d_hidden * slope
        gbin[:, s * sub : (s + 1) * sub] += fold(d_pre)
        hid_ref[:, s * sub : (s + 1) * sub] = act.astype(bf16)
        dpre_ref[:, s * sub : (s + 1) * sub] = d_pre.astype(bf16)
    at = pl.ds(base, width)
    hidden, d_pre = hid_ref[...], dpre_ref[...]
    branch = dot(hidden, w_out[:, at], NT)
    d_norm = dot(d_pre, w_in[at, :], NN)
    return hidden, d_pre, branch, d_norm


def pack_grads(core, keep, send, gwin, gwout, gbin_ref, gbin):
    width, channels = gwin.shape

    def store(first, second):
        for j in range(channels // LANES):
            first[j * width : (j + 1) * width, :] = gwin[:, j * LANES : (j + 1) * LANES].astype(bf16)
        for j in range(width // LANES):
            second[j * channels : (j + 1) * channels, :] = gwout[
                :, j * LANES : (j + 1) * LANES
            ].astype(bf16)

    pl.when(core[0] == 0)(lambda: store(keep, send))
    pl.when(core[0] != 0)(lambda: store(send, keep))
    gbin_ref[...] = jnp.sum(gbin[...], axis=0, keepdims=True)


MLP_BLOCK = 256


def mlp_first_kernel(
    base, width, core, ln_ref, cot, w_in, w_out, b_in, scale, branch_ref, dnorm_ref, keep, send, gbin_ref,
    hid_ref, dpre_ref, gwin, gwout, gbin,
):
    gwin[...] = jnp.zeros_like(gwin)
    gwout[...] = jnp.zeros_like(gwout)
    gbin[...] = jnp.zeros_like(gbin)

    def step(i, _):
        at = pl.ds(pl.multiple_of(i * MLP_BLOCK, MLP_BLOCK), MLP_BLOCK)
        ln = ln_ref[at, :]
        d_branch = (scale[...] * cot[at, :].astype(f32)).astype(bf16)
        hidden, d_pre, branch, d_norm = mlp_block(
            ln, d_branch, w_in, w_out, b_in, base, width, hid_ref, dpre_ref, gbin
        )
        branch_ref[at, :] = branch
        dnorm_ref[at, :] = d_norm
        gwin[...] += dot(d_pre, ln, TN)
        gwout[...] += dot(d_branch, hidden, TN)
        return _

    lax.fori_loop(0, ln_ref.shape[0] // MLP_BLOCK, step, 0)
    pack_grads(core, keep, send, gwin, gwout, gbin_ref, gbin)


def mlp_second_kernel(
    base, width, core, ln_ref, cot, w_in, w_out, b_in, scale, b_out, gain, page, normed_ref, inv_ref,
    branch_ref, dnorm_ref,
    result, d_depth_ref, keep, send, gbin_ref, sums_ref,
    hid_ref, dpre_ref, gwin, gwout, gbin, sums,
):
    gwin[...] = jnp.zeros_like(gwin)
    gwout[...] = jnp.zeros_like(gwout)
    gbin[...] = jnp.zeros_like(gbin)
    sums[...] = jnp.zeros_like(sums)

    def step(i, _):
        at = pl.ds(pl.multiple_of(i * MLP_BLOCK, MLP_BLOCK), MLP_BLOCK)
        ln = ln_ref[at, :]
        cot32 = cot[at, :].astype(f32)
        d_branch32 = scale[...] * cot32
        d_branch = d_branch32.astype(bf16)
        hidden, d_pre, branch, d_norm = mlp_block(
            ln, d_branch, w_in, w_out, b_in, base, width, hid_ref, dpre_ref, gbin
        )
        gwin[...] += dot(d_pre, ln, TN)
        gwout[...] += dot(d_branch, hidden, TN)
        branch = branch + branch_ref[at, :] + b_out[...]
        result[at, :] = (page[at, :].astype(f32) + scale[...] * branch).astype(bf16)
        d_norm = d_norm + dnorm_ref[at, :]
        normed = normed_ref[at, :]
        inv = inv_ref[at, 0:1]
        weighted = d_norm * normed
        s = d_norm * gain[...]
        mean_s = jnp.mean(s, axis=-1, keepdims=True)
        mean_sn = jnp.mean(s * normed, axis=-1, keepdims=True)
        d_depth = (inv * (s - mean_s - normed * mean_sn)).astype(bf16)
        d_depth_ref[at, :] = d_depth
        sums[0] += fold(cot32 * branch)
        sums[1] += fold(d_branch32)
        sums[2] += fold(weighted)
        sums[3] += fold(d_norm)
        sums[4] += fold(d_depth.astype(f32))
        return _

    lax.fori_loop(0, ln_ref.shape[0] // MLP_BLOCK, step, 0)
    pack_grads(core, keep, send, gwin, gwout, gbin_ref, gbin)
    for j in range(5):
        sums_ref[j : j + 1, :] = jnp.sum(sums[j], axis=0, keepdims=True)


SMALL = 64


def kernel_grad_kernel(
    core, tile, top, bottom, left, right, d_depth, sums, gbin_a, gbin_b, keep, send, pad, d32, acc_ref
):
    rows, cols, channels = tile.shape
    fill(pad, tile, top, bottom, left, right)
    d32[...] = d_depth[...].astype(f32)
    acc_ref[...] = jnp.zeros_like(acc_ref)

    def piece(slab, col, row):
        grads = []
        for i in range(BAND):
            at = pl.ds(pl.multiple_of((row + i) * cols + col, 8), 8)
            grads.append(d32[at, lanes(slab)])
        for b in range(7):
            acc = [None] * 7
            for r in range(BAND + 6):
                x = pad[slab, row + r, pl.ds(col + EDGE - 3 + b, 8), :]
                for a in range(7):
                    i = r - a
                    if 0 <= i < BAND:
                        acc[a] = x * grads[i] if acc[a] is None else acc[a] + x * grads[i]
            for a in range(7):
                acc_ref[slab, a * 7 + b] += acc[a]

    steps(rows, cols, channels, piece)

    def store(first, second):
        second[...] = jnp.zeros_like(second)
        slabs = channels // LANES
        for slab in range(slabs):
            at = slice(slab * LANES, (slab + 1) * LANES)
            part = [jnp.sum(acc_ref[slab], axis=1), sums[:5, at]]
            for j in range((gbin_a.shape[1] + gbin_b.shape[1]) // channels):
                lane = (j * slabs + slab) * LANES
                source = gbin_a if lane < gbin_a.shape[1] else gbin_b
                lane = lane if lane < gbin_a.shape[1] else lane - gbin_a.shape[1]
                part.append(source[:, lane : lane + LANES])
            part = jnp.concatenate(part)
            part = jnp.concatenate([part, jnp.zeros((SMALL - part.shape[0], LANES), f32)])
            first[slab * SMALL : (slab + 1) * SMALL, :] = part.astype(bf16)
        rest = first.shape[0] - slabs * SMALL
        first[slabs * SMALL :, :] = jnp.zeros((rest, LANES), bf16)

    pl.when(core[0] == 0)(lambda: store(keep, send))
    pl.when(core[0] != 0)(lambda: store(send, keep))


def conv_grad_kernel(tile, top, bottom, left, right, kernel, cot, out, pad, total):
    rows, cols, channels = tile.shape
    fill(pad, tile, top, bottom, left, right)

    def piece(slab, col, row):
        acc = taps(pad, kernel, slab, col, row, True)
        for i in range(BAND):
            at = pl.ds(pl.multiple_of((row + i) * cols + col, 8), 8)
            total[at, lanes(slab)] = acc[i]

    steps(rows, cols, channels, piece)
    block = 128

    def finish(i, _):
        at = pl.ds(pl.multiple_of(i * block, block), block)
        out[at, :] = (cot[at, :].astype(f32) + total[at, :]).astype(bf16)
        return _

    lax.fori_loop(0, rows * cols // block, finish, 0)


def call(body, outs, scratch, args, flops, scalars=0, after=(), size=24 << 20):
    held = len(args)

    def kernel(*refs):
        body(*refs[:held], *refs[held + len(after) :])

    vmem = pl.BlockSpec(memory_space=pltpu.VMEM)
    smem = pl.BlockSpec(memory_space=pltpu.SMEM)
    return pl.pallas_call(
        kernel,
        out_shape=[jax.ShapeDtypeStruct(shape, dtype) for shape, dtype in outs],
        in_specs=[smem] * scalars
        + [vmem] * (held - scalars)
        + [pl.BlockSpec(memory_space=pl.ANY)] * len(after),
        out_specs=[vmem] * len(outs),
        scratch_shapes=[pltpu.VMEM(shape, dtype) for shape, dtype in scratch],
        compiler_params=pltpu.CompilerParams(vmem_limit_bytes=size),
        cost_estimate=pl.CostEstimate(flops=flops, bytes_accessed=flops >> 10, transcendentals=0),
    )(*args, *after)


def bits(axis):
    return [(axis, j) for j in range(max(lax.axis_size(axis).bit_length() - 1, 0))]


def plane():
    return [("gy", 1), ("gx", 0)]


def beyond():
    return bits("gy")[2:] + bits("gx")[1:] + bits("rep")


def exchange(x, flips):
    sizes = [lax.axis_size(axis) for axis in AXES]
    perm = []
    for i in range(math.prod(sizes)):
        at = {"gy": i // (sizes[1] * sizes[2]), "gx": i // sizes[2] % sizes[1], "rep": i % sizes[2]}
        for axis, bit in flips:
            at[axis] ^= 1 << bit
        perm.append((i, (at["gy"] * sizes[1] + at["gx"]) * sizes[2] + at["rep"]))
    return lax.ppermute(x, AXES, perm)


def spread(parts):
    flips = [[g for j, g in enumerate(plane()) if delta >> j & 1] for delta in range(1, 4)]
    return [parts[0]] + [exchange(x, flip) for x, flip in zip(parts[1:], flips)]


def hold(arrays):
    return lax.optimization_barrier(arrays)


def chunks(rows, body):
    size = max(n for n in (128, 64, 32, 16) if rows % n == 0)

    def step(i, _):
        body(pl.multiple_of(i * size, size), size)
        return _

    lax.fori_loop(0, rows // size, step, 0, unroll=2 if rows // size > 1 else 1)


def first_sum_kernel(has_small, mine, *refs):
    wide, outs = refs[:2], refs[4 if has_small else 2 :]
    rows = wide[0].shape[0] // len(outs)
    for delta, out in enumerate(outs):
        to = mine[0] ^ delta

        def add(at, size):
            part = pl.ds(pl.multiple_of(to * rows + at, 16), size)
            out[pl.ds(at, size), :] = (wide[0][part, :].astype(f32) + wide[1][part, :].astype(f32)).astype(bf16)

        chunks(rows, add)
        end = rows
        if has_small:
            small = refs[2:4]
            size = small[0].shape[0] // len(outs)
            part = pl.ds(pl.multiple_of(to * size, 16), size)
            out[end : end + size, :] = (small[0][part, :].astype(f32) + small[1][part, :].astype(f32)).astype(bf16)
            end += size
        if end < out.shape[0]:
            out[end:, :] = jnp.zeros((out.shape[0] - end, LANES), bf16)


def sum_kernel(*refs):
    ins, out = refs[:-1], refs[-1]

    def add(at, size):
        part = pl.ds(at, size)
        out[part, :] = sum(r[part, :].astype(f32) for r in ins).astype(bf16)

    chunks(out.shape[0], add)


def join_kernel(mine, *refs):
    out = refs[-1]
    rows = refs[0].shape[0]
    for delta, ref in enumerate(refs[:-1]):
        out[pl.ds(pl.multiple_of((mine[0] ^ delta) * rows, 16), rows), :] = ref[...]


SUM_FLOPS = 1 << 20


def add_halves(mine, keep, other, *small):
    rows = (keep.shape[0] + (small[0].shape[0] if small else 0)) // 4
    return call(
        functools.partial(first_sum_kernel, bool(small)),
        [((rows, LANES), bf16)] * 4,
        [],
        (mine, keep, other, *small),
        SUM_FLOPS,
        1,
    )


def add(*arrays):
    (x,) = call(sum_kernel, [(arrays[0].shape, bf16)], [], arrays, SUM_FLOPS)
    return x


def join(mine, *parts):
    (x,) = call(join_kernel, [((4 * parts[0].shape[0], LANES), bf16)], [], (mine, *parts), SUM_FLOPS, 1)
    return x


def finish_kernel(
    factor, widths, core, own_a, other_a, own_b, other_b,
    win, wout, gk, scale, b_out, gain, shift, bias, b_in,
):
    channels = wout.shape[0]

    def store(firsts, seconds):
        base = 0
        for width, first, second in zip(widths, firsts, seconds):
            part = first.shape[0] // 4
            block = width * channels // LANES // 4

            def rows(ref, at):
                start = at // block * part + at % block
                return ref[start : start + LANES, :].astype(f32) * factor

            for j in range(channels // LANES):
                for i in range(0, width, LANES):
                    win[base + i : base + i + LANES, j * LANES : (j + 1) * LANES] = rows(first, j * width + i)
            for j in range(width // LANES):
                for i in range(0, channels, LANES):
                    wout[i : i + LANES, base + j * LANES : base + (j + 1) * LANES] = rows(
                        second, j * channels + i
                    )
            base += width
        slabs = channels // LANES
        for slab in range(slabs):
            at = slice(slab * LANES, (slab + 1) * LANES)
            start = slab * part + block
            values = firsts[1][start : start + SMALL, :].astype(f32) * factor
            for j in range(7):
                gk[j, :, at] = values[7 * j : 7 * j + 7]
            for j, ref in enumerate((scale, b_out, gain, shift, bias)):
                ref[at] = values[49 + j]
            for j in range(b_in.shape[0] // channels):
                lane = (j * slabs + slab) * LANES
                b_in[lane : lane + LANES] = values[54 + j]

    pl.when(core[0] == 0)(lambda: store((own_a, own_b), (other_a, other_b)))
    pl.when(core[0] != 0)(lambda: store((other_a, other_b), (own_a, own_b)))


def shards(
    pages,
    cotangent,
    conv_kernel,
    conv_bias,
    norm_gain,
    norm_bias,
    w_in,
    b_in,
    w_out,
    b_out,
    layer_scale,
):
    _, rows, cols, channels = pages.shape
    hid = w_in.shape[0]
    pixels = rows * cols
    tile = pages.reshape(rows, cols, channels)
    page = pages.reshape(pixels, channels)
    cot = cotangent.reshape(pixels, channels)
    kernel = conv_kernel.reshape(49, channels)
    row = lambda v: v.reshape(1, -1)
    gain, shift, scale = row(norm_gain), row(norm_bias), row(layer_scale)
    pad = ((channels // LANES, rows + 6, EDGE + cols + 8, LANES), f32)
    full = (pixels, channels)

    even_y = lax.axis_index("gy") % 2 == 0
    even_x = lax.axis_index("gx") % 2 == 0
    core = (lax.axis_index("gy") % 2).astype(jnp.int32).reshape(1)
    mine = (lax.axis_index("gy") // 2 % 2 + lax.axis_index("gx") % 2 * 2).astype(jnp.int32).reshape(1)
    even_y, even_x, core, mine, tile = hold((even_y, even_x, core, mine, tile))
    around = halo(tile, even_y, even_x)
    conv_flops = 2 * 49 * pixels * channels * 60
    normed, inv, ln_out = call(
        conv_norm_kernel,
        [(full, f32), ((pixels, LANES), f32), (full, bf16)],
        [pad, (full, f32)],
        (tile, *around, kernel, row(conv_bias), gain, shift),
        conv_flops,
    )
    grads = lambda width: [
        ((MLP_BLOCK, width), bf16),
        ((MLP_BLOCK, width), bf16),
        ((width, channels), f32),
        ((channels, width), f32),
        ((8, width), f32),
    ]
    packed = lambda width: [((width * channels // LANES, LANES), bf16)] * 2 + [((1, width), f32)]
    core_flip = [("gy", 0)]
    mlp_flops = 12 * pixels * channels * hid
    weights = (w_in, w_out, row(b_in), scale)
    first, second = hid * 2 // 3, hid // 3
    branch, d_norm, keep_a, send_a, gbin_a = call(
        functools.partial(mlp_first_kernel, 0, first),
        [(full, f32), (full, f32)] + packed(first),
        grads(first),
        (core, ln_out, cot, *weights),
        mlp_flops,
        1,
    )
    other_a = exchange(send_a, core_flip)
    result, d_depth, keep_b, send_b, gbin_b, sums = call(
        functools.partial(mlp_second_kernel, first, second),
        [(full, bf16), (full, bf16)] + packed(second) + [((8, channels), f32)],
        grads(second) + [((8, 8, channels), f32)],
        (core, ln_out, cot, *weights, row(b_out), gain, page, normed, inv, branch, d_norm),
        mlp_flops,
        1,
    )
    d_tile = d_depth.reshape(tile.shape)
    other_a, d_tile, keep_b, send_b = hold((other_a, d_tile, keep_b, send_b))
    parts_a = add_halves(mine, keep_a, other_a)
    got_a = spread(parts_a)
    other_b = exchange(send_b, core_flip)
    d_around = halo(d_tile, even_y, even_x)
    small_rows = ((4 * SMALL, LANES), bf16)
    keep_s, send_s = call(
        kernel_grad_kernel,
        [small_rows, small_rows],
        [pad, (full, f32), ((channels // LANES, 49, 8, LANES), f32)],
        (core, tile, *around, d_tile.reshape(full), sums, gbin_a, gbin_b),
        conv_flops,
        1,
        (parts_a[1],),
    )
    got_a, keep_s, send_s, other_b = hold((got_a, keep_s, send_s, other_b))
    other_s = exchange(send_s, core_flip)
    part_a = add(*got_a)
    parts_b = add_halves(mine, keep_b, other_b, keep_s, other_s)
    flips = [[bit] for bit in beyond()]
    got_a, got_b = exchange(part_a, flips[0]), spread(parts_b)
    (grad_pages,) = call(
        conv_grad_kernel,
        [(full, bf16)],
        [pad, (full, f32)],
        (d_tile, *d_around, kernel, cot),
        conv_flops,
        0,
        (part_a, parts_b[1]),
    )
    got_a, got_b, grad_pages = hold((got_a, got_b, grad_pages))
    part_a, part_b = add(part_a, got_a), add(*got_b)
    for ahead, behind in zip(flips[1:], flips):
        got_a, got_b = hold((exchange(part_a, ahead), exchange(part_b, behind)))
        part_a, part_b = add(part_a, got_a), add(part_b, got_b)
    got_a, got_b = hold((spread([part_a] * 4), exchange(part_b, flips[-1])))
    half_a, part_b = join(mine, *got_a), add(part_b, got_b)
    got_a, got_b = hold(([half_a, exchange(half_a, core_flip)], spread([part_b] * 4)))
    half_b = join(mine, *got_b)
    got_b = [half_b, exchange(half_b, core_flip)]
    factor = float(pixels * lax.axis_size("gy") * lax.axis_size("gx") * lax.axis_size("rep")) ** (-0.5)
    line = ((channels,), f32)
    win, wout, gk, g_scale, g_bout, g_gain, g_shift, g_bias, g_bin = call(
        functools.partial(finish_kernel, factor, (first, second)),
        [((hid, channels), f32), ((channels, hid), f32), ((7, 7, channels), f32)] + [line] * 5 + [((hid,), f32)],
        [],
        (core, *got_a, *got_b),
        SUM_FLOPS,
        1,
    )
    return (
        result.reshape(pages.shape),
        grad_pages.reshape(pages.shape),
        gk,
        g_bias,
        g_gain,
        g_shift,
        win,
        g_bin,
        wout,
        g_bout,
        g_scale,
    )


def solution(mesh):
    split = P("rep", "gy", "gx", None)
    return jax.shard_map(
        shards,
        mesh=mesh,
        in_specs=(split, split) + (P(),) * 9,
        out_specs=(split, split) + (P(),) * 9,
        check_vma=False,
    )
```

```python
import functools
import math

import jax
import jax.numpy as jnp
from jax import lax
from jax.experimental import pallas as pl
from jax.experimental.pallas import tpu as pltpu
from jax.sharding import PartitionSpec as P

norm_epsilon = 1e-06
inv_root_two = 0.7071067811865476
inv_root_tau = 0.3989422804014327
log2_e = 1.4426950408889634

LANES = 128
EDGE = 8
BAND = 32
AXES = ("gy", "gx", "rep")
f32 = jnp.float32
bf16 = jnp.bfloat16


def dot(a, b, dims):
    return lax.dot_general(a, b, (dims, ((), ())), preferred_element_type=f32)


NN = ((1,), (0,))
NT = ((1,), (1,))
TN = ((0,), (0,))


def pair_rounds(count):
    first = [(i, i + 1) for i in range(0, count - 1, 2)]
    second = [(i, i + 1) for i in range(1, count - 1, 2)]
    return [pairs + [(b, a) for a, b in pairs] for pairs in (first, second)]


def halo(tile, even_y, even_x):
    rows, cols, _ = tile.shape

    def swap_edges(low, high, axis, even):
        got = []
        for pairs, is_high in zip(pair_rounds(lax.axis_size(axis)), (even, ~even)):
            if pairs:
                got.append(lax.ppermute(jnp.where(is_high, high, low), axis, pairs))
            else:
                got.append(jnp.zeros_like(low))
        return jnp.where(even, got[1], got[0]), jnp.where(even, got[0], got[1])

    top, bottom = swap_edges(tile[:3], tile[rows - 3 :], "gy", even_y)
    column = [
        jnp.concatenate([part[:, at : at + 3] for part in (top, tile, bottom)], axis=0) for at in (0, cols - 3)
    ]
    left, right = swap_edges(*column, "gx", even_x)
    return top, bottom, left, right


def fill(pad, tile, top, bottom, left, right):
    rows, cols, channels = tile.shape
    for slab in range(channels // LANES):
        at = slice(slab * LANES, (slab + 1) * LANES)
        pad[slab, 0:3, EDGE : EDGE + cols, :] = top[:, :, at].astype(f32)
        pad[slab, 3 + rows :, EDGE : EDGE + cols, :] = bottom[:, :, at].astype(f32)
        pad[slab, :, EDGE - 3 : EDGE, :] = left[:, :, at].astype(f32)
        pad[slab, :, EDGE + cols : EDGE + cols + 3, :] = right[:, :, at].astype(f32)

        def body(row, _):
            pad[slab, row + 3, EDGE : EDGE + cols, :] = tile[row, :, at].astype(f32)
            return _

        lax.fori_loop(0, rows, body, 0, unroll=4)


def steps(rows, cols, channels, body):
    slabs, tiles, bands = channels // LANES, cols // 8, rows // BAND

    def step(i, _):
        slab = i // (tiles * bands)
        rest = i % (tiles * bands)
        body(slab, pl.multiple_of(rest // bands * 8, 8), rest % bands * BAND)
        return _

    lax.fori_loop(0, slabs * tiles * bands, step, 0)


def lanes(slab):
    return pl.ds(pl.multiple_of(slab * LANES, LANES), LANES)


def taps(pad, kernel, slab, col, row, flip):
    acc = [None] * BAND
    for b in range(7):
        scale = []
        for a in range(7):
            i, j = (6 - a, 6 - b) if flip else (a, b)
            scale.append(jnp.broadcast_to(kernel[i, j : j + 1, lanes(slab)], (8, LANES)))
        for r in range(BAND + 6):
            x = pad[slab, row + r, pl.ds(col + EDGE - 3 + b, 8), :]
            for a in range(7):
                i = r - a
                if 0 <= i < BAND:
                    acc[i] = x * scale[a] if acc[i] is None else acc[i] + x * scale[a]
    return acc


def line(ref, at=slice(None)):
    return ref[at].reshape(1, -1)


def conv_norm_kernel(
    tile, top, bottom, left, right, kernel, bias, gain, shift, normed_ref, inv_ref, ln_ref, pad, depth
):
    rows, cols, channels = tile.shape
    fill(pad, tile, top, bottom, left, right)

    def piece(slab, col, row):
        acc = taps(pad, kernel, slab, col, row, False)
        add = jnp.broadcast_to(line(bias, lanes(slab)), (8, LANES))
        for i in range(BAND):
            at = pl.ds(pl.multiple_of((row + i) * cols + col, 8), 8)
            depth[at, lanes(slab)] = acc[i] + add

    steps(rows, cols, channels, piece)
    block = 128

    def norm(i, _):
        at = pl.ds(pl.multiple_of(i * block, block), block)
        x = depth[at, :]
        centred = x - jnp.mean(x, axis=-1, keepdims=True)
        inv = lax.rsqrt(jnp.mean(centred * centred, axis=-1, keepdims=True) + norm_epsilon)
        normed = centred * inv
        normed_ref[at, :] = normed
        inv_ref[at, :] = jnp.broadcast_to(inv, (block, LANES))
        ln_ref[at, :] = (normed * line(gain) + line(shift)).astype(bf16)
        return _

    lax.fori_loop(0, rows * cols // block, norm, 0)


def gelu_pair(u):
    bell = jnp.exp2(u * u * (-0.5 * log2_e))
    t = 1.0 / (1.0 + jnp.abs(u) * (0.3275911 * inv_root_two))
    poly = 0.5 * 1.061405429
    for term in (-1.453152027, 1.421413741, -0.284496736, 0.254829592):
        poly = poly * t + 0.5 * term
    tail = poly * t * bell
    cdf = jnp.where(u < 0.0, tail, 1.0 - tail)
    return u * cdf, cdf + u * (bell * inv_root_tau)


def fold(x):
    return jnp.sum(x.reshape(-1, 8, x.shape[1]), axis=0)


def mlp_block(ln, d_branch, w_in, w_out, b_in, base, width, hid_ref, dpre_ref, gbin):
    sub = 256
    count = width // sub

    def products(s):
        at = pl.ds(base + s * sub, sub)
        return dot(ln, w_in[at, :], NT), dot(d_branch, w_out[:, at], NN)

    ahead = products(0)
    for s in range(count):
        pre, d_hidden = ahead
        if s + 1 < count:
            ahead = products(s + 1)
        act, slope = gelu_pair(pre + line(b_in, pl.ds(base + s * sub, sub)))
        d_pre = d_hidden * slope
        gbin[:, s * sub : (s + 1) * sub] += fold(d_pre)
        hid_ref[:, s * sub : (s + 1) * sub] = act.astype(bf16)
        dpre_ref[:, s * sub : (s + 1) * sub] = d_pre.astype(bf16)
    at = pl.ds(base, width)
    hidden, d_pre = hid_ref[...], dpre_ref[...]
    branch = dot(hidden, w_out[:, at], NT)
    d_norm = dot(d_pre, w_in[at, :], NN)
    return hidden, d_pre, branch, d_norm


def pack_grads(core, keep, send, gwin, gwout, gbin_ref, gbin):
    width, channels = gwin.shape

    def store(first, second):
        for j in range(channels // LANES):
            first[j * width : (j + 1) * width, :] = gwin[:, j * LANES : (j + 1) * LANES].astype(bf16)
        for j in range(width // LANES):
            second[j * channels : (j + 1) * channels, :] = gwout[
                :, j * LANES : (j + 1) * LANES
            ].astype(bf16)

    pl.when(core[0] == 0)(lambda: store(keep, send))
    pl.when(core[0] != 0)(lambda: store(send, keep))
    gbin_ref[...] = jnp.sum(gbin[...], axis=0, keepdims=True)


MLP_BLOCK = 256


def mlp_first_kernel(
    base, width, core, ln_ref, cot, w_in, w_out, b_in, scale, branch_ref, dnorm_ref, keep, send, gbin_ref,
    hid_ref, dpre_ref, gwin, gwout, gbin,
):
    gwin[...] = jnp.zeros_like(gwin)
    gwout[...] = jnp.zeros_like(gwout)
    gbin[...] = jnp.zeros_like(gbin)

    def step(i, _):
        at = pl.ds(pl.multiple_of(i * MLP_BLOCK, MLP_BLOCK), MLP_BLOCK)
        ln = ln_ref[at, :]
        d_branch = (line(scale) * cot[at, :].astype(f32)).astype(bf16)
        hidden, d_pre, branch, d_norm = mlp_block(
            ln, d_branch, w_in, w_out, b_in, base, width, hid_ref, dpre_ref, gbin
        )
        branch_ref[at, :] = branch
        dnorm_ref[at, :] = d_norm
        gwin[...] += dot(d_pre, ln, TN)
        gwout[...] += dot(d_branch, hidden, TN)
        return _

    lax.fori_loop(0, ln_ref.shape[0] // MLP_BLOCK, step, 0)
    pack_grads(core, keep, send, gwin, gwout, gbin_ref, gbin)


def mlp_second_kernel(
    base, width, core, ln_ref, cot, w_in, w_out, b_in, scale, b_out, gain, page, normed_ref, inv_ref,
    branch_ref, dnorm_ref,
    result, d_depth_ref, keep, send, gbin_ref, sums_ref,
    hid_ref, dpre_ref, gwin, gwout, gbin, sums,
):
    gwin[...] = jnp.zeros_like(gwin)
    gwout[...] = jnp.zeros_like(gwout)
    gbin[...] = jnp.zeros_like(gbin)
    sums[...] = jnp.zeros_like(sums)

    def step(i, _):
        at = pl.ds(pl.multiple_of(i * MLP_BLOCK, MLP_BLOCK), MLP_BLOCK)
        ln = ln_ref[at, :]
        cot32 = cot[at, :].astype(f32)
        d_branch32 = line(scale) * cot32
        d_branch = d_branch32.astype(bf16)
        hidden, d_pre, branch, d_norm = mlp_block(
            ln, d_branch, w_in, w_out, b_in, base, width, hid_ref, dpre_ref, gbin
        )
        gwin[...] += dot(d_pre, ln, TN)
        gwout[...] += dot(d_branch, hidden, TN)
        branch = branch + branch_ref[at, :] + line(b_out)
        result[at, :] = (page[at, :].astype(f32) + line(scale) * branch).astype(bf16)
        d_norm = d_norm + dnorm_ref[at, :]
        normed = normed_ref[at, :]
        inv = inv_ref[at, 0:1]
        weighted = d_norm * normed
        s = d_norm * line(gain)
        mean_s = jnp.mean(s, axis=-1, keepdims=True)
        mean_sn = jnp.mean(s * normed, axis=-1, keepdims=True)
        d_depth = (inv * (s - mean_s - normed * mean_sn)).astype(bf16)
        d_depth_ref[at, :] = d_depth
        sums[0] += fold(cot32 * branch)
        sums[1] += fold(d_branch32)
        sums[2] += fold(weighted)
        sums[3] += fold(d_norm)
        sums[4] += fold(d_depth.astype(f32))
        return _

    lax.fori_loop(0, ln_ref.shape[0] // MLP_BLOCK, step, 0)
    pack_grads(core, keep, send, gwin, gwout, gbin_ref, gbin)
    for j in range(5):
        sums_ref[j : j + 1, :] = jnp.sum(sums[j], axis=0, keepdims=True)


SMALL = 64


def kernel_grad_kernel(
    core, tile, top, bottom, left, right, d_depth, sums, gbin_a, gbin_b, keep, send, pad, d32, acc_ref
):
    rows, cols, channels = tile.shape
    fill(pad, tile, top, bottom, left, right)
    d32[...] = d_depth[...].astype(f32)
    acc_ref[...] = jnp.zeros_like(acc_ref)

    def piece(slab, col, row):
        grads = []
        for i in range(BAND):
            at = pl.ds(pl.multiple_of((row + i) * cols + col, 8), 8)
            grads.append(d32[at, lanes(slab)])
        for b in range(7):
            acc = [None] * 7
            for r in range(BAND + 6):
                x = pad[slab, row + r, pl.ds(col + EDGE - 3 + b, 8), :]
                for a in range(7):
                    i = r - a
                    if 0 <= i < BAND:
                        acc[a] = x * grads[i] if acc[a] is None else acc[a] + x * grads[i]
            for a in range(7):
                acc_ref[slab, a * 7 + b] += acc[a]

    steps(rows, cols, channels, piece)

    def store(first, second):
        second[...] = jnp.zeros_like(second)
        slabs = channels // LANES
        for slab in range(slabs):
            at = slice(slab * LANES, (slab + 1) * LANES)
            part = [jnp.sum(acc_ref[slab], axis=1), sums[:5, at]]
            for j in range((gbin_a.shape[1] + gbin_b.shape[1]) // channels):
                lane = (j * slabs + slab) * LANES
                source = gbin_a if lane < gbin_a.shape[1] else gbin_b
                lane = lane if lane < gbin_a.shape[1] else lane - gbin_a.shape[1]
                part.append(source[:, lane : lane + LANES])
            part = jnp.concatenate(part)
            part = jnp.concatenate([part, jnp.zeros((SMALL - part.shape[0], LANES), f32)])
            first[slab * SMALL : (slab + 1) * SMALL, :] = part.astype(bf16)
        rest = first.shape[0] - slabs * SMALL
        first[slabs * SMALL :, :] = jnp.zeros((rest, LANES), bf16)

    pl.when(core[0] == 0)(lambda: store(keep, send))
    pl.when(core[0] != 0)(lambda: store(send, keep))


def conv_grad_kernel(tile, top, bottom, left, right, kernel, cot, out, pad, total):
    rows, cols, channels = tile.shape
    fill(pad, tile, top, bottom, left, right)

    def piece(slab, col, row):
        acc = taps(pad, kernel, slab, col, row, True)
        for i in range(BAND):
            at = pl.ds(pl.multiple_of((row + i) * cols + col, 8), 8)
            total[at, lanes(slab)] = acc[i]

    steps(rows, cols, channels, piece)
    block = 128

    def finish(i, _):
        at = pl.ds(pl.multiple_of(i * block, block), block)
        out[at, :] = (cot[at, :].astype(f32) + total[at, :]).astype(bf16)
        return _

    lax.fori_loop(0, rows * cols // block, finish, 0)


def call(body, outs, scratch, args, flops, scalars=0, after=(), size=24 << 20):
    held = len(args)

    def kernel(*refs):
        body(*refs[:held], *refs[held + len(after) :])

    vmem = pl.BlockSpec(memory_space=pltpu.VMEM)
    smem = pl.BlockSpec(memory_space=pltpu.SMEM)
    return pl.pallas_call(
        kernel,
        out_shape=[jax.ShapeDtypeStruct(shape, dtype) for shape, dtype in outs],
        in_specs=[smem] * scalars
        + [vmem] * (held - scalars)
        + [pl.BlockSpec(memory_space=pl.ANY)] * len(after),
        out_specs=[vmem] * len(outs),
        scratch_shapes=[pltpu.VMEM(shape, dtype) for shape, dtype in scratch],
        compiler_params=pltpu.CompilerParams(vmem_limit_bytes=size),
        cost_estimate=pl.CostEstimate(flops=flops, bytes_accessed=flops >> 10, transcendentals=0),
    )(*args, *after)


def bits(axis):
    return [(axis, j) for j in range(max(lax.axis_size(axis).bit_length() - 1, 0))]


def plane():
    return [("gy", 1), ("gx", 0)]


def beyond():
    return bits("gy")[2:] + bits("gx")[1:] + bits("rep")


def exchange(x, flips):
    sizes = [lax.axis_size(axis) for axis in AXES]
    perm = []
    for i in range(math.prod(sizes)):
        at = {"gy": i // (sizes[1] * sizes[2]), "gx": i // sizes[2] % sizes[1], "rep": i % sizes[2]}
        for axis, bit in flips:
            at[axis] ^= 1 << bit
        perm.append((i, (at["gy"] * sizes[1] + at["gx"]) * sizes[2] + at["rep"]))
    return lax.ppermute(x, AXES, perm)


def spread(parts):
    flips = [[g for j, g in enumerate(plane()) if delta >> j & 1] for delta in range(1, 4)]
    return [parts[0]] + [exchange(x, flip) for x, flip in zip(parts[1:], flips)]


def hold(arrays):
    return lax.optimization_barrier(arrays)


def chunks(rows, body):
    size = max(n for n in (128, 64, 32, 16) if rows % n == 0)

    def step(i, _):
        body(pl.multiple_of(i * size, size), size)
        return _

    lax.fori_loop(0, rows // size, step, 0, unroll=2 if rows // size > 1 else 1)


def first_sum_kernel(has_small, mine, *refs):
    wide, outs = refs[:2], refs[4 if has_small else 2 :]
    rows = wide[0].shape[0] // len(outs)
    for delta, out in enumerate(outs):
        to = mine[0] ^ delta

        def add(at, size):
            part = pl.ds(pl.multiple_of(to * rows + at, 16), size)
            out[pl.ds(at, size), :] = (wide[0][part, :].astype(f32) + wide[1][part, :].astype(f32)).astype(bf16)

        chunks(rows, add)
        end = rows
        if has_small:
            small = refs[2:4]
            size = small[0].shape[0] // len(outs)
            part = pl.ds(pl.multiple_of(to * size, 16), size)
            out[end : end + size, :] = (small[0][part, :].astype(f32) + small[1][part, :].astype(f32)).astype(bf16)
            end += size
        if end < out.shape[0]:
            out[end:, :] = jnp.zeros((out.shape[0] - end, LANES), bf16)


def sum_kernel(*refs):
    ins, out = refs[:-1], refs[-1]

    def add(at, size):
        part = pl.ds(at, size)
        out[part, :] = sum(r[part, :].astype(f32) for r in ins).astype(bf16)

    chunks(out.shape[0], add)


def join_kernel(mine, *refs):
    out = refs[-1]
    rows = refs[0].shape[0]
    for delta, ref in enumerate(refs[:-1]):
        out[pl.ds(pl.multiple_of((mine[0] ^ delta) * rows, 16), rows), :] = ref[...]


SUM_FLOPS = 1 << 20


def add_halves(mine, keep, other, *small):
    rows = (keep.shape[0] + (small[0].shape[0] if small else 0)) // 4
    return call(
        functools.partial(first_sum_kernel, bool(small)),
        [((rows, LANES), bf16)] * 4,
        [],
        (mine, keep, other, *small),
        SUM_FLOPS,
        1,
    )


def add(*arrays):
    (x,) = call(sum_kernel, [(arrays[0].shape, bf16)], [], arrays, SUM_FLOPS)
    return x


def join(mine, *parts):
    (x,) = call(join_kernel, [((4 * parts[0].shape[0], LANES), bf16)], [], (mine, *parts), SUM_FLOPS, 1)
    return x


def finish_kernel(
    factor, widths, core, own_a, other_a, own_b, other_b,
    win, wout, gk, scale, b_out, gain, shift, bias, b_in,
):
    channels, unit = wout.shape
    slabs = channels // LANES

    def rows(ref, width, at):
        part, block = ref.shape[0] // 4, width * slabs // 4
        start = at // block * part + at % block
        return ref[start : start + LANES, :].astype(f32) * factor

    def store(first, second, width, offset):
        for j in range(slabs):
            for i in range(0, unit, LANES):
                win[i : i + LANES, j * LANES : (j + 1) * LANES] = rows(first, width, j * width + offset + i)
        for j in range(unit // LANES):
            for i in range(0, channels, LANES):
                wout[i : i + LANES, j * LANES : (j + 1) * LANES] = rows(
                    second, width, (offset // LANES + j) * channels + i
                )

    def store_small(first):
        for slab in range(slabs):
            at = slice(slab * LANES, (slab + 1) * LANES)
            start = slab * (first.shape[0] // 4) + widths[1] * slabs // 4
            values = first[start : start + SMALL, :].astype(f32) * factor
            for j in range(7):
                gk[j, :, at] = values[7 * j : 7 * j + 7]
            for j, ref in enumerate((scale, b_out, gain, shift, bias)):
                ref[at] = values[49 + j]
            for j in range(b_in.shape[0] // channels):
                lane = (j * slabs + slab) * LANES
                b_in[lane : lane + LANES] = values[54 + j]

    is_first = core[0] == 0
    step = pl.program_id(0)
    for i in range(sum(widths) // unit):
        offset, halves = i * unit, (own_a, other_a)
        width = widths[0]
        if offset >= widths[0]:
            offset, halves, width = offset - widths[0], (own_b, other_b), widths[1]
        here = step == i
        pl.when(here & is_first)(functools.partial(store, *halves, width, offset))
        pl.when(here & ~is_first)(functools.partial(store, *halves[::-1], width, offset))
    pl.when((step == 0) & is_first)(lambda: store_small(own_b))
    pl.when((step == 0) & ~is_first)(lambda: store_small(other_b))


def finish(factor, widths, channels, core, *halves):
    hid, unit = sum(widths), widths[1]
    vmem = pl.BlockSpec(memory_space=pltpu.VMEM)
    outs = [(hid, channels), (channels, hid), (7, 7, channels)] + [(channels,)] * 5 + [(hid,)]
    return pl.pallas_call(
        functools.partial(finish_kernel, factor, widths),
        grid=(hid // unit,),
        out_shape=[jax.ShapeDtypeStruct(shape, f32) for shape in outs],
        in_specs=[pl.BlockSpec(memory_space=pltpu.SMEM)] + [vmem] * len(halves),
        out_specs=[
            pl.BlockSpec((unit, channels), lambda i: (i, 0)),
            pl.BlockSpec((channels, unit), lambda i: (0, i)),
        ]
        + [vmem] * 7,
        compiler_params=pltpu.CompilerParams(vmem_limit_bytes=24 << 20),
    )(core, *halves)


def shards(
    pages,
    cotangent,
    conv_kernel,
    conv_bias,
    norm_gain,
    norm_bias,
    w_in,
    b_in,
    w_out,
    b_out,
    layer_scale,
):
    _, rows, cols, channels = pages.shape
    hid = w_in.shape[0]
    pixels = rows * cols
    tile = pages.reshape(rows, cols, channels)
    page = pages.reshape(pixels, channels)
    cot = cotangent.reshape(pixels, channels)
    pad = ((channels // LANES, rows + 6, EDGE + cols + 8, LANES), f32)
    full = (pixels, channels)

    even_y = lax.axis_index("gy") % 2 == 0
    even_x = lax.axis_index("gx") % 2 == 0
    core = (lax.axis_index("gy") % 2).astype(jnp.int32).reshape(1)
    mine = (lax.axis_index("gy") // 2 % 2 + lax.axis_index("gx") % 2 * 2).astype(jnp.int32).reshape(1)
    even_y, even_x, core, mine, tile = hold((even_y, even_x, core, mine, tile))
    around = halo(tile, even_y, even_x)
    conv_flops = 2 * 49 * pixels * channels * 60
    normed, inv, ln_out = call(
        conv_norm_kernel,
        [(full, f32), ((pixels, LANES), f32), (full, bf16)],
        [pad, (full, f32)],
        (tile, *around, conv_kernel, conv_bias, norm_gain, norm_bias),
        conv_flops,
    )
    grads = lambda width: [
        ((MLP_BLOCK, width), bf16),
        ((MLP_BLOCK, width), bf16),
        ((width, channels), f32),
        ((channels, width), f32),
        ((8, width), f32),
    ]
    packed = lambda width: [((width * channels // LANES, LANES), bf16)] * 2 + [((1, width), f32)]
    core_flip = [("gy", 0)]
    mlp_flops = 12 * pixels * channels * hid
    weights = (w_in, w_out, b_in, layer_scale)
    first, second = hid * 2 // 3, hid // 3
    branch, d_norm, keep_a, send_a, gbin_a = call(
        functools.partial(mlp_first_kernel, 0, first),
        [(full, f32), (full, f32)] + packed(first),
        grads(first),
        (core, ln_out, cot, *weights),
        mlp_flops,
        1,
    )
    other_a = exchange(send_a, core_flip)
    result, d_depth, keep_b, send_b, gbin_b, sums = call(
        functools.partial(mlp_second_kernel, first, second),
        [(full, bf16), (full, bf16)] + packed(second) + [((8, channels), f32)],
        grads(second) + [((8, 8, channels), f32)],
        (core, ln_out, cot, *weights, b_out, norm_gain, page, normed, inv, branch, d_norm),
        mlp_flops,
        1,
    )
    d_tile = d_depth.reshape(tile.shape)
    other_a, d_tile, keep_b, send_b = hold((other_a, d_tile, keep_b, send_b))
    parts_a = add_halves(mine, keep_a, other_a)
    got_a = spread(parts_a)
    other_b = exchange(send_b, core_flip)
    d_around = halo(d_tile, even_y, even_x)
    small_rows = ((4 * SMALL, LANES), bf16)
    keep_s, send_s = call(
        kernel_grad_kernel,
        [small_rows, small_rows],
        [pad, (full, f32), ((channels // LANES, 49, 8, LANES), f32)],
        (core, tile, *around, d_tile.reshape(full), sums, gbin_a, gbin_b),
        conv_flops,
        1,
        (parts_a[1],),
    )
    got_a, keep_s, send_s, other_b = hold((got_a, keep_s, send_s, other_b))
    other_s = exchange(send_s, core_flip)
    part_a = add(*got_a)
    parts_b = add_halves(mine, keep_b, other_b, keep_s, other_s)
    flips = [[bit] for bit in beyond()]
    got_a, got_b = exchange(part_a, flips[0]), spread(parts_b)
    (grad_pages,) = call(
        conv_grad_kernel,
        [(full, bf16)],
        [pad, (full, f32)],
        (d_tile, *d_around, conv_kernel, cot),
        conv_flops,
        0,
        (part_a, parts_b[1]),
    )
    got_a, got_b, grad_pages = hold((got_a, got_b, grad_pages))
    part_a, part_b = add(part_a, got_a), add(*got_b)
    for ahead, behind in zip(flips[1:], flips):
        got_a, got_b = hold((exchange(part_a, ahead), exchange(part_b, behind)))
        part_a, part_b = add(part_a, got_a), add(part_b, got_b)
    got_a, got_b = hold((spread([part_a] * 4), exchange(part_b, flips[-1])))
    half_a, part_b = join(mine, *got_a), add(part_b, got_b)
    got_a, got_b = hold(([half_a, exchange(half_a, core_flip)], spread([part_b] * 4)))
    half_b = join(mine, *got_b)
    got_b = [half_b, exchange(half_b, core_flip)]
    factor = float(pixels * lax.axis_size("gy") * lax.axis_size("gx") * lax.axis_size("rep")) ** (-0.5)
    win, wout, gk, g_scale, g_bout, g_gain, g_shift, g_bias, g_bin = finish(
        factor, (first, second), channels, core, *got_a, *got_b
    )
    return (
        result.reshape(pages.shape),
        grad_pages.reshape(pages.shape),
        gk,
        g_bias,
        g_gain,
        g_shift,
        win,
        g_bin,
        wout,
        g_bout,
        g_scale,
    )


def solution(mesh):
    split = P("rep", "gy", "gx", None)
    return jax.shard_map(
        shards,
        mesh=mesh,
        in_specs=(split, split) + (P(),) * 9,
        out_specs=(split, split) + (P(),) * 9,
        check_vma=False,
    )
```

```python
import functools
import math

import jax
import jax.numpy as jnp
from jax import lax
from jax.experimental import pallas as pl
from jax.experimental.pallas import tpu as pltpu
from jax.sharding import PartitionSpec as P

norm_epsilon = 1e-06
inv_root_two = 0.7071067811865476
inv_root_tau = 0.3989422804014327

LANES = 128
EDGE = 8
BAND = 32
AXES = ("gy", "gx", "rep")
f32 = jnp.float32
bf16 = jnp.bfloat16


def dot(a, b, dims):
    return lax.dot_general(a, b, (dims, ((), ())), preferred_element_type=f32)


NN = ((1,), (0,))
NT = ((1,), (1,))
TN = ((0,), (0,))


def pair_rounds(count):
    first = [(i, i + 1) for i in range(0, count - 1, 2)]
    second = [(i, i + 1) for i in range(1, count - 1, 2)]
    return [pairs + [(b, a) for a, b in pairs] for pairs in (first, second)]


def halo(tile, even_y, even_x):
    rows, cols, _ = tile.shape

    def swap_edges(low, high, axis, even):
        got = []
        for pairs, is_high in zip(pair_rounds(lax.axis_size(axis)), (even, ~even)):
            if pairs:
                got.append(lax.ppermute(jnp.where(is_high, high, low), axis, pairs))
            else:
                got.append(jnp.zeros_like(low))
        return jnp.where(even, got[1], got[0]), jnp.where(even, got[0], got[1])

    top, bottom = swap_edges(tile[:3], tile[rows - 3 :], "gy", even_y)
    column = [
        jnp.concatenate([part[:, at : at + 3] for part in (top, tile, bottom)], axis=0) for at in (0, cols - 3)
    ]
    left, right = swap_edges(*column, "gx", even_x)
    return top, bottom, left, right


def fill(pad, tile, top, bottom, left, right):
    rows, cols, channels = tile.shape
    for slab in range(channels // LANES):
        at = slice(slab * LANES, (slab + 1) * LANES)
        pad[slab, 0:3, EDGE : EDGE + cols, :] = top[:, :, at].astype(f32)
        pad[slab, 3 + rows :, EDGE : EDGE + cols, :] = bottom[:, :, at].astype(f32)
        pad[slab, :, EDGE - 3 : EDGE, :] = left[:, :, at].astype(f32)
        pad[slab, :, EDGE + cols : EDGE + cols + 3, :] = right[:, :, at].astype(f32)

        def body(row, _):
            pad[slab, row + 3, EDGE : EDGE + cols, :] = tile[row, :, at].astype(f32)
            return _

        lax.fori_loop(0, rows, body, 0, unroll=4)


def steps(rows, cols, channels, body):
    slabs, tiles, bands = channels // LANES, cols // 8, rows // BAND

    def step(i, _):
        slab = i // (tiles * bands)
        rest = i % (tiles * bands)
        body(slab, pl.multiple_of(rest // bands * 8, 8), rest % bands * BAND)
        return _

    lax.fori_loop(0, slabs * tiles * bands, step, 0)


def lanes(slab):
    return pl.ds(pl.multiple_of(slab * LANES, LANES), LANES)


def taps(pad, kernel, slab, col, row, flip):
    acc = [None] * BAND
    for b in range(7):
        scale = []
        for a in range(7):
            i, j = (6 - a, 6 - b) if flip else (a, b)
            scale.append(jnp.broadcast_to(kernel[i, j : j + 1, lanes(slab)], (8, LANES)))
        for r in range(BAND + 6):
            x = pad[slab, row + r, pl.ds(col + EDGE - 3 + b, 8), :]
            for a in range(7):
                i = r - a
                if 0 <= i < BAND:
                    acc[i] = x * scale[a] if acc[i] is None else acc[i] + x * scale[a]
    return acc


def line(ref, at=slice(None)):
    return ref[at].reshape(1, -1)


def conv_norm_kernel(
    tile, top, bottom, left, right, kernel, bias, gain, shift, normed_ref, inv_ref, ln_ref, pad, depth
):
    rows, cols, channels = tile.shape
    fill(pad, tile, top, bottom, left, right)

    def piece(slab, col, row):
        acc = taps(pad, kernel, slab, col, row, False)
        add = jnp.broadcast_to(line(bias, lanes(slab)), (8, LANES))
        for i in range(BAND):
            at = pl.ds(pl.multiple_of((row + i) * cols + col, 8), 8)
            depth[at, lanes(slab)] = acc[i] + add

    steps(rows, cols, channels, piece)
    block = 128

    def norm(i, _):
        at = pl.ds(pl.multiple_of(i * block, block), block)
        x = depth[at, :]
        centred = x - jnp.mean(x, axis=-1, keepdims=True)
        inv = lax.rsqrt(jnp.mean(centred * centred, axis=-1, keepdims=True) + norm_epsilon)
        normed = centred * inv
        normed_ref[at, :] = normed
        inv_ref[at, :] = jnp.broadcast_to(inv, (block, LANES))
        ln_ref[at, :] = (normed * line(gain) + line(shift)).astype(bf16)
        return _

    lax.fori_loop(0, rows * cols // block, norm, 0)


def gelu_pair(u):
    cdf = 0.5 * (1.0 + lax.erf(u * inv_root_two))
    pdf = jnp.exp(-0.5 * u * u) * inv_root_tau
    return u * cdf, cdf + u * pdf


def fold(x):
    return jnp.sum(x.reshape(-1, 8, x.shape[1]), axis=0)


def mlp(core, ln_ref, d_branch, w_in, w_out, b_in, base, width, hid_ref, dpre_ref, keep, send, gbin_ref):
    sub = 256
    count = width // sub
    channels = ln_ref.shape[1]
    ln = ln_ref[...]

    def products(s):
        at = pl.ds(base + s * sub, sub)
        return dot(ln, w_in[at, :], NT), dot(d_branch[...], w_out[:, at], NN)

    ahead = products(0)
    for s in range(count):
        pre, d_hidden = ahead
        if s + 1 < count:
            ahead = products(s + 1)
        act, slope = gelu_pair(pre + line(b_in, pl.ds(base + s * sub, sub)))
        d_pre = d_hidden * slope
        at = slice(s * sub, (s + 1) * sub)
        gbin_ref[:, at] = jnp.sum(d_pre, axis=0, keepdims=True)
        hid_ref[:, at] = act.astype(bf16)
        dpre_ref[:, at] = d_pre.astype(bf16)

    def store(first, second):
        for s in range(count):
            at = slice(s * sub, (s + 1) * sub)
            gwin = dot(dpre_ref[:, at], ln_ref[...], TN).astype(bf16)
            for j in range(channels // LANES):
                start = j * width + s * sub
                first[start : start + sub, :] = gwin[:, j * LANES : (j + 1) * LANES]
            gwout = dot(d_branch[...], hid_ref[:, at], TN).astype(bf16)
            for j in range(sub // LANES):
                start = (s * sub // LANES + j) * channels
                second[start : start + channels, :] = gwout[:, j * LANES : (j + 1) * LANES]

    pl.when(core[0] == 0)(lambda: store(keep, send))
    pl.when(core[0] != 0)(lambda: store(send, keep))


PIXELS = 256


def mlp_first_kernel(
    base, width, core, ln_ref, cot, w_in, w_out, b_in, scale, branch_ref, dnorm_ref, d_branch_ref,
    keep, send, gbin_ref, hid_ref, dpre_ref,
):
    d_branch_ref[...] = (line(scale) * cot[...].astype(f32)).astype(bf16)
    mlp(core, ln_ref, d_branch_ref, w_in, w_out, b_in, base, width, hid_ref, dpre_ref, keep, send, gbin_ref)
    at = pl.ds(base, width)

    def step(i, _):
        to = pl.ds(pl.multiple_of(i * PIXELS, PIXELS), PIXELS)
        branch_ref[to, :] = dot(hid_ref[to, :], w_out[:, at], NT)
        dnorm_ref[to, :] = dot(dpre_ref[to, :], w_in[at, :], NN)
        return _

    lax.fori_loop(0, ln_ref.shape[0] // PIXELS, step, 0)


def mlp_second_kernel(
    base, width, core, ln_ref, cot, w_in, w_out, b_in, scale, b_out, gain, page, normed_ref, inv_ref,
    branch_ref, dnorm_ref, d_branch_ref,
    result, d_depth_ref, keep, send, gbin_ref, sums_ref,
    hid_ref, dpre_ref, sums,
):
    sums[...] = jnp.zeros_like(sums)
    mlp(core, ln_ref, d_branch_ref, w_in, w_out, b_in, base, width, hid_ref, dpre_ref, keep, send, gbin_ref)
    units = pl.ds(base, width)

    def step(i, _):
        at = pl.ds(pl.multiple_of(i * PIXELS, PIXELS), PIXELS)
        cot32 = cot[at, :].astype(f32)
        branch = dot(hid_ref[at, :], w_out[:, units], NT) + branch_ref[at, :] + line(b_out)
        result[at, :] = (page[at, :].astype(f32) + line(scale) * branch).astype(bf16)
        d_norm = dot(dpre_ref[at, :], w_in[units, :], NN) + dnorm_ref[at, :]
        normed = normed_ref[at, :]
        inv = inv_ref[at, 0:1]
        weighted = d_norm * normed
        s = d_norm * line(gain)
        mean_s = jnp.mean(s, axis=-1, keepdims=True)
        mean_sn = jnp.mean(s * normed, axis=-1, keepdims=True)
        d_depth = (inv * (s - mean_s - normed * mean_sn)).astype(bf16)
        d_depth_ref[at, :] = d_depth
        sums[0] += fold(cot32 * branch)
        sums[1] += fold(line(scale) * cot32)
        sums[2] += fold(weighted)
        sums[3] += fold(d_norm)
        sums[4] += fold(d_depth.astype(f32))
        return _

    lax.fori_loop(0, ln_ref.shape[0] // PIXELS, step, 0)
    for j in range(5):
        sums_ref[j : j + 1, :] = jnp.sum(sums[j], axis=0, keepdims=True)


SMALL = 64


def kernel_grad_kernel(
    core, tile, top, bottom, left, right, d_depth, sums, gbin_a, gbin_b, keep, send, pad, d32, acc_ref
):
    rows, cols, channels = tile.shape
    fill(pad, tile, top, bottom, left, right)
    d32[...] = d_depth[...].astype(f32)
    acc_ref[...] = jnp.zeros_like(acc_ref)

    def piece(slab, col, row):
        grads = []
        for i in range(BAND):
            at = pl.ds(pl.multiple_of((row + i) * cols + col, 8), 8)
            grads.append(d32[at, lanes(slab)])
        for b in range(7):
            acc = [None] * 7
            for r in range(BAND + 6):
                x = pad[slab, row + r, pl.ds(col + EDGE - 3 + b, 8), :]
                for a in range(7):
                    i = r - a
                    if 0 <= i < BAND:
                        acc[a] = x * grads[i] if acc[a] is None else acc[a] + x * grads[i]
            for a in range(7):
                acc_ref[slab, a * 7 + b] += acc[a]

    steps(rows, cols, channels, piece)

    def store(first, second):
        slabs, half = channels // LANES, SMALL // 2
        for slab in range(slabs):
            at = slice(slab * LANES, (slab + 1) * LANES)
            part = [jnp.sum(acc_ref[slab], axis=1), sums[:5, at]]
            for j in range((gbin_a.shape[1] + gbin_b.shape[1]) // channels):
                lane = (j * slabs + slab) * LANES
                source = gbin_a if lane < gbin_a.shape[1] else gbin_b
                lane = lane if lane < gbin_a.shape[1] else lane - gbin_a.shape[1]
                part.append(source[:, lane : lane + LANES])
            part = jnp.concatenate(part)
            part = jnp.concatenate([part, jnp.zeros((SMALL - part.shape[0], LANES), f32)])
            first[slab * half : (slab + 1) * half, :] = part[:half].astype(bf16)
            second[slab * half : (slab + 1) * half, :] = part[half:].astype(bf16)
        for ref in (first, second):
            ref[slabs * half :, :] = jnp.zeros((ref.shape[0] - slabs * half, LANES), bf16)

    pl.when(core[0] == 0)(lambda: store(keep, send))
    pl.when(core[0] != 0)(lambda: store(send, keep))


def conv_grad_kernel(tile, top, bottom, left, right, kernel, cot, out, pad, total):
    rows, cols, channels = tile.shape
    fill(pad, tile, top, bottom, left, right)

    def piece(slab, col, row):
        acc = taps(pad, kernel, slab, col, row, True)
        for i in range(BAND):
            at = pl.ds(pl.multiple_of((row + i) * cols + col, 8), 8)
            total[at, lanes(slab)] = acc[i]

    steps(rows, cols, channels, piece)
    block = 128

    def finish(i, _):
        at = pl.ds(pl.multiple_of(i * block, block), block)
        out[at, :] = (cot[at, :].astype(f32) + total[at, :]).astype(bf16)
        return _

    lax.fori_loop(0, rows * cols // block, finish, 0)


def call(body, outs, scratch, args, flops, scalars=0, after=(), size=24 << 20):
    held = len(args)

    def kernel(*refs):
        body(*refs[:held], *refs[held + len(after) :])

    vmem = pl.BlockSpec(memory_space=pltpu.VMEM)
    smem = pl.BlockSpec(memory_space=pltpu.SMEM)
    return pl.pallas_call(
        kernel,
        out_shape=[jax.ShapeDtypeStruct(shape, dtype) for shape, dtype in outs],
        in_specs=[smem] * scalars
        + [vmem] * (held - scalars)
        + [pl.BlockSpec(memory_space=pl.ANY)] * len(after),
        out_specs=[vmem] * len(outs),
        scratch_shapes=[pltpu.VMEM(shape, dtype) for shape, dtype in scratch],
        compiler_params=pltpu.CompilerParams(vmem_limit_bytes=size),
        cost_estimate=pl.CostEstimate(flops=flops, bytes_accessed=flops >> 10, transcendentals=0),
    )(*args, *after)


def bits(axis):
    return [(axis, j) for j in range(max(lax.axis_size(axis).bit_length() - 1, 0))]


def plane():
    return [("gy", 1), ("gx", 0)]


def beyond():
    return bits("gy")[2:] + bits("gx")[1:] + bits("rep")


def exchange(x, flips):
    sizes = [lax.axis_size(axis) for axis in AXES]
    perm = []
    for i in range(math.prod(sizes)):
        at = {"gy": i // (sizes[1] * sizes[2]), "gx": i // sizes[2] % sizes[1], "rep": i % sizes[2]}
        for axis, bit in flips:
            at[axis] ^= 1 << bit
        perm.append((i, (at["gy"] * sizes[1] + at["gx"]) * sizes[2] + at["rep"]))
    return lax.ppermute(x, AXES, perm)


def spread(parts):
    flips = [[g for j, g in enumerate(plane()) if delta >> j & 1] for delta in range(1, 4)]
    return [parts[0]] + [exchange(x, flip) for x, flip in zip(parts[1:], flips)]


def hold(arrays):
    return lax.optimization_barrier(arrays)


def chunks(rows, body):
    size = max(n for n in (128, 64, 32, 16) if rows % n == 0)

    def step(i, _):
        body(pl.multiple_of(i * size, size), size)
        return _

    lax.fori_loop(0, rows // size, step, 0, unroll=2 if rows // size > 1 else 1)


def first_sum_kernel(has_small, mine, *refs):
    wide, outs = refs[:2], refs[4 if has_small else 2 :]
    rows = wide[0].shape[0] // len(outs)
    for delta, out in enumerate(outs):
        to = mine[0] ^ delta

        def add(at, size):
            part = pl.ds(pl.multiple_of(to * rows + at, 16), size)
            out[pl.ds(at, size), :] = (wide[0][part, :].astype(f32) + wide[1][part, :].astype(f32)).astype(bf16)

        chunks(rows, add)
        end = rows
        if has_small:
            small = refs[2:4]
            size = small[0].shape[0] // len(outs)
            part = pl.ds(pl.multiple_of(to * size, 16), size)
            out[end : end + size, :] = (small[0][part, :].astype(f32) + small[1][part, :].astype(f32)).astype(bf16)
            end += size
        if end < out.shape[0]:
            out[end:, :] = jnp.zeros((out.shape[0] - end, LANES), bf16)


def sum_kernel(*refs):
    ins, out = refs[:-1], refs[-1]

    def add(at, size):
        part = pl.ds(at, size)
        out[part, :] = sum(r[part, :].astype(f32) for r in ins).astype(bf16)

    chunks(out.shape[0], add)


def join_kernel(mine, *refs):
    out = refs[-1]
    rows = refs[0].shape[0]
    for delta, ref in enumerate(refs[:-1]):
        out[pl.ds(pl.multiple_of((mine[0] ^ delta) * rows, 16), rows), :] = ref[...]


SUM_FLOPS = 1 << 20


def add_halves(mine, keep, other, *small):
    rows = (keep.shape[0] + (small[0].shape[0] if small else 0)) // 4
    return call(
        functools.partial(first_sum_kernel, bool(small)),
        [((rows, LANES), bf16)] * 4,
        [],
        (mine, keep, other, *small),
        SUM_FLOPS,
        1,
    )


def add(*arrays):
    (x,) = call(sum_kernel, [(arrays[0].shape, bf16)], [], arrays, SUM_FLOPS)
    return x


def join(mine, *parts):
    (x,) = call(join_kernel, [((4 * parts[0].shape[0], LANES), bf16)], [], (mine, *parts), SUM_FLOPS, 1)
    return x


def finish_kernel(
    factor, widths, core, own_a, other_a, own_b, other_b,
    win, wout, gk, scale, b_out, gain, shift, bias, b_in,
):
    channels, unit = wout.shape
    slabs = channels // LANES

    def rows(ref, width, at):
        part, block = ref.shape[0] // 4, width * slabs // 4
        start = at // block * part + at % block
        return ref[start : start + LANES, :].astype(f32) * factor

    def store(first, second, width, offset):
        for j in range(slabs):
            for i in range(0, unit, LANES):
                win[i : i + LANES, j * LANES : (j + 1) * LANES] = rows(first, width, j * width + offset + i)
        for j in range(unit // LANES):
            for i in range(0, channels, LANES):
                wout[i : i + LANES, j * LANES : (j + 1) * LANES] = rows(
                    second, width, (offset // LANES + j) * channels + i
                )

    def store_small(*halves):
        for slab in range(slabs):
            at = slice(slab * LANES, (slab + 1) * LANES)
            start = slab * (halves[0].shape[0] // 4) + widths[1] * slabs // 4
            values = jnp.concatenate([ref[start : start + SMALL // 2, :].astype(f32) for ref in halves]) * factor
            for j in range(7):
                gk[j, :, at] = values[7 * j : 7 * j + 7]
            for j, ref in enumerate((scale, b_out, gain, shift, bias)):
                ref[at] = values[49 + j]
            for j in range(b_in.shape[0] // channels):
                lane = (j * slabs + slab) * LANES
                b_in[lane : lane + LANES] = values[54 + j]

    is_first = core[0] == 0
    step = pl.program_id(0)
    for i in range(sum(widths) // unit):
        offset, halves = i * unit, (own_a, other_a)
        width = widths[0]
        if offset >= widths[0]:
            offset, halves, width = offset - widths[0], (own_b, other_b), widths[1]
        here = step == i
        pl.when(here & is_first)(functools.partial(store, *halves, width, offset))
        pl.when(here & ~is_first)(functools.partial(store, *halves[::-1], width, offset))
    pl.when((step == 0) & is_first)(lambda: store_small(own_b, other_b))
    pl.when((step == 0) & ~is_first)(lambda: store_small(other_b, own_b))


def finish(factor, widths, channels, core, *halves):
    hid, unit = sum(widths), widths[1]
    vmem = pl.BlockSpec(memory_space=pltpu.VMEM)
    outs = [(hid, channels), (channels, hid), (7, 7, channels)] + [(channels,)] * 5 + [(hid,)]
    return pl.pallas_call(
        functools.partial(finish_kernel, factor, widths),
        grid=(hid // unit,),
        out_shape=[jax.ShapeDtypeStruct(shape, f32) for shape in outs],
        in_specs=[pl.BlockSpec(memory_space=pltpu.SMEM)] + [vmem] * len(halves),
        out_specs=[
            pl.BlockSpec((unit, channels), lambda i: (i, 0)),
            pl.BlockSpec((channels, unit), lambda i: (0, i)),
        ]
        + [vmem] * 7,
        compiler_params=pltpu.CompilerParams(vmem_limit_bytes=24 << 20),
    )(core, *halves)


def shards(
    pages,
    cotangent,
    conv_kernel,
    conv_bias,
    norm_gain,
    norm_bias,
    w_in,
    b_in,
    w_out,
    b_out,
    layer_scale,
):
    _, rows, cols, channels = pages.shape
    hid = w_in.shape[0]
    pixels = rows * cols
    tile = pages.reshape(rows, cols, channels)
    page = pages.reshape(pixels, channels)
    cot = cotangent.reshape(pixels, channels)
    pad = ((channels // LANES, rows + 6, EDGE + cols + 8, LANES), f32)
    full = (pixels, channels)

    even_y = lax.axis_index("gy") % 2 == 0
    even_x = lax.axis_index("gx") % 2 == 0
    core = (lax.axis_index("gy") % 2).astype(jnp.int32).reshape(1)
    mine = (lax.axis_index("gy") // 2 % 2 + lax.axis_index("gx") % 2 * 2).astype(jnp.int32).reshape(1)
    even_y, even_x, core, mine, tile = hold((even_y, even_x, core, mine, tile))
    around = halo(tile, even_y, even_x)
    conv_flops = 2 * 49 * pixels * channels * 60
    normed, inv, ln_out = call(
        conv_norm_kernel,
        [(full, f32), ((pixels, LANES), f32), (full, bf16)],
        [pad, (full, f32)],
        (tile, *around, conv_kernel, conv_bias, norm_gain, norm_bias),
        conv_flops,
    )
    acts = lambda width: [((pixels, width), bf16)] * 2
    packed = lambda width: [((width * channels // LANES, LANES), bf16)] * 2 + [((1, width), f32)]
    core_flip = [("gy", 0)]
    mlp_flops = 12 * pixels * channels * hid
    weights = (w_in, w_out, b_in, layer_scale)
    first, second = hid * 2 // 3, hid // 3
    branch, d_norm, d_branch, keep_a, send_a, gbin_a = call(
        functools.partial(mlp_first_kernel, 0, first),
        [(full, f32), (full, f32), (full, bf16)] + packed(first),
        acts(first),
        (core, ln_out, cot, *weights),
        mlp_flops,
        1,
    )
    other_a = exchange(send_a, core_flip)
    result, d_depth, keep_b, send_b, gbin_b, sums = call(
        functools.partial(mlp_second_kernel, first, second),
        [(full, bf16), (full, bf16)] + packed(second) + [((8, channels), f32)],
        acts(second) + [((8, 8, channels), f32)],
        (core, ln_out, cot, *weights, b_out, norm_gain, page, normed, inv, branch, d_norm, d_branch),
        mlp_flops,
        1,
    )
    d_tile = d_depth.reshape(tile.shape)
    other_a, d_tile, keep_b, send_b = hold((other_a, d_tile, keep_b, send_b))
    parts_a = add_halves(mine, keep_a, other_a)
    got_a = spread(parts_a)
    other_b = exchange(send_b, core_flip)
    d_around = halo(d_tile, even_y, even_x)
    small_rows = ((2 * SMALL, LANES), bf16)
    keep_s, send_s = call(
        kernel_grad_kernel,
        [small_rows, small_rows],
        [pad, (full, f32), ((channels // LANES, 49, 8, LANES), f32)],
        (core, tile, *around, d_tile.reshape(full), sums, gbin_a, gbin_b),
        conv_flops,
        1,
        (parts_a[1],),
    )
    got_a, keep_s, send_s, other_b = hold((got_a, keep_s, send_s, other_b))
    other_s = exchange(send_s, core_flip)
    part_a = add(*got_a)
    parts_b = add_halves(mine, keep_b, other_b, keep_s, other_s)
    flips = [[bit] for bit in beyond()]
    got_a, got_b = exchange(part_a, flips[0]), spread(parts_b)
    got_a, got_b = hold((got_a, got_b))
    part_a, part_b = add(part_a, got_a), add(*got_b)
    (grad_pages,) = call(
        conv_grad_kernel,
        [(full, bf16)],
        [pad, (full, f32)],
        (d_tile, *d_around, conv_kernel, cot),
        conv_flops,
        0,
        (part_a, part_b),
    )
    for ahead, behind in zip(flips[1:], flips):
        got_a, got_b, grad_pages = hold((exchange(part_a, ahead), exchange(part_b, behind), grad_pages))
        part_a, part_b = add(part_a, got_a), add(part_b, got_b)
    got_a, got_b = hold((spread([part_a] * 4), exchange(part_b, flips[-1])))
    half_a, part_b = join(mine, *got_a), add(part_b, got_b)
    got_a, got_b = hold(([half_a, exchange(half_a, core_flip)], spread([part_b] * 4)))
    half_b = join(mine, *got_b)
    got_b = [half_b, exchange(half_b, core_flip)]
    factor = float(pixels * lax.axis_size("gy") * lax.axis_size("gx") * lax.axis_size("rep")) ** (-0.5)
    win, wout, gk, g_scale, g_bout, g_gain, g_shift, g_bias, g_bin = finish(
        factor, (first, second), channels, core, *got_a, *got_b
    )
    return (
        result.reshape(pages.shape),
        grad_pages.reshape(pages.shape),
        gk,
        g_bias,
        g_gain,
        g_shift,
        win,
        g_bin,
        wout,
        g_bout,
        g_scale,
    )


def solution(mesh):
    split = P("rep", "gy", "gx", None)
    return jax.shard_map(
        shards,
        mesh=mesh,
        in_specs=(split, split) + (P(),) * 9,
        out_specs=(split, split) + (P(),) * 9,
        check_vma=False,
    )
```

```python
import functools
import math

import jax
import jax.numpy as jnp
from jax import lax
from jax.experimental import pallas as pl
from jax.experimental.pallas import tpu as pltpu
from jax.sharding import PartitionSpec as P

norm_epsilon = 1e-06
inv_root_two = 0.7071067811865476
inv_root_tau = 0.3989422804014327

LANES = 128
EDGE = 8
BAND = 32
AXES = ("gy", "gx", "rep")
f32 = jnp.float32
bf16 = jnp.bfloat16


def dot(a, b, dims):
    return lax.dot_general(a, b, (dims, ((), ())), preferred_element_type=f32)


NN = ((1,), (0,))
NT = ((1,), (1,))
TN = ((0,), (0,))


def pair_rounds(count):
    first = [(i, i + 1) for i in range(0, count - 1, 2)]
    second = [(i, i + 1) for i in range(1, count - 1, 2)]
    return [pairs + [(b, a) for a, b in pairs] for pairs in (first, second)]


def halo(tile, even_y, even_x):
    rows, cols, _ = tile.shape

    def swap_edges(low, high, axis, even):
        got = []
        for pairs, is_high in zip(pair_rounds(lax.axis_size(axis)), (even, ~even)):
            if pairs:
                got.append(lax.ppermute(jnp.where(is_high, high, low), axis, pairs))
            else:
                got.append(jnp.zeros_like(low))
        return jnp.where(even, got[1], got[0]), jnp.where(even, got[0], got[1])

    top, bottom = swap_edges(tile[:3], tile[rows - 3 :], "gy", even_y)
    column = [
        jnp.concatenate([part[:, at : at + 3] for part in (top, tile, bottom)], axis=0) for at in (0, cols - 3)
    ]
    left, right = swap_edges(*column, "gx", even_x)
    return top, bottom, left, right


def whole_halo(tile, even_y, even_x):
    rows, cols, _ = tile.shape
    rounds_y = list(enumerate(pair_rounds(lax.axis_size("gy"))))
    rounds_x = list(enumerate(pair_rounds(lax.axis_size("gx"))))
    high_y, high_x = (even_y, ~even_y), (even_x, ~even_x)
    received = {}
    for y, pairs in rounds_y:
        strip = jnp.where(high_y[y], tile[rows - 3 :], tile[:3])
        if pairs:
            received[y, None] = lax.ppermute(strip, "gy", pairs)
    for x, pairs in rounds_x:
        strip = jnp.where(high_x[x], tile[:, cols - 3 :], tile[:, :3])
        if pairs:
            received[None, x] = lax.ppermute(strip, "gx", pairs)
    count = lax.axis_size("gx")
    for y, pairs_y in rounds_y:
        for x, pairs_x in rounds_x:
            pairs = [(a * count + c, b * count + d) for a, b in pairs_y for c, d in pairs_x]
            if pairs:
                strip = jnp.where(high_y[y], tile[rows - 3 :], tile[:3])
                strip = jnp.where(high_x[x], strip[:, cols - 3 :], strip[:, :3])
                received[y, x] = lax.ppermute(strip, ("gy", "gx"), pairs)
    return received


def fill_tile(pad, tile, at, slab):
    rows, cols, _ = tile.shape

    def body(row, _):
        pad[slab, row + 3, EDGE : EDGE + cols, :] = tile[row, :, at].astype(f32)
        return _

    lax.fori_loop(0, rows, body, 0, unroll=4)


def fill_around(pad, even, tile, received):
    rows, cols, channels = tile.shape
    even_y, even_x = even[0] == 1, even[1] == 1
    tall = {False: slice(0, 3), None: slice(3, rows + 3), True: slice(rows + 3, rows + 6)}
    wide = {
        False: slice(EDGE - 3, EDGE),
        None: slice(EDGE, EDGE + cols),
        True: slice(EDGE + cols, EDGE + cols + 3),
    }
    for slab in range(channels // LANES):
        at = slice(slab * LANES, (slab + 1) * LANES)
        fill_tile(pad, tile, at, slab)

        def value(y, x, shape):
            if (y, x) in received:
                return received[y, x][:, :, at].astype(f32)
            return jnp.zeros(shape, f32)

        def pick(even, high, first, second):
            return jnp.where(even, first, second) if high else jnp.where(even, second, first)

        for high_y in (None, False, True):
            for high_x in (None, False, True):
                if high_y is None and high_x is None:
                    continue
                shape = (rows if high_y is None else 3, cols if high_x is None else 3, LANES)
                found = []
                for y in (None,) if high_y is None else (0, 1):
                    line_x = [value(y, x, shape) for x in ((None,) if high_x is None else (0, 1))]
                    found.append(line_x[0] if high_x is None else pick(even_x, high_x, *line_x))
                part = found[0] if high_y is None else pick(even_y, high_y, *found)
                pad[slab, tall[high_y], wide[high_x], :] = part


def fill(pad, tile, top, bottom, left, right):
    rows, cols, channels = tile.shape
    for slab in range(channels // LANES):
        at = slice(slab * LANES, (slab + 1) * LANES)
        pad[slab, 0:3, EDGE : EDGE + cols, :] = top[:, :, at].astype(f32)
        pad[slab, 3 + rows :, EDGE : EDGE + cols, :] = bottom[:, :, at].astype(f32)
        pad[slab, :, EDGE - 3 : EDGE, :] = left[:, :, at].astype(f32)
        pad[slab, :, EDGE + cols : EDGE + cols + 3, :] = right[:, :, at].astype(f32)

        def body(row, _):
            pad[slab, row + 3, EDGE : EDGE + cols, :] = tile[row, :, at].astype(f32)
            return _

        lax.fori_loop(0, rows, body, 0, unroll=4)


def steps(rows, cols, channels, body):
    slabs, tiles, bands = channels // LANES, cols // 8, rows // BAND

    def step(i, _):
        slab = i // (tiles * bands)
        rest = i % (tiles * bands)
        body(slab, pl.multiple_of(rest // bands * 8, 8), rest % bands * BAND)
        return _

    lax.fori_loop(0, slabs * tiles * bands, step, 0)


def lanes(slab):
    return pl.ds(pl.multiple_of(slab * LANES, LANES), LANES)


def taps(pad, kernel, slab, col, row, flip):
    acc = [None] * BAND
    for b in range(7):
        scale = []
        for a in range(7):
            i, j = (6 - a, 6 - b) if flip else (a, b)
            scale.append(jnp.broadcast_to(kernel[i, j : j + 1, lanes(slab)], (8, LANES)))
        for r in range(BAND + 6):
            x = pad[slab, row + r, pl.ds(col + EDGE - 3 + b, 8), :]
            for a in range(7):
                i = r - a
                if 0 <= i < BAND:
                    acc[i] = x * scale[a] if acc[i] is None else acc[i] + x * scale[a]
    return acc


def line(ref, at=slice(None)):
    return ref[at].reshape(1, -1)


def inner(cols, col):
    return (col > 0) & (col < cols - 8)


def conv_inner_kernel(tile, kernel, depth, pad):
    rows, cols, channels = tile.shape
    for slab in range(channels // LANES):
        fill_tile(pad, tile, slice(slab * LANES, (slab + 1) * LANES), slab)
    for edge in (pl.ds(0, 3), pl.ds(rows + 3, 3)):
        pad[:, edge, :, :] = jnp.zeros((channels // LANES, 3, pad.shape[2], LANES), f32)

    def piece(slab, col, row):
        @pl.when(inner(cols, col))
        def _():
            acc = taps(pad, kernel, slab, col, row, False)
            for i in range(BAND):
                at = pl.ds(pl.multiple_of((row + i) * cols + col, 8), 8)
                depth[at, lanes(slab)] = acc[i]

    steps(rows, cols, channels, piece)


def edge_taps(pad, kernel, slab, col, rows):
    acc = {}
    for b in range(7):
        for r in (0, 1, 2, rows + 3, rows + 4, rows + 5):
            x = pad[slab, r, pl.ds(col + EDGE - 3 + b, 8), :]
            for a in range(7):
                i = r - a
                if 0 <= i < rows:
                    term = x * jnp.broadcast_to(kernel[a, b : b + 1, lanes(slab)], (8, LANES))
                    acc[i] = acc[i] + term if i in acc else term
    return acc


def conv_norm_kernel(keys, even, tile, depth_in, kernel, bias, gain, shift, *refs):
    received = dict(zip(keys, refs))
    normed_ref, inv_ref, ln_ref, pad, depth = refs[len(keys) :]
    rows, cols, channels = tile.shape
    fill_around(pad, even, tile, received)

    def piece(slab, col, row):
        add = jnp.broadcast_to(line(bias, lanes(slab)), (8, LANES))

        @pl.when(~inner(cols, col))
        def _():
            acc = taps(pad, kernel, slab, col, row, False)
            for i in range(BAND):
                at = pl.ds(pl.multiple_of((row + i) * cols + col, 8), 8)
                depth[at, lanes(slab)] = acc[i] + add

        @pl.when(inner(cols, col) & (row == 0))
        def _():
            acc = edge_taps(pad, kernel, slab, col, rows)
            for i in range(rows):
                at = pl.ds(pl.multiple_of(i * cols + col, 8), 8)
                value = depth_in[at, lanes(slab)] + add
                depth[at, lanes(slab)] = value + acc[i] if i in acc else value

    steps(rows, cols, channels, piece)
    block = 128

    def norm(i, _):
        at = pl.ds(pl.multiple_of(i * block, block), block)
        x = depth[at, :]
        centred = x - jnp.mean(x, axis=-1, keepdims=True)
        inv = lax.rsqrt(jnp.mean(centred * centred, axis=-1, keepdims=True) + norm_epsilon)
        normed = centred * inv
        normed_ref[at, :] = normed
        inv_ref[at, :] = jnp.broadcast_to(inv, (block, LANES))
        ln_ref[at, :] = (normed * line(gain) + line(shift)).astype(bf16)
        return _

    lax.fori_loop(0, rows * cols // block, norm, 0)


def gelu_pair(u):
    cdf = 0.5 * (1.0 + lax.erf(u * inv_root_two))
    pdf = jnp.exp(-0.5 * u * u) * inv_root_tau
    return u * cdf, cdf + u * pdf


def fold(x):
    return jnp.sum(x.reshape(-1, 8, x.shape[1]), axis=0)


def mlp(core, ln_ref, d_branch, w_in, w_out, b_in, base, width, hid_ref, dpre_ref, keep, send, gbin_ref):
    sub = 256
    count = width // sub
    channels = ln_ref.shape[1]
    ln = ln_ref[...]

    def products(s):
        at = pl.ds(base + s * sub, sub)
        return dot(ln, w_in[at, :], NT), dot(d_branch[...], w_out[:, at], NN)

    ahead = products(0)
    for s in range(count):
        pre, d_hidden = ahead
        if s + 1 < count:
            ahead = products(s + 1)
        act, slope = gelu_pair(pre + line(b_in, pl.ds(base + s * sub, sub)))
        d_pre = d_hidden * slope
        at = slice(s * sub, (s + 1) * sub)
        gbin_ref[:, at] = jnp.sum(d_pre, axis=0, keepdims=True)
        hid_ref[:, at] = act.astype(bf16)
        dpre_ref[:, at] = d_pre.astype(bf16)

    def store(first, second):
        for s in range(count):
            at = slice(s * sub, (s + 1) * sub)
            gwin = dot(dpre_ref[:, at], ln_ref[...], TN).astype(bf16)
            for j in range(channels // LANES):
                start = j * width + s * sub
                first[start : start + sub, :] = gwin[:, j * LANES : (j + 1) * LANES]
            gwout = dot(d_branch[...], hid_ref[:, at], TN).astype(bf16)
            for j in range(sub // LANES):
                start = (s * sub // LANES + j) * channels
                second[start : start + channels, :] = gwout[:, j * LANES : (j + 1) * LANES]

    pl.when(core[0] == 0)(lambda: store(keep, send))
    pl.when(core[0] != 0)(lambda: store(send, keep))


PIXELS = 256


def mlp_first_kernel(
    base, width, core, ln_ref, cot, w_in, w_out, b_in, scale, branch_ref, dnorm_ref, d_branch_ref,
    keep, send, gbin_ref, hid_ref, dpre_ref,
):
    d_branch_ref[...] = (line(scale) * cot[...].astype(f32)).astype(bf16)
    mlp(core, ln_ref, d_branch_ref, w_in, w_out, b_in, base, width, hid_ref, dpre_ref, keep, send, gbin_ref)
    at = pl.ds(base, width)

    def step(i, _):
        to = pl.ds(pl.multiple_of(i * PIXELS, PIXELS), PIXELS)
        branch_ref[to, :] = dot(hid_ref[to, :], w_out[:, at], NT)
        dnorm_ref[to, :] = dot(dpre_ref[to, :], w_in[at, :], NN)
        return _

    lax.fori_loop(0, ln_ref.shape[0] // PIXELS, step, 0)


def mlp_second_kernel(
    base, width, core, ln_ref, cot, w_in, w_out, b_in, scale, b_out, gain, page, normed_ref, inv_ref,
    branch_ref, dnorm_ref, d_branch_ref,
    result, d_depth_ref, keep, send, gbin_ref, sums_ref,
    hid_ref, dpre_ref, sums,
):
    sums[...] = jnp.zeros_like(sums)
    mlp(core, ln_ref, d_branch_ref, w_in, w_out, b_in, base, width, hid_ref, dpre_ref, keep, send, gbin_ref)
    units = pl.ds(base, width)

    def step(i, _):
        at = pl.ds(pl.multiple_of(i * PIXELS, PIXELS), PIXELS)
        cot32 = cot[at, :].astype(f32)
        branch = dot(hid_ref[at, :], w_out[:, units], NT) + branch_ref[at, :] + line(b_out)
        result[at, :] = (page[at, :].astype(f32) + line(scale) * branch).astype(bf16)
        d_norm = dot(dpre_ref[at, :], w_in[units, :], NN) + dnorm_ref[at, :]
        normed = normed_ref[at, :]
        inv = inv_ref[at, 0:1]
        weighted = d_norm * normed
        s = d_norm * line(gain)
        mean_s = jnp.mean(s, axis=-1, keepdims=True)
        mean_sn = jnp.mean(s * normed, axis=-1, keepdims=True)
        d_depth = (inv * (s - mean_s - normed * mean_sn)).astype(bf16)
        d_depth_ref[at, :] = d_depth
        sums[0] += fold(cot32 * branch)
        sums[1] += fold(line(scale) * cot32)
        sums[2] += fold(weighted)
        sums[3] += fold(d_norm)
        sums[4] += fold(d_depth.astype(f32))
        return _

    lax.fori_loop(0, ln_ref.shape[0] // PIXELS, step, 0)
    for j in range(5):
        sums_ref[j : j + 1, :] = jnp.sum(sums[j], axis=0, keepdims=True)


SMALL = 64


def kernel_grad_kernel(keys, core, even, tile, d_depth, sums, gbin_a, gbin_b, *refs):
    received = dict(zip(keys, refs))
    keep, send, pad, d32, acc_ref = refs[len(keys) :]
    rows, cols, channels = tile.shape
    fill_around(pad, even, tile, received)
    d32[...] = d_depth[...].astype(f32)
    acc_ref[...] = jnp.zeros_like(acc_ref)

    def piece(slab, col, row):
        grads = []
        for i in range(BAND):
            at = pl.ds(pl.multiple_of((row + i) * cols + col, 8), 8)
            grads.append(d32[at, lanes(slab)])
        for b in range(7):
            acc = [None] * 7
            for r in range(BAND + 6):
                x = pad[slab, row + r, pl.ds(col + EDGE - 3 + b, 8), :]
                for a in range(7):
                    i = r - a
                    if 0 <= i < BAND:
                        acc[a] = x * grads[i] if acc[a] is None else acc[a] + x * grads[i]
            for a in range(7):
                acc_ref[slab, a * 7 + b] += acc[a]

    steps(rows, cols, channels, piece)

    def store(first, second):
        slabs, half = channels // LANES, SMALL // 2
        for slab in range(slabs):
            at = slice(slab * LANES, (slab + 1) * LANES)
            part = [jnp.sum(acc_ref[slab], axis=1), sums[:5, at]]
            for j in range((gbin_a.shape[1] + gbin_b.shape[1]) // channels):
                lane = (j * slabs + slab) * LANES
                source = gbin_a if lane < gbin_a.shape[1] else gbin_b
                lane = lane if lane < gbin_a.shape[1] else lane - gbin_a.shape[1]
                part.append(source[:, lane : lane + LANES])
            part = jnp.concatenate(part)
            part = jnp.concatenate([part, jnp.zeros((SMALL - part.shape[0], LANES), f32)])
            first[slab * half : (slab + 1) * half, :] = part[:half].astype(bf16)
            second[slab * half : (slab + 1) * half, :] = part[half:].astype(bf16)
        for ref in (first, second):
            ref[slabs * half :, :] = jnp.zeros((ref.shape[0] - slabs * half, LANES), bf16)

    pl.when(core[0] == 0)(lambda: store(keep, send))
    pl.when(core[0] != 0)(lambda: store(send, keep))


def conv_grad_kernel(tile, top, bottom, left, right, kernel, cot, out, pad, total):
    rows, cols, channels = tile.shape
    fill(pad, tile, top, bottom, left, right)

    def piece(slab, col, row):
        acc = taps(pad, kernel, slab, col, row, True)
        for i in range(BAND):
            at = pl.ds(pl.multiple_of((row + i) * cols + col, 8), 8)
            total[at, lanes(slab)] = acc[i]

    steps(rows, cols, channels, piece)
    block = 128

    def finish(i, _):
        at = pl.ds(pl.multiple_of(i * block, block), block)
        out[at, :] = (cot[at, :].astype(f32) + total[at, :]).astype(bf16)
        return _

    lax.fori_loop(0, rows * cols // block, finish, 0)


def call(body, outs, scratch, args, flops, scalars=0, after=(), size=24 << 20):
    held = len(args)

    def kernel(*refs):
        body(*refs[:held], *refs[held + len(after) :])

    vmem = pl.BlockSpec(memory_space=pltpu.VMEM)
    smem = pl.BlockSpec(memory_space=pltpu.SMEM)
    return pl.pallas_call(
        kernel,
        out_shape=[jax.ShapeDtypeStruct(shape, dtype) for shape, dtype in outs],
        in_specs=[smem] * scalars
        + [vmem] * (held - scalars)
        + [pl.BlockSpec(memory_space=pl.ANY)] * len(after),
        out_specs=[vmem] * len(outs),
        scratch_shapes=[pltpu.VMEM(shape, dtype) for shape, dtype in scratch],
        compiler_params=pltpu.CompilerParams(vmem_limit_bytes=size),
        cost_estimate=pl.CostEstimate(flops=flops, bytes_accessed=flops >> 10, transcendentals=0),
    )(*args, *after)


def bits(axis):
    return [(axis, j) for j in range(max(lax.axis_size(axis).bit_length() - 1, 0))]


def plane():
    return [("gy", 1), ("gx", 0)]


def beyond():
    return bits("gy")[2:] + bits("gx")[1:] + bits("rep")


def exchange(x, flips):
    sizes = [lax.axis_size(axis) for axis in AXES]
    perm = []
    for i in range(math.prod(sizes)):
        at = {"gy": i // (sizes[1] * sizes[2]), "gx": i // sizes[2] % sizes[1], "rep": i % sizes[2]}
        for axis, bit in flips:
            at[axis] ^= 1 << bit
        perm.append((i, (at["gy"] * sizes[1] + at["gx"]) * sizes[2] + at["rep"]))
    return lax.ppermute(x, AXES, perm)


def spread(parts):
    flips = [[g for j, g in enumerate(plane()) if delta >> j & 1] for delta in range(1, 4)]
    return [parts[0]] + [exchange(x, flip) for x, flip in zip(parts[1:], flips)]


def hold(arrays):
    return lax.optimization_barrier(arrays)


def chunks(rows, body):
    size = max(n for n in (128, 64, 32, 16) if rows % n == 0)

    def step(i, _):
        body(pl.multiple_of(i * size, size), size)
        return _

    lax.fori_loop(0, rows // size, step, 0, unroll=2 if rows // size > 1 else 1)


def first_sum_kernel(has_small, mine, *refs):
    wide, outs = refs[:2], refs[4 if has_small else 2 :]
    rows = wide[0].shape[0] // len(outs)
    for delta, out in enumerate(outs):
        to = mine[0] ^ delta

        def add(at, size):
            part = pl.ds(pl.multiple_of(to * rows + at, 16), size)
            out[pl.ds(at, size), :] = (wide[0][part, :].astype(f32) + wide[1][part, :].astype(f32)).astype(bf16)

        chunks(rows, add)
        end = rows
        if has_small:
            small = refs[2:4]
            size = small[0].shape[0] // len(outs)
            part = pl.ds(pl.multiple_of(to * size, 16), size)
            out[end : end + size, :] = (small[0][part, :].astype(f32) + small[1][part, :].astype(f32)).astype(bf16)
            end += size
        if end < out.shape[0]:
            out[end:, :] = jnp.zeros((out.shape[0] - end, LANES), bf16)


def sum_kernel(*refs):
    ins, out = refs[:-1], refs[-1]

    def add(at, size):
        part = pl.ds(at, size)
        out[part, :] = sum(r[part, :].astype(f32) for r in ins).astype(bf16)

    chunks(out.shape[0], add)


def join_kernel(mine, *refs):
    out = refs[-1]
    rows = refs[0].shape[0]
    for delta, ref in enumerate(refs[:-1]):
        out[pl.ds(pl.multiple_of((mine[0] ^ delta) * rows, 16), rows), :] = ref[...]


SUM_FLOPS = 1 << 20


def add_halves(mine, keep, other, *small):
    rows = (keep.shape[0] + (small[0].shape[0] if small else 0)) // 4
    return call(
        functools.partial(first_sum_kernel, bool(small)),
        [((rows, LANES), bf16)] * 4,
        [],
        (mine, keep, other, *small),
        SUM_FLOPS,
        1,
    )


def add(*arrays):
    (x,) = call(sum_kernel, [(arrays[0].shape, bf16)], [], arrays, SUM_FLOPS)
    return x


def join(mine, *parts):
    (x,) = call(join_kernel, [((4 * parts[0].shape[0], LANES), bf16)], [], (mine, *parts), SUM_FLOPS, 1)
    return x


def finish_kernel(
    factor, widths, core, own_a, other_a, own_b, other_b,
    win, wout, gk, scale, b_out, gain, shift, bias, b_in,
):
    channels, unit = wout.shape
    slabs = channels // LANES

    def rows(ref, width, at):
        part, block = ref.shape[0] // 4, width * slabs // 4
        start = at // block * part + at % block
        return ref[start : start + LANES, :].astype(f32) * factor

    def store(first, second, width, offset):
        for j in range(slabs):
            for i in range(0, unit, LANES):
                win[i : i + LANES, j * LANES : (j + 1) * LANES] = rows(first, width, j * width + offset + i)
        for j in range(unit // LANES):
            for i in range(0, channels, LANES):
                wout[i : i + LANES, j * LANES : (j + 1) * LANES] = rows(
                    second, width, (offset // LANES + j) * channels + i
                )

    def store_small(*halves):
        for slab in range(slabs):
            at = slice(slab * LANES, (slab + 1) * LANES)
            start = slab * (halves[0].shape[0] // 4) + widths[1] * slabs // 4
            values = jnp.concatenate([ref[start : start + SMALL // 2, :].astype(f32) for ref in halves]) * factor
            for j in range(7):
                gk[j, :, at] = values[7 * j : 7 * j + 7]
            for j, ref in enumerate((scale, b_out, gain, shift, bias)):
                ref[at] = values[49 + j]
            for j in range(b_in.shape[0] // channels):
                lane = (j * slabs + slab) * LANES
                b_in[lane : lane + LANES] = values[54 + j]

    is_first = core[0] == 0
    step = pl.program_id(0)
    for i in range(sum(widths) // unit):
        offset, halves = i * unit, (own_a, other_a)
        width = widths[0]
        if offset >= widths[0]:
            offset, halves, width = offset - widths[0], (own_b, other_b), widths[1]
        here = step == i
        pl.when(here & is_first)(functools.partial(store, *halves, width, offset))
        pl.when(here & ~is_first)(functools.partial(store, *halves[::-1], width, offset))
    pl.when((step == 0) & is_first)(lambda: store_small(own_b, other_b))
    pl.when((step == 0) & ~is_first)(lambda: store_small(other_b, own_b))


def finish(factor, widths, channels, core, *halves):
    hid, unit = sum(widths), widths[1]
    vmem = pl.BlockSpec(memory_space=pltpu.VMEM)
    outs = [(hid, channels), (channels, hid), (7, 7, channels)] + [(channels,)] * 5 + [(hid,)]
    return pl.pallas_call(
        functools.partial(finish_kernel, factor, widths),
        grid=(hid // unit,),
        out_shape=[jax.ShapeDtypeStruct(shape, f32) for shape in outs],
        in_specs=[pl.BlockSpec(memory_space=pltpu.SMEM)] + [vmem] * len(halves),
        out_specs=[
            pl.BlockSpec((unit, channels), lambda i: (i, 0)),
            pl.BlockSpec((channels, unit), lambda i: (0, i)),
        ]
        + [vmem] * 7,
        compiler_params=pltpu.CompilerParams(vmem_limit_bytes=24 << 20),
    )(core, *halves)


def shards(
    pages,
    cotangent,
    conv_kernel,
    conv_bias,
    norm_gain,
    norm_bias,
    w_in,
    b_in,
    w_out,
    b_out,
    layer_scale,
):
    _, rows, cols, channels = pages.shape
    hid = w_in.shape[0]
    pixels = rows * cols
    tile = pages.reshape(rows, cols, channels)
    page = pages.reshape(pixels, channels)
    cot = cotangent.reshape(pixels, channels)
    pad = ((channels // LANES, rows + 6, EDGE + cols + 8, LANES), f32)
    full = (pixels, channels)

    even_y = lax.axis_index("gy") % 2 == 0
    even_x = lax.axis_index("gx") % 2 == 0
    core = (lax.axis_index("gy") % 2).astype(jnp.int32).reshape(1)
    mine = (lax.axis_index("gy") // 2 % 2 + lax.axis_index("gx") % 2 * 2).astype(jnp.int32).reshape(1)
    even = jnp.stack([even_y, even_x]).astype(jnp.int32)
    even_y, even_x, even, core, mine, tile = hold((even_y, even_x, even, core, mine, tile))
    around = whole_halo(tile, even_y, even_x)
    conv_flops = 2 * 49 * pixels * channels * 60
    (inner_depth,) = call(conv_inner_kernel, [(full, f32)], [pad], (tile, conv_kernel), conv_flops)
    normed, inv, ln_out = call(
        functools.partial(conv_norm_kernel, tuple(around)),
        [(full, f32), ((pixels, LANES), f32), (full, bf16)],
        [pad, (full, f32)],
        (even, tile, inner_depth, conv_kernel, conv_bias, norm_gain, norm_bias, *around.values()),
        conv_flops,
        1,
    )
    acts = lambda width: [((pixels, width), bf16)] * 2
    packed = lambda width: [((width * channels // LANES, LANES), bf16)] * 2 + [((1, width), f32)]
    core_flip = [("gy", 0)]
    mlp_flops = 12 * pixels * channels * hid
    weights = (w_in, w_out, b_in, layer_scale)
    first, second = hid * 2 // 3, hid // 3
    branch, d_norm, d_branch, keep_a, send_a, gbin_a = call(
        functools.partial(mlp_first_kernel, 0, first),
        [(full, f32), (full, f32), (full, bf16)] + packed(first),
        acts(first),
        (core, ln_out, cot, *weights),
        mlp_flops,
        1,
    )
    other_a = exchange(send_a, core_flip)
    result, d_depth, keep_b, send_b, gbin_b, sums = call(
        functools.partial(mlp_second_kernel, first, second),
        [(full, bf16), (full, bf16)] + packed(second) + [((8, channels), f32)],
        acts(second) + [((8, 8, channels), f32)],
        (core, ln_out, cot, *weights, b_out, norm_gain, page, normed, inv, branch, d_norm, d_branch),
        mlp_flops,
        1,
    )
    d_tile = d_depth.reshape(tile.shape)
    other_a, d_tile, keep_b, send_b = hold((other_a, d_tile, keep_b, send_b))
    parts_a = add_halves(mine, keep_a, other_a)
    got_a = spread(parts_a)
    other_b = exchange(send_b, core_flip)
    d_around = halo(d_tile, even_y, even_x)
    small_rows = ((2 * SMALL, LANES), bf16)
    keep_s, send_s = call(
        functools.partial(kernel_grad_kernel, tuple(around)),
        [small_rows, small_rows],
        [pad, (full, f32), ((channels // LANES, 49, 8, LANES), f32)],
        (core, even, tile, d_tile.reshape(full), sums, gbin_a, gbin_b, *around.values()),
        conv_flops,
        2,
        (parts_a[1],),
    )
    got_a, keep_s, send_s, other_b = hold((got_a, keep_s, send_s, other_b))
    other_s = exchange(send_s, core_flip)
    part_a = add(*got_a)
    parts_b = add_halves(mine, keep_b, other_b, keep_s, other_s)
    flips = [[bit] for bit in beyond()]
    got_a, got_b = exchange(part_a, flips[0]), spread(parts_b)
    got_a, got_b = hold((got_a, got_b))
    part_a, part_b = add(part_a, got_a), add(*got_b)
    (grad_pages,) = call(
        conv_grad_kernel,
        [(full, bf16)],
        [pad, (full, f32)],
        (d_tile, *d_around, conv_kernel, cot),
        conv_flops,
        0,
        (part_a, part_b),
    )
    for ahead, behind in zip(flips[1:], flips):
        got_a, got_b, grad_pages = hold((exchange(part_a, ahead), exchange(part_b, behind), grad_pages))
        part_a, part_b = add(part_a, got_a), add(part_b, got_b)
    got_a, got_b = hold((spread([part_a] * 4), exchange(part_b, flips[-1])))
    half_a, part_b = join(mine, *got_a), add(part_b, got_b)
    got_a, got_b = hold(([half_a, exchange(half_a, core_flip)], spread([part_b] * 4)))
    half_b = join(mine, *got_b)
    got_b = [half_b, exchange(half_b, core_flip)]
    factor = float(pixels * lax.axis_size("gy") * lax.axis_size("gx") * lax.axis_size("rep")) ** (-0.5)
    win, wout, gk, g_scale, g_bout, g_gain, g_shift, g_bias, g_bin = finish(
        factor, (first, second), channels, core, *got_a, *got_b
    )
    return (
        result.reshape(pages.shape),
        grad_pages.reshape(pages.shape),
        gk,
        g_bias,
        g_gain,
        g_shift,
        win,
        g_bin,
        wout,
        g_bout,
        g_scale,
    )


def solution(mesh):
    split = P("rep", "gy", "gx", None)
    return jax.shard_map(
        shards,
        mesh=mesh,
        in_specs=(split, split) + (P(),) * 9,
        out_specs=(split, split) + (P(),) * 9,
        check_vma=False,
    )
```

```python
import functools
import math

import jax
import jax.numpy as jnp
from jax import lax
from jax.experimental import pallas as pl
from jax.experimental.pallas import tpu as pltpu
from jax.sharding import PartitionSpec as P

norm_epsilon = 1e-06
inv_root_two = 0.7071067811865476
inv_root_tau = 0.3989422804014327

LANES = 128
EDGE = 8
BAND = 32
AXES = ("gy", "gx", "rep")
f32 = jnp.float32
bf16 = jnp.bfloat16


def dot(a, b, dims):
    return lax.dot_general(a, b, (dims, ((), ())), preferred_element_type=f32)


NN = ((1,), (0,))
NT = ((1,), (1,))
TN = ((0,), (0,))


def pair_rounds(count):
    first = [(i, i + 1) for i in range(0, count - 1, 2)]
    second = [(i, i + 1) for i in range(1, count - 1, 2)]
    return [pairs + [(b, a) for a, b in pairs] for pairs in (first, second)]


def swap_edges(low, high, axis, even):
    got = []
    for pairs, is_high in zip(pair_rounds(lax.axis_size(axis)), (even, ~even)):
        if pairs:
            got.append(lax.ppermute(jnp.where(is_high, high, low), axis, pairs))
        else:
            got.append(jnp.zeros_like(low))
    return jnp.where(even, got[1], got[0]), jnp.where(even, got[0], got[1])


def halo_rows(tile, even):
    return swap_edges(tile[:3], tile[tile.shape[0] - 3 :], "gy", even)


def halo_cols(tile, top, bottom, even):
    column = [
        jnp.concatenate([part[:, at : at + 3] for part in (top, tile, bottom)], axis=0)
        for at in (0, tile.shape[1] - 3)
    ]
    return swap_edges(*column, "gx", even)


def fill_tile(pad, tile):
    rows, cols, channels = tile.shape
    for slab in range(channels // LANES):

        def body(row, _):
            pad[slab, row + 3, EDGE : EDGE + cols, :] = tile[row, :, slab * LANES : (slab + 1) * LANES].astype(f32)
            return _

        lax.fori_loop(0, rows, body, 0, unroll=4)


def fill(pad, tile, top, bottom, left, right):
    rows, cols, channels = tile.shape
    fill_tile(pad, tile)
    for slab in range(channels // LANES):
        at = slice(slab * LANES, (slab + 1) * LANES)
        pad[slab, 0:3, EDGE : EDGE + cols, :] = top[:, :, at].astype(f32)
        pad[slab, 3 + rows :, EDGE : EDGE + cols, :] = bottom[:, :, at].astype(f32)
        pad[slab, :, EDGE - 3 : EDGE, :] = left[:, :, at].astype(f32)
        pad[slab, :, EDGE + cols : EDGE + cols + 3, :] = right[:, :, at].astype(f32)


def steps(rows, cols, channels, body):
    slabs, tiles, bands = channels // LANES, cols // 8, rows // BAND

    def step(i, _):
        slab = i // (tiles * bands)
        rest = i % (tiles * bands)
        body(slab, pl.multiple_of(rest // bands * 8, 8), rest % bands * BAND)
        return _

    lax.fori_loop(0, slabs * tiles * bands, step, 0)


def lanes(slab):
    return pl.ds(pl.multiple_of(slab * LANES, LANES), LANES)


def taps(pad, kernel, slab, col, row, flip):
    acc = [None] * BAND
    for b in range(7):
        scale = []
        for a in range(7):
            i, j = (6 - a, 6 - b) if flip else (a, b)
            scale.append(jnp.broadcast_to(kernel[i, j : j + 1, lanes(slab)], (8, LANES)))
        for r in range(BAND + 6):
            x = pad[slab, row + r, pl.ds(col + EDGE - 3 + b, 8), :]
            for a in range(7):
                i = r - a
                if 0 <= i < BAND:
                    acc[i] = x * scale[a] if acc[i] is None else acc[i] + x * scale[a]
    return acc


def line(ref, at=slice(None)):
    return ref[at].reshape(1, -1)


def inner(cols, col):
    return (col > 0) & (col < cols - 8)


def conv_inner_kernel(tile, kernel, depth, pad):
    rows, cols, channels = tile.shape
    fill_tile(pad, tile)
    for edge in (pl.ds(0, 3), pl.ds(rows + 3, 3)):
        pad[:, edge, :, :] = jnp.zeros((channels // LANES, 3, pad.shape[2], LANES), f32)

    def piece(slab, col, row):
        @pl.when(inner(cols, col))
        def _():
            acc = taps(pad, kernel, slab, col, row, False)
            for i in range(BAND):
                at = pl.ds(pl.multiple_of((row + i) * cols + col, 8), 8)
                depth[at, lanes(slab)] = acc[i]

    steps(rows, cols, channels, piece)


def edge_taps(pad, kernel, slab, col, rows):
    acc = {}
    for b in range(7):
        for r in (0, 1, 2, rows + 3, rows + 4, rows + 5):
            x = pad[slab, r, pl.ds(col + EDGE - 3 + b, 8), :]
            for a in range(7):
                i = r - a
                if 0 <= i < rows:
                    term = x * jnp.broadcast_to(kernel[a, b : b + 1, lanes(slab)], (8, LANES))
                    acc[i] = acc[i] + term if i in acc else term
    return acc


def conv_norm_kernel(
    tile, top, bottom, left, right, depth_in, kernel, bias, gain, shift, normed_ref, inv_ref, ln_ref, pad, depth
):
    rows, cols, channels = tile.shape
    fill(pad, tile, top, bottom, left, right)

    def piece(slab, col, row):
        add = jnp.broadcast_to(line(bias, lanes(slab)), (8, LANES))

        @pl.when(~inner(cols, col))
        def _():
            acc = taps(pad, kernel, slab, col, row, False)
            for i in range(BAND):
                at = pl.ds(pl.multiple_of((row + i) * cols + col, 8), 8)
                depth[at, lanes(slab)] = acc[i] + add

        @pl.when(inner(cols, col) & (row == 0))
        def _():
            acc = edge_taps(pad, kernel, slab, col, rows)
            for i in range(rows):
                at = pl.ds(pl.multiple_of(i * cols + col, 8), 8)
                value = depth_in[at, lanes(slab)] + add
                depth[at, lanes(slab)] = value + acc[i] if i in acc else value

    steps(rows, cols, channels, piece)
    block = 128

    def norm(i, _):
        at = pl.ds(pl.multiple_of(i * block, block), block)
        x = depth[at, :]
        centred = x - jnp.mean(x, axis=-1, keepdims=True)
        inv = lax.rsqrt(jnp.mean(centred * centred, axis=-1, keepdims=True) + norm_epsilon)
        normed = centred * inv
        normed_ref[at, :] = normed
        inv_ref[at, :] = jnp.broadcast_to(inv, (block, LANES))
        ln_ref[at, :] = (normed * line(gain) + line(shift)).astype(bf16)
        return _

    lax.fori_loop(0, rows * cols // block, norm, 0)


def gelu_pair(u):
    cdf = 0.5 * (1.0 + lax.erf(u * inv_root_two))
    pdf = jnp.exp(-0.5 * u * u) * inv_root_tau
    return u * cdf, cdf + u * pdf


def fold(x):
    return jnp.sum(x.reshape(-1, 8, x.shape[1]), axis=0)


def mlp(core, ln_ref, d_branch, w_in, w_out, b_in, base, width, hid_ref, dpre_ref, first, second, keep, send, gbin_ref):
    sub = 256
    count = width // sub
    channels = ln_ref.shape[1]
    ln = ln_ref[...]

    def products(s):
        at = pl.ds(base + s * sub, sub)
        return dot(ln, w_in[at, :], NT), dot(d_branch[...], w_out[:, at], NN)

    ahead = products(0)
    for s in range(count):
        pre, d_hidden = ahead
        if s + 1 < count:
            ahead = products(s + 1)
        act, slope = gelu_pair(pre + line(b_in, pl.ds(base + s * sub, sub)))
        d_pre = d_hidden * slope
        at = slice(s * sub, (s + 1) * sub)
        gbin_ref[:, at] = jnp.sum(d_pre, axis=0, keepdims=True)
        hid_ref[:, at] = act.astype(bf16)
        dpre_ref[:, at] = d_pre.astype(bf16)
        gwin = dot(dpre_ref[:, at], ln, TN).astype(bf16)
        for j in range(channels // LANES):
            start = j * width + s * sub
            first[start : start + sub, :] = gwin[:, j * LANES : (j + 1) * LANES]
        gwout = dot(d_branch[...], hid_ref[:, at], TN).astype(bf16)
        for j in range(sub // LANES):
            start = (s * sub // LANES + j) * channels
            second[start : start + channels, :] = gwout[:, j * LANES : (j + 1) * LANES]

    def store(one, two):
        one[...] = first[...]
        two[...] = second[...]

    pl.when(core[0] == 0)(lambda: store(keep, send))
    pl.when(core[0] != 0)(lambda: store(send, keep))


PIXELS = 256


def mlp_first_kernel(
    base, width, core, ln_ref, cot, w_in, w_out, b_in, scale, branch_ref, dnorm_ref, d_branch_ref,
    keep, send, gbin_ref, hid_ref, dpre_ref, gwin, gwout,
):
    d_branch_ref[...] = (line(scale) * cot[...].astype(f32)).astype(bf16)
    mlp(core, ln_ref, d_branch_ref, w_in, w_out, b_in, base, width, hid_ref, dpre_ref, gwin, gwout, keep, send, gbin_ref)
    at = pl.ds(base, width)

    def step(i, _):
        to = pl.ds(pl.multiple_of(i * PIXELS, PIXELS), PIXELS)
        branch_ref[to, :] = dot(hid_ref[to, :], w_out[:, at], NT)
        dnorm_ref[to, :] = dot(dpre_ref[to, :], w_in[at, :], NN)
        return _

    lax.fori_loop(0, ln_ref.shape[0] // PIXELS, step, 0)


def mlp_second_kernel(
    base, width, core, ln_ref, cot, w_in, w_out, b_in, scale, b_out, gain, page, normed_ref, inv_ref,
    branch_ref, dnorm_ref, d_branch_ref,
    result, d_depth_ref, keep, send, gbin_ref, sums_ref,
    hid_ref, dpre_ref, gwin, gwout, sums,
):
    sums[...] = jnp.zeros_like(sums)
    mlp(core, ln_ref, d_branch_ref, w_in, w_out, b_in, base, width, hid_ref, dpre_ref, gwin, gwout, keep, send, gbin_ref)
    units = pl.ds(base, width)

    def step(i, _):
        at = pl.ds(pl.multiple_of(i * PIXELS, PIXELS), PIXELS)
        cot32 = cot[at, :].astype(f32)
        branch = dot(hid_ref[at, :], w_out[:, units], NT) + branch_ref[at, :] + line(b_out)
        result[at, :] = (page[at, :].astype(f32) + line(scale) * branch).astype(bf16)
        d_norm = dot(dpre_ref[at, :], w_in[units, :], NN) + dnorm_ref[at, :]
        normed = normed_ref[at, :]
        inv = inv_ref[at, 0:1]
        weighted = d_norm * normed
        s = d_norm * line(gain)
        mean_s = jnp.mean(s, axis=-1, keepdims=True)
        mean_sn = jnp.mean(s * normed, axis=-1, keepdims=True)
        d_depth = (inv * (s - mean_s - normed * mean_sn)).astype(bf16)
        d_depth_ref[at, :] = d_depth
        sums[0] += fold(cot32 * branch)
        sums[1] += fold(line(scale) * cot32)
        sums[2] += fold(weighted)
        sums[3] += fold(d_norm)
        sums[4] += fold(d_depth.astype(f32))
        return _

    lax.fori_loop(0, ln_ref.shape[0] // PIXELS, step, 0)
    for j in range(5):
        sums_ref[j : j + 1, :] = jnp.sum(sums[j], axis=0, keepdims=True)


SMALL = 64


def kernel_grad_kernel(
    core, tile, top, bottom, left, right, d_depth, sums, gbin_a, gbin_b, keep, send, pad, d32, acc_ref
):
    rows, cols, channels = tile.shape
    fill(pad, tile, top, bottom, left, right)
    d32[...] = d_depth[...].astype(f32)
    acc_ref[...] = jnp.zeros_like(acc_ref)

    def piece(slab, col, row):
        grads = []
        for i in range(BAND):
            at = pl.ds(pl.multiple_of((row + i) * cols + col, 8), 8)
            grads.append(d32[at, lanes(slab)])
        for b in range(7):
            acc = [None] * 7
            for r in range(BAND + 6):
                x = pad[slab, row + r, pl.ds(col + EDGE - 3 + b, 8), :]
                for a in range(7):
                    i = r - a
                    if 0 <= i < BAND:
                        acc[a] = x * grads[i] if acc[a] is None else acc[a] + x * grads[i]
            for a in range(7):
                acc_ref[slab, a * 7 + b] += acc[a]

    steps(rows, cols, channels, piece)

    def store(first, second):
        slabs, half = channels // LANES, SMALL // 2
        for slab in range(slabs):
            at = slice(slab * LANES, (slab + 1) * LANES)
            part = [jnp.sum(acc_ref[slab], axis=1), sums[:5, at]]
            for j in range((gbin_a.shape[1] + gbin_b.shape[1]) // channels):
                lane = (j * slabs + slab) * LANES
                source = gbin_a if lane < gbin_a.shape[1] else gbin_b
                lane = lane if lane < gbin_a.shape[1] else lane - gbin_a.shape[1]
                part.append(source[:, lane : lane + LANES])
            part = jnp.concatenate(part)
            part = jnp.concatenate([part, jnp.zeros((SMALL - part.shape[0], LANES), f32)])
            first[slab * half : (slab + 1) * half, :] = part[:half].astype(bf16)
            second[slab * half : (slab + 1) * half, :] = part[half:].astype(bf16)
        for ref in (first, second):
            ref[slabs * half :, :] = jnp.zeros((ref.shape[0] - slabs * half, LANES), bf16)

    pl.when(core[0] == 0)(lambda: store(keep, send))
    pl.when(core[0] != 0)(lambda: store(send, keep))


def conv_grad_kernel(tile, top, bottom, left, right, kernel, cot, out, pad, total):
    rows, cols, channels = tile.shape
    fill(pad, tile, top, bottom, left, right)

    def piece(slab, col, row):
        acc = taps(pad, kernel, slab, col, row, True)
        for i in range(BAND):
            at = pl.ds(pl.multiple_of((row + i) * cols + col, 8), 8)
            total[at, lanes(slab)] = acc[i]

    steps(rows, cols, channels, piece)
    block = 128

    def finish(i, _):
        at = pl.ds(pl.multiple_of(i * block, block), block)
        out[at, :] = (cot[at, :].astype(f32) + total[at, :]).astype(bf16)
        return _

    lax.fori_loop(0, rows * cols // block, finish, 0)


def call(body, outs, scratch, args, flops, scalars=0, after=(), size=24 << 20):
    held = len(args)

    def kernel(*refs):
        body(*refs[:held], *refs[held + len(after) :])

    vmem = pl.BlockSpec(memory_space=pltpu.VMEM)
    smem = pl.BlockSpec(memory_space=pltpu.SMEM)
    return pl.pallas_call(
        kernel,
        out_shape=[jax.ShapeDtypeStruct(shape, dtype) for shape, dtype in outs],
        in_specs=[smem] * scalars
        + [vmem] * (held - scalars)
        + [pl.BlockSpec(memory_space=pl.ANY)] * len(after),
        out_specs=[vmem] * len(outs),
        scratch_shapes=[pltpu.VMEM(shape, dtype) for shape, dtype in scratch],
        compiler_params=pltpu.CompilerParams(vmem_limit_bytes=size),
        cost_estimate=pl.CostEstimate(flops=flops, bytes_accessed=flops >> 10, transcendentals=0),
    )(*args, *after)


def bits(axis):
    return [(axis, j) for j in range(max(lax.axis_size(axis).bit_length() - 1, 0))]


def plane():
    return [("gy", 1), ("gx", 0)]


def beyond():
    return bits("gy")[2:] + bits("gx")[1:] + bits("rep")


def exchange(x, flips):
    sizes = [lax.axis_size(axis) for axis in AXES]
    perm = []
    for i in range(math.prod(sizes)):
        at = {"gy": i // (sizes[1] * sizes[2]), "gx": i // sizes[2] % sizes[1], "rep": i % sizes[2]}
        for axis, bit in flips:
            at[axis] ^= 1 << bit
        perm.append((i, (at["gy"] * sizes[1] + at["gx"]) * sizes[2] + at["rep"]))
    return lax.ppermute(x, AXES, perm)


def spread(parts):
    flips = [[g for j, g in enumerate(plane()) if delta >> j & 1] for delta in range(1, 4)]
    return [parts[0]] + [exchange(x, flip) for x, flip in zip(parts[1:], flips)]


def hold(arrays):
    return lax.optimization_barrier(arrays)


def chunks(rows, body):
    size = max(n for n in (128, 64, 32, 16) if rows % n == 0)

    def step(i, _):
        body(pl.multiple_of(i * size, size), size)
        return _

    lax.fori_loop(0, rows // size, step, 0, unroll=2 if rows // size > 1 else 1)


def first_sum_kernel(has_small, mine, *refs):
    wide, outs = refs[:2], refs[4 if has_small else 2 :]
    rows = wide[0].shape[0] // len(outs)
    for delta, out in enumerate(outs):
        to = mine[0] ^ delta

        def add(at, size):
            part = pl.ds(pl.multiple_of(to * rows + at, 16), size)
            out[pl.ds(at, size), :] = (wide[0][part, :].astype(f32) + wide[1][part, :].astype(f32)).astype(bf16)

        chunks(rows, add)
        end = rows
        if has_small:
            small = refs[2:4]
            size = small[0].shape[0] // len(outs)
            part = pl.ds(pl.multiple_of(to * size, 16), size)
            out[end : end + size, :] = (small[0][part, :].astype(f32) + small[1][part, :].astype(f32)).astype(bf16)
            end += size
        if end < out.shape[0]:
            out[end:, :] = jnp.zeros((out.shape[0] - end, LANES), bf16)


def sum_kernel(*refs):
    ins, out = refs[:-1], refs[-1]

    def add(at, size):
        part = pl.ds(at, size)
        out[part, :] = sum(r[part, :].astype(f32) for r in ins).astype(bf16)

    chunks(out.shape[0], add)


def join_kernel(mine, *refs):
    out = refs[-1]
    rows = refs[0].shape[0]
    for delta, ref in enumerate(refs[:-1]):
        out[pl.ds(pl.multiple_of((mine[0] ^ delta) * rows, 16), rows), :] = ref[...]


SUM_FLOPS = 1 << 20


def add_halves(mine, keep, other, *small):
    rows = (keep.shape[0] + (small[0].shape[0] if small else 0)) // 4
    return call(
        functools.partial(first_sum_kernel, bool(small)),
        [((rows, LANES), bf16)] * 4,
        [],
        (mine, keep, other, *small),
        SUM_FLOPS,
        1,
    )


def add(*arrays):
    (x,) = call(sum_kernel, [(arrays[0].shape, bf16)], [], arrays, SUM_FLOPS)
    return x


def join(mine, *parts):
    (x,) = call(join_kernel, [((4 * parts[0].shape[0], LANES), bf16)], [], (mine, *parts), SUM_FLOPS, 1)
    return x


def finish_kernel(factor, width, core, own, other, win, wout, *smalls):
    channels, unit = wout.shape
    slabs = channels // LANES

    def rows(ref, at):
        part, block = ref.shape[0] // 4, width * slabs // 4
        start = at // block * part + at % block
        return ref[start : start + LANES, :].astype(f32) * factor

    def store(first, second, offset):
        for j in range(slabs):
            for i in range(0, unit, LANES):
                win[i : i + LANES, j * LANES : (j + 1) * LANES] = rows(first, j * width + offset + i)
        for j in range(unit // LANES):
            for i in range(0, channels, LANES):
                wout[i : i + LANES, j * LANES : (j + 1) * LANES] = rows(
                    second, (offset // LANES + j) * channels + i
                )

    def store_small(*halves):
        gk, scale, b_out, gain, shift, bias, b_in = smalls
        for slab in range(slabs):
            at = slice(slab * LANES, (slab + 1) * LANES)
            start = slab * (halves[0].shape[0] // 4) + width * slabs // 4
            values = jnp.concatenate([ref[start : start + SMALL // 2, :].astype(f32) for ref in halves]) * factor
            for j in range(7):
                gk[j, :, at] = values[7 * j : 7 * j + 7]
            for j, ref in enumerate((scale, b_out, gain, shift, bias)):
                ref[at] = values[49 + j]
            for j in range(b_in.shape[0] // channels):
                lane = (j * slabs + slab) * LANES
                b_in[lane : lane + LANES] = values[54 + j]

    is_first = core[0] == 0
    step = pl.program_id(0)
    for i in range(width // unit):
        here = step == i
        pl.when(here & is_first)(functools.partial(store, own, other, i * unit))
        pl.when(here & ~is_first)(functools.partial(store, other, own, i * unit))
    if smalls:
        pl.when(is_first)(lambda: store_small(own, other))
        pl.when(~is_first)(lambda: store_small(other, own))


def finish(factor, base, width, unit, hid, channels, core, own, other, whole=()):
    vmem = pl.BlockSpec(memory_space=pltpu.VMEM)
    start = base // unit
    outs = [(hid, channels), (channels, hid)]
    smalls = [(7, 7, channels)] + [(channels,)] * 5 + [(hid,)] if whole else []

    def kernel(core, own, other, *refs):
        finish_kernel(factor, width, core, own, other, *refs[len(whole) :])

    return pl.pallas_call(
        kernel,
        grid=(width // unit,),
        out_shape=[jax.ShapeDtypeStruct(shape, f32) for shape in outs + smalls],
        in_specs=[pl.BlockSpec(memory_space=pltpu.SMEM), vmem, vmem]
        + [pl.BlockSpec(memory_space=pl.ANY)] * len(whole),
        out_specs=[
            pl.BlockSpec((unit, channels), lambda i: (start + i, 0)),
            pl.BlockSpec((channels, unit), lambda i: (0, start + i)),
        ]
        + [vmem] * len(smalls),
        input_output_aliases={3: 0, 4: 1} if whole else {},
        compiler_params=pltpu.CompilerParams(vmem_limit_bytes=24 << 20),
    )(core, own, other, *whole)


def shards(
    pages,
    cotangent,
    conv_kernel,
    conv_bias,
    norm_gain,
    norm_bias,
    w_in,
    b_in,
    w_out,
    b_out,
    layer_scale,
):
    _, rows, cols, channels = pages.shape
    hid = w_in.shape[0]
    pixels = rows * cols
    tile = pages.reshape(rows, cols, channels)
    page = pages.reshape(pixels, channels)
    cot = cotangent.reshape(pixels, channels)
    pad = ((channels // LANES, rows + 6, EDGE + cols + 8, LANES), f32)
    full = (pixels, channels)

    even_y = lax.axis_index("gy") % 2 == 0
    even_x = lax.axis_index("gx") % 2 == 0
    core = (lax.axis_index("gy") % 2).astype(jnp.int32).reshape(1)
    mine = (lax.axis_index("gy") // 2 % 2 + lax.axis_index("gx") % 2 * 2).astype(jnp.int32).reshape(1)
    even_y, even_x, core, mine, tile = hold((even_y, even_x, core, mine, tile))
    around = halo_rows(tile, even_y)
    around += halo_cols(tile, *around, even_x)
    conv_flops = 2 * 49 * pixels * channels * 60
    (inner_depth,) = call(conv_inner_kernel, [(full, f32)], [pad], (tile, conv_kernel), conv_flops)
    normed, inv, ln_out = call(
        conv_norm_kernel,
        [(full, f32), ((pixels, LANES), f32), (full, bf16)],
        [pad, (full, f32)],
        (tile, *around, inner_depth, conv_kernel, conv_bias, norm_gain, norm_bias),
        conv_flops,
    )
    acts = lambda width: [((pixels, width), bf16)] * 2 + [((width * channels // LANES, LANES), bf16)] * 2
    packed = lambda width: [((width * channels // LANES, LANES), bf16)] * 2 + [((1, width), f32)]
    core_flip = [("gy", 0)]
    mlp_flops = 12 * pixels * channels * hid
    weights = (w_in, w_out, b_in, layer_scale)
    first, second = hid * 2 // 3, hid // 3
    branch, d_norm, d_branch, keep_a, send_a, gbin_a = call(
        functools.partial(mlp_first_kernel, 0, first),
        [(full, f32), (full, f32), (full, bf16)] + packed(first),
        acts(first),
        (core, ln_out, cot, *weights),
        mlp_flops,
        1,
    )
    other_a = exchange(send_a, core_flip)
    result, d_depth, keep_b, send_b, gbin_b, sums = call(
        functools.partial(mlp_second_kernel, first, second),
        [(full, bf16), (full, bf16)] + packed(second) + [((8, channels), f32)],
        acts(second) + [((8, 8, channels), f32)],
        (core, ln_out, cot, *weights, b_out, norm_gain, page, normed, inv, branch, d_norm, d_branch),
        mlp_flops,
        1,
    )
    d_tile = d_depth.reshape(tile.shape)
    other_a, d_tile, keep_b, send_b = hold((other_a, d_tile, keep_b, send_b))
    parts_a = add_halves(mine, keep_a, other_a)
    got_a = spread(parts_a)
    other_b = exchange(send_b, core_flip)
    small_rows = ((2 * SMALL, LANES), bf16)
    keep_s, send_s = call(
        kernel_grad_kernel,
        [small_rows, small_rows],
        [pad, (full, f32), ((channels // LANES, 49, 8, LANES), f32)],
        (core, tile, *around, d_tile.reshape(full), sums, gbin_a, gbin_b),
        conv_flops,
        1,
        (parts_a[1],),
    )
    got_a, keep_s, send_s, other_b = hold((got_a, keep_s, send_s, other_b))
    other_s = exchange(send_s, core_flip)
    part_a = add(*got_a)
    parts_b = add_halves(mine, keep_b, other_b, keep_s, other_s)
    flips = [[bit] for bit in beyond()]
    parts_b, d_tile = hold((parts_b, d_tile))
    got_a, got_b, d_rows = hold((exchange(part_a, flips[0]), spread(parts_b), halo_rows(d_tile, even_y)))
    part_a, part_b = add(part_a, got_a), add(*got_b)
    d_around = d_rows + halo_cols(d_tile, *d_rows, even_x)
    for ahead, behind in zip(flips[1:], flips):
        got_a, got_b, d_around = hold((exchange(part_a, ahead), exchange(part_b, behind), d_around))
        part_a, part_b = add(part_a, got_a), add(part_b, got_b)
    (grad_pages,) = call(
        conv_grad_kernel,
        [(full, bf16)],
        [pad, (full, f32)],
        (d_tile, *d_around, conv_kernel, cot),
        conv_flops,
        0,
        (part_a, part_b),
    )
    got_a, got_b, grad_pages = hold((spread([part_a] * 4), exchange(part_b, flips[-1]), grad_pages))
    half_a, part_b = join(mine, *got_a), add(part_b, got_b)
    got_a, got_b = hold(([half_a, exchange(half_a, core_flip)], spread([part_b] * 4)))
    half_b = join(mine, *got_b)
    got_b = [half_b, exchange(half_b, core_flip)]
    factor = float(pixels * lax.axis_size("gy") * lax.axis_size("gx") * lax.axis_size("rep")) ** (-0.5)
    begun = finish(factor, 0, first, second, hid, channels, core, *got_a)
    win, wout, gk, g_scale, g_bout, g_gain, g_shift, g_bias, g_bin = finish(
        factor, first, second, second, hid, channels, core, *got_b, begun
    )
    return (
        result.reshape(pages.shape),
        grad_pages.reshape(pages.shape),
        gk,
        g_bias,
        g_gain,
        g_shift,
        win,
        g_bin,
        wout,
        g_bout,
        g_scale,
    )


def solution(mesh):
    split = P("rep", "gy", "gx", None)
    return jax.shard_map(
        shards,
        mesh=mesh,
        in_specs=(split, split) + (P(),) * 9,
        out_specs=(split, split) + (P(),) * 9,
        check_vma=False,
    )
```

```python
import functools
import math

import jax
import jax.numpy as jnp
from jax import lax
from jax.experimental import pallas as pl
from jax.experimental.pallas import tpu as pltpu
from jax.sharding import PartitionSpec as P

norm_epsilon = 1e-06
inv_root_two = 0.7071067811865476
inv_root_tau = 0.3989422804014327

LANES = 128
EDGE = 8
BAND = 32
AXES = ("gy", "gx", "rep")
f32 = jnp.float32
bf16 = jnp.bfloat16


def dot(a, b, dims):
    return lax.dot_general(a, b, (dims, ((), ())), preferred_element_type=f32)


NN = ((1,), (0,))
NT = ((1,), (1,))
TN = ((0,), (0,))


def pair_rounds(count):
    first = [(i, i + 1) for i in range(0, count - 1, 2)]
    second = [(i, i + 1) for i in range(1, count - 1, 2)]
    return [pairs + [(b, a) for a, b in pairs] for pairs in (first, second)]


def halo(tile, even_y, even_x):
    rows, cols, _ = tile.shape

    def swap_edges(low, high, axis, even):
        got = []
        for pairs, is_high in zip(pair_rounds(lax.axis_size(axis)), (even, ~even)):
            if pairs:
                got.append(lax.ppermute(jnp.where(is_high, high, low), axis, pairs))
            else:
                got.append(jnp.zeros_like(low))
        return jnp.where(even, got[1], got[0]), jnp.where(even, got[0], got[1])

    top, bottom = swap_edges(tile[:3], tile[rows - 3 :], "gy", even_y)
    column = [
        jnp.concatenate([part[:, at : at + 3] for part in (top, tile, bottom)], axis=0) for at in (0, cols - 3)
    ]
    left, right = swap_edges(*column, "gx", even_x)
    return top, bottom, left, right


def fill(pad, tile, top, bottom, left, right):
    rows, cols, channels = tile.shape
    for slab in range(channels // LANES):
        at = slice(slab * LANES, (slab + 1) * LANES)
        pad[slab, 0:3, EDGE : EDGE + cols, :] = top[:, :, at].astype(f32)
        pad[slab, 3 + rows :, EDGE : EDGE + cols, :] = bottom[:, :, at].astype(f32)
        pad[slab, :, EDGE - 3 : EDGE, :] = left[:, :, at].astype(f32)
        pad[slab, :, EDGE + cols : EDGE + cols + 3, :] = right[:, :, at].astype(f32)

        def body(row, _):
            pad[slab, row + 3, EDGE : EDGE + cols, :] = tile[row, :, at].astype(f32)
            return _

        lax.fori_loop(0, rows, body, 0, unroll=4)


def steps(rows, cols, channels, body):
    slabs, tiles, bands = channels // LANES, cols // 8, rows // BAND

    def step(i, _):
        slab = i // (tiles * bands)
        rest = i % (tiles * bands)
        body(slab, pl.multiple_of(rest // bands * 8, 8), rest % bands * BAND)
        return _

    lax.fori_loop(0, slabs * tiles * bands, step, 0)


def lanes(slab):
    return pl.ds(pl.multiple_of(slab * LANES, LANES), LANES)


def taps(pad, kernel, slab, col, row, flip):
    acc = [None] * BAND
    for b in range(7):
        scale = []
        for a in range(7):
            i, j = (6 - a, 6 - b) if flip else (a, b)
            scale.append(jnp.broadcast_to(kernel[i, j : j + 1, lanes(slab)], (8, LANES)))
        for r in range(BAND + 6):
            x = pad[slab, row + r, pl.ds(col + EDGE - 3 + b, 8), :]
            for a in range(7):
                i = r - a
                if 0 <= i < BAND:
                    acc[i] = x * scale[a] if acc[i] is None else acc[i] + x * scale[a]
    return acc


def line(ref, at=slice(None)):
    return ref[at].reshape(1, -1)


def conv_norm_kernel(
    tile, top, bottom, left, right, kernel, bias, gain, shift, normed_ref, inv_ref, ln_ref, pad, depth
):
    rows, cols, channels = tile.shape
    fill(pad, tile, top, bottom, left, right)

    def piece(slab, col, row):
        acc = taps(pad, kernel, slab, col, row, False)
        add = jnp.broadcast_to(line(bias, lanes(slab)), (8, LANES))
        for i in range(BAND):
            at = pl.ds(pl.multiple_of((row + i) * cols + col, 8), 8)
            depth[at, lanes(slab)] = acc[i] + add

    steps(rows, cols, channels, piece)
    block = 128

    def norm(i, _):
        at = pl.ds(pl.multiple_of(i * block, block), block)
        x = depth[at, :]
        centred = x - jnp.mean(x, axis=-1, keepdims=True)
        inv = lax.rsqrt(jnp.mean(centred * centred, axis=-1, keepdims=True) + norm_epsilon)
        normed = centred * inv
        normed_ref[at, :] = normed
        inv_ref[at, :] = jnp.broadcast_to(inv, (block, LANES))
        ln_ref[at, :] = (normed * line(gain) + line(shift)).astype(bf16)
        return _

    lax.fori_loop(0, rows * cols // block, norm, 0)


def gelu_pair(u):
    cdf = 0.5 * (1.0 + lax.erf(u * inv_root_two))
    pdf = jnp.exp(-0.5 * u * u) * inv_root_tau
    return u * cdf, cdf + u * pdf


def fold(x):
    return jnp.sum(x.reshape(-1, 8, x.shape[1]), axis=0)


def mlp(core, ln_ref, d_branch, w_in, w_out, b_in, base, width, hid_ref, dpre_ref, keep, send, gbin_ref):
    sub = 256
    count = width // sub
    channels = ln_ref.shape[1]
    ln = ln_ref[...]

    def products(s):
        at = pl.ds(base + s * sub, sub)
        return dot(ln, w_in[at, :], NT), dot(d_branch[...], w_out[:, at], NN)

    ahead = products(0)
    for s in range(count):
        pre, d_hidden = ahead
        if s + 1 < count:
            ahead = products(s + 1)
        act, slope = gelu_pair(pre + line(b_in, pl.ds(base + s * sub, sub)))
        d_pre = d_hidden * slope
        at = slice(s * sub, (s + 1) * sub)
        gbin_ref[:, at] = jnp.sum(d_pre, axis=0, keepdims=True)
        hid_ref[:, at] = act.astype(bf16)
        dpre_ref[:, at] = d_pre.astype(bf16)

    def store(first, second):
        for s in range(count):
            at = slice(s * sub, (s + 1) * sub)
            gwin = dot(dpre_ref[:, at], ln_ref[...], TN).astype(bf16)
            for j in range(channels // LANES):
                start = j * width + s * sub
                first[start : start + sub, :] = gwin[:, j * LANES : (j + 1) * LANES]
            gwout = dot(d_branch[...], hid_ref[:, at], TN).astype(bf16)
            for j in range(sub // LANES):
                start = (s * sub // LANES + j) * channels
                second[start : start + channels, :] = gwout[:, j * LANES : (j + 1) * LANES]

    pl.when(core[0] == 0)(lambda: store(keep, send))
    pl.when(core[0] != 0)(lambda: store(send, keep))


PIXELS = 256


def mlp_block(ln, d_branch, w_in, w_out, b_in, base, width, hid_ref, dpre_ref, gbin):
    sub = 256
    count = width // sub

    def products(s):
        at = pl.ds(base + s * sub, sub)
        return dot(ln, w_in[at, :], NT), dot(d_branch, w_out[:, at], NN)

    ahead = products(0)
    for s in range(count):
        pre, d_hidden = ahead
        if s + 1 < count:
            ahead = products(s + 1)
        act, slope = gelu_pair(pre + line(b_in, pl.ds(base + s * sub, sub)))
        d_pre = d_hidden * slope
        gbin[:, s * sub : (s + 1) * sub] += fold(d_pre)
        hid_ref[:, s * sub : (s + 1) * sub] = act.astype(bf16)
        dpre_ref[:, s * sub : (s + 1) * sub] = d_pre.astype(bf16)
    at = pl.ds(base, width)
    hidden, d_pre = hid_ref[...], dpre_ref[...]
    branch = dot(hidden, w_out[:, at], NT)
    d_norm = dot(d_pre, w_in[at, :], NN)
    return hidden, d_pre, branch, d_norm


def pack_grads(core, keep, send, gwin, gwout, gbin_ref, gbin):
    width, channels = gwin.shape

    def store(first, second):
        for j in range(channels // LANES):
            first[j * width : (j + 1) * width, :] = gwin[:, j * LANES : (j + 1) * LANES].astype(bf16)
        for j in range(width // LANES):
            second[j * channels : (j + 1) * channels, :] = gwout[
                :, j * LANES : (j + 1) * LANES
            ].astype(bf16)

    pl.when(core[0] == 0)(lambda: store(keep, send))
    pl.when(core[0] != 0)(lambda: store(send, keep))
    gbin_ref[...] = jnp.sum(gbin[...], axis=0, keepdims=True)


MLP_BLOCK = 256


def mlp_first_kernel(
    base, width, core, ln_ref, cot, w_in, w_out, b_in, scale, branch_ref, dnorm_ref, d_branch_ref, keep, send, gbin_ref,
    hid_ref, dpre_ref, gwin, gwout, gbin,
):
    gwin[...] = jnp.zeros_like(gwin)
    gwout[...] = jnp.zeros_like(gwout)
    gbin[...] = jnp.zeros_like(gbin)

    def step(i, _):
        at = pl.ds(pl.multiple_of(i * MLP_BLOCK, MLP_BLOCK), MLP_BLOCK)
        ln = ln_ref[at, :]
        d_branch = (line(scale) * cot[at, :].astype(f32)).astype(bf16)
        hidden, d_pre, branch, d_norm = mlp_block(
            ln, d_branch, w_in, w_out, b_in, base, width, hid_ref, dpre_ref, gbin
        )
        d_branch_ref[at, :] = d_branch
        branch_ref[at, :] = branch
        dnorm_ref[at, :] = d_norm
        gwin[...] += dot(d_pre, ln, TN)
        gwout[...] += dot(d_branch, hidden, TN)
        return _

    lax.fori_loop(0, ln_ref.shape[0] // MLP_BLOCK, step, 0)
    pack_grads(core, keep, send, gwin, gwout, gbin_ref, gbin)


def mlp_second_kernel(
    base, width, core, ln_ref, cot, w_in, w_out, b_in, scale, b_out, gain, page, normed_ref, inv_ref,
    branch_ref, dnorm_ref, d_branch_ref,
    result, d_depth_ref, keep, send, gbin_ref, sums_ref,
    hid_ref, dpre_ref, sums,
):
    sums[...] = jnp.zeros_like(sums)
    mlp(core, ln_ref, d_branch_ref, w_in, w_out, b_in, base, width, hid_ref, dpre_ref, keep, send, gbin_ref)
    units = pl.ds(base, width)

    def step(i, _):
        at = pl.ds(pl.multiple_of(i * PIXELS, PIXELS), PIXELS)
        cot32 = cot[at, :].astype(f32)
        branch = dot(hid_ref[at, :], w_out[:, units], NT) + branch_ref[at, :] + line(b_out)
        result[at, :] = (page[at, :].astype(f32) + line(scale) * branch).astype(bf16)
        d_norm = dot(dpre_ref[at, :], w_in[units, :], NN) + dnorm_ref[at, :]
        normed = normed_ref[at, :]
        inv = inv_ref[at, 0:1]
        weighted = d_norm * normed
        s = d_norm * line(gain)
        mean_s = jnp.mean(s, axis=-1, keepdims=True)
        mean_sn = jnp.mean(s * normed, axis=-1, keepdims=True)
        d_depth = (inv * (s - mean_s - normed * mean_sn)).astype(bf16)
        d_depth_ref[at, :] = d_depth
        sums[0] += fold(cot32 * branch)
        sums[1] += fold(line(scale) * cot32)
        sums[2] += fold(weighted)
        sums[3] += fold(d_norm)
        sums[4] += fold(d_depth.astype(f32))
        return _

    lax.fori_loop(0, ln_ref.shape[0] // PIXELS, step, 0)
    for j in range(5):
        sums_ref[j : j + 1, :] = jnp.sum(sums[j], axis=0, keepdims=True)


SMALL = 64


def kernel_grad_kernel(
    core, tile, top, bottom, left, right, d_depth, sums, gbin_a, gbin_b, keep, send, pad, d32, acc_ref
):
    rows, cols, channels = tile.shape
    fill(pad, tile, top, bottom, left, right)
    d32[...] = d_depth[...].astype(f32)
    acc_ref[...] = jnp.zeros_like(acc_ref)

    def piece(slab, col, row):
        grads = []
        for i in range(BAND):
            at = pl.ds(pl.multiple_of((row + i) * cols + col, 8), 8)
            grads.append(d32[at, lanes(slab)])
        for b in range(7):
            acc = [None] * 7
            for r in range(BAND + 6):
                x = pad[slab, row + r, pl.ds(col + EDGE - 3 + b, 8), :]
                for a in range(7):
                    i = r - a
                    if 0 <= i < BAND:
                        acc[a] = x * grads[i] if acc[a] is None else acc[a] + x * grads[i]
            for a in range(7):
                acc_ref[slab, a * 7 + b] += acc[a]

    steps(rows, cols, channels, piece)

    def store(first, second):
        slabs, half = channels // LANES, SMALL // 2
        for slab in range(slabs):
            at = slice(slab * LANES, (slab + 1) * LANES)
            part = [jnp.sum(acc_ref[slab], axis=1), sums[:5, at]]
            for j in range((gbin_a.shape[1] + gbin_b.shape[1]) // channels):
                lane = (j * slabs + slab) * LANES
                source = gbin_a if lane < gbin_a.shape[1] else gbin_b
                lane = lane if lane < gbin_a.shape[1] else lane - gbin_a.shape[1]
                part.append(source[:, lane : lane + LANES])
            part = jnp.concatenate(part)
            part = jnp.concatenate([part, jnp.zeros((SMALL - part.shape[0], LANES), f32)])
            first[slab * half : (slab + 1) * half, :] = part[:half].astype(bf16)
            second[slab * half : (slab + 1) * half, :] = part[half:].astype(bf16)
        for ref in (first, second):
            ref[slabs * half :, :] = jnp.zeros((ref.shape[0] - slabs * half, LANES), bf16)

    pl.when(core[0] == 0)(lambda: store(keep, send))
    pl.when(core[0] != 0)(lambda: store(send, keep))


def conv_grad_kernel(tile, top, bottom, left, right, kernel, cot, out, pad, total):
    rows, cols, channels = tile.shape
    fill(pad, tile, top, bottom, left, right)

    def piece(slab, col, row):
        acc = taps(pad, kernel, slab, col, row, True)
        for i in range(BAND):
            at = pl.ds(pl.multiple_of((row + i) * cols + col, 8), 8)
            total[at, lanes(slab)] = acc[i]

    steps(rows, cols, channels, piece)
    block = 128

    def finish(i, _):
        at = pl.ds(pl.multiple_of(i * block, block), block)
        out[at, :] = (cot[at, :].astype(f32) + total[at, :]).astype(bf16)
        return _

    lax.fori_loop(0, rows * cols // block, finish, 0)


def call(body, outs, scratch, args, flops, scalars=0, after=(), size=24 << 20):
    held = len(args)

    def kernel(*refs):
        body(*refs[:held], *refs[held + len(after) :])

    vmem = pl.BlockSpec(memory_space=pltpu.VMEM)
    smem = pl.BlockSpec(memory_space=pltpu.SMEM)
    return pl.pallas_call(
        kernel,
        out_shape=[jax.ShapeDtypeStruct(shape, dtype) for shape, dtype in outs],
        in_specs=[smem] * scalars
        + [vmem] * (held - scalars)
        + [pl.BlockSpec(memory_space=pl.ANY)] * len(after),
        out_specs=[vmem] * len(outs),
        scratch_shapes=[pltpu.VMEM(shape, dtype) for shape, dtype in scratch],
        compiler_params=pltpu.CompilerParams(vmem_limit_bytes=size),
        cost_estimate=pl.CostEstimate(flops=flops, bytes_accessed=flops >> 10, transcendentals=0),
    )(*args, *after)


def bits(axis):
    return [(axis, j) for j in range(max(lax.axis_size(axis).bit_length() - 1, 0))]


def plane():
    return [("gy", 1), ("gx", 0)]


def beyond():
    return bits("gy")[2:] + bits("gx")[1:] + bits("rep")


def exchange(x, flips):
    sizes = [lax.axis_size(axis) for axis in AXES]
    perm = []
    for i in range(math.prod(sizes)):
        at = {"gy": i // (sizes[1] * sizes[2]), "gx": i // sizes[2] % sizes[1], "rep": i % sizes[2]}
        for axis, bit in flips:
            at[axis] ^= 1 << bit
        perm.append((i, (at["gy"] * sizes[1] + at["gx"]) * sizes[2] + at["rep"]))
    return lax.ppermute(x, AXES, perm)


def spread(parts):
    flips = [[g for j, g in enumerate(plane()) if delta >> j & 1] for delta in range(1, 4)]
    return [parts[0]] + [exchange(x, flip) for x, flip in zip(parts[1:], flips)]


def hold(arrays):
    return lax.optimization_barrier(arrays)


def chunks(rows, body):
    size = max(n for n in (128, 64, 32, 16) if rows % n == 0)

    def step(i, _):
        body(pl.multiple_of(i * size, size), size)
        return _

    lax.fori_loop(0, rows // size, step, 0, unroll=2 if rows // size > 1 else 1)


def first_sum_kernel(has_small, mine, *refs):
    wide, outs = refs[:2], refs[4 if has_small else 2 :]
    rows = wide[0].shape[0] // len(outs)
    for delta, out in enumerate(outs):
        to = mine[0] ^ delta

        def add(at, size):
            part = pl.ds(pl.multiple_of(to * rows + at, 16), size)
            out[pl.ds(at, size), :] = (wide[0][part, :].astype(f32) + wide[1][part, :].astype(f32)).astype(bf16)

        chunks(rows, add)
        end = rows
        if has_small:
            small = refs[2:4]
            size = small[0].shape[0] // len(outs)
            part = pl.ds(pl.multiple_of(to * size, 16), size)
            out[end : end + size, :] = (small[0][part, :].astype(f32) + small[1][part, :].astype(f32)).astype(bf16)
            end += size
        if end < out.shape[0]:
            out[end:, :] = jnp.zeros((out.shape[0] - end, LANES), bf16)


def sum_kernel(*refs):
    ins, out = refs[:-1], refs[-1]

    def add(at, size):
        part = pl.ds(at, size)
        out[part, :] = sum(r[part, :].astype(f32) for r in ins).astype(bf16)

    chunks(out.shape[0], add)


def join_kernel(mine, *refs):
    out = refs[-1]
    rows = refs[0].shape[0]
    for delta, ref in enumerate(refs[:-1]):
        out[pl.ds(pl.multiple_of((mine[0] ^ delta) * rows, 16), rows), :] = ref[...]


SUM_FLOPS = 1 << 20


def add_halves(mine, keep, other, *small):
    rows = (keep.shape[0] + (small[0].shape[0] if small else 0)) // 4
    return call(
        functools.partial(first_sum_kernel, bool(small)),
        [((rows, LANES), bf16)] * 4,
        [],
        (mine, keep, other, *small),
        SUM_FLOPS,
        1,
    )


def add(*arrays):
    (x,) = call(sum_kernel, [(arrays[0].shape, bf16)], [], arrays, SUM_FLOPS)
    return x


def join(mine, *parts):
    (x,) = call(join_kernel, [((4 * parts[0].shape[0], LANES), bf16)], [], (mine, *parts), SUM_FLOPS, 1)
    return x


def finish_kernel(factor, width, core, own, other, win, wout, *smalls):
    channels, unit = wout.shape
    slabs = channels // LANES

    def rows(ref, at):
        part, block = ref.shape[0] // 4, width * slabs // 4
        start = at // block * part + at % block
        return ref[start : start + LANES, :].astype(f32) * factor

    def store(first, second, offset):
        for j in range(slabs):
            for i in range(0, unit, LANES):
                win[i : i + LANES, j * LANES : (j + 1) * LANES] = rows(first, j * width + offset + i)
        for j in range(unit // LANES):
            for i in range(0, channels, LANES):
                wout[i : i + LANES, j * LANES : (j + 1) * LANES] = rows(
                    second, (offset // LANES + j) * channels + i
                )

    def store_small(*halves):
        gk, scale, b_out, gain, shift, bias, b_in = smalls
        for slab in range(slabs):
            at = slice(slab * LANES, (slab + 1) * LANES)
            start = slab * (halves[0].shape[0] // 4) + width * slabs // 4
            values = jnp.concatenate([ref[start : start + SMALL // 2, :].astype(f32) for ref in halves]) * factor
            for j in range(7):
                gk[j, :, at] = values[7 * j : 7 * j + 7]
            for j, ref in enumerate((scale, b_out, gain, shift, bias)):
                ref[at] = values[49 + j]
            for j in range(b_in.shape[0] // channels):
                lane = (j * slabs + slab) * LANES
                b_in[lane : lane + LANES] = values[54 + j]

    is_first = core[0] == 0
    step = pl.program_id(0)
    for i in range(width // unit):
        here = step == i
        pl.when(here & is_first)(functools.partial(store, own, other, i * unit))
        pl.when(here & ~is_first)(functools.partial(store, other, own, i * unit))
    if smalls:
        pl.when(is_first)(lambda: store_small(own, other))
        pl.when(~is_first)(lambda: store_small(other, own))


def finish(factor, base, width, unit, hid, channels, core, own, other, whole=()):
    vmem = pl.BlockSpec(memory_space=pltpu.VMEM)
    start = base // unit
    outs = [(hid, channels), (channels, hid)]
    smalls = [(7, 7, channels)] + [(channels,)] * 5 + [(hid,)] if whole else []

    def kernel(core, own, other, *refs):
        finish_kernel(factor, width, core, own, other, *refs[len(whole) :])

    return pl.pallas_call(
        kernel,
        grid=(width // unit,),
        out_shape=[jax.ShapeDtypeStruct(shape, f32) for shape in outs + smalls],
        in_specs=[pl.BlockSpec(memory_space=pltpu.SMEM), vmem, vmem]
        + [pl.BlockSpec(memory_space=pl.ANY)] * len(whole),
        out_specs=[
            pl.BlockSpec((unit, channels), lambda i: (start + i, 0)),
            pl.BlockSpec((channels, unit), lambda i: (0, start + i)),
        ]
        + [vmem] * len(smalls),
        input_output_aliases={3: 0, 4: 1} if whole else {},
        compiler_params=pltpu.CompilerParams(vmem_limit_bytes=24 << 20),
    )(core, own, other, *whole)


def shards(
    pages,
    cotangent,
    conv_kernel,
    conv_bias,
    norm_gain,
    norm_bias,
    w_in,
    b_in,
    w_out,
    b_out,
    layer_scale,
):
    _, rows, cols, channels = pages.shape
    hid = w_in.shape[0]
    pixels = rows * cols
    tile = pages.reshape(rows, cols, channels)
    page = pages.reshape(pixels, channels)
    cot = cotangent.reshape(pixels, channels)
    pad = ((channels // LANES, rows + 6, EDGE + cols + 8, LANES), f32)
    full = (pixels, channels)

    even_y = lax.axis_index("gy") % 2 == 0
    even_x = lax.axis_index("gx") % 2 == 0
    core = (lax.axis_index("gy") % 2).astype(jnp.int32).reshape(1)
    mine = (lax.axis_index("gy") // 2 % 2 + lax.axis_index("gx") % 2 * 2).astype(jnp.int32).reshape(1)
    even_y, even_x, core, mine, tile = hold((even_y, even_x, core, mine, tile))
    around = halo(tile, even_y, even_x)
    conv_flops = 2 * 49 * pixels * channels * 60
    normed, inv, ln_out = call(
        conv_norm_kernel,
        [(full, f32), ((pixels, LANES), f32), (full, bf16)],
        [pad, (full, f32)],
        (tile, *around, conv_kernel, conv_bias, norm_gain, norm_bias),
        conv_flops,
    )
    acts = lambda width: [((pixels, width), bf16)] * 2
    packed = lambda width: [((width * channels // LANES, LANES), bf16)] * 2 + [((1, width), f32)]
    core_flip = [("gy", 0)]
    mlp_flops = 12 * pixels * channels * hid
    weights = (w_in, w_out, b_in, layer_scale)
    first, second = hid * 2 // 3, hid // 3
    branch, d_norm, d_branch, keep_a, send_a, gbin_a = call(
        functools.partial(mlp_first_kernel, 0, first),
        [(full, f32), (full, f32), (full, bf16)] + packed(first),
        [
            ((MLP_BLOCK, first), bf16),
            ((MLP_BLOCK, first), bf16),
            ((first, channels), f32),
            ((channels, first), f32),
            ((8, first), f32),
        ],
        (core, ln_out, cot, *weights),
        mlp_flops,
        1,
    )
    other_a = exchange(send_a, core_flip)
    result, d_depth, keep_b, send_b, gbin_b, sums = call(
        functools.partial(mlp_second_kernel, first, second),
        [(full, bf16), (full, bf16)] + packed(second) + [((8, channels), f32)],
        acts(second) + [((8, 8, channels), f32)],
        (core, ln_out, cot, *weights, b_out, norm_gain, page, normed, inv, branch, d_norm, d_branch),
        mlp_flops,
        1,
    )
    d_tile = d_depth.reshape(tile.shape)
    other_a, d_tile, keep_b, send_b = hold((other_a, d_tile, keep_b, send_b))
    parts_a = add_halves(mine, keep_a, other_a)
    got_a = spread(parts_a)
    other_b = exchange(send_b, core_flip)
    d_around = halo(d_tile, even_y, even_x)
    small_rows = ((2 * SMALL, LANES), bf16)
    keep_s, send_s = call(
        kernel_grad_kernel,
        [small_rows, small_rows],
        [pad, (full, f32), ((channels // LANES, 49, 8, LANES), f32)],
        (core, tile, *around, d_tile.reshape(full), sums, gbin_a, gbin_b),
        conv_flops,
        1,
        (parts_a[1],),
    )
    got_a, keep_s, send_s, other_b = hold((got_a, keep_s, send_s, other_b))
    other_s = exchange(send_s, core_flip)
    part_a = add(*got_a)
    parts_b = add_halves(mine, keep_b, other_b, keep_s, other_s)
    flips = [[bit] for bit in beyond()]
    got_a, got_b = exchange(part_a, flips[0]), spread(parts_b)
    got_a, got_b = hold((got_a, got_b))
    part_a, part_b = add(part_a, got_a), add(*got_b)
    (grad_pages,) = call(
        conv_grad_kernel,
        [(full, bf16)],
        [pad, (full, f32)],
        (d_tile, *d_around, conv_kernel, cot),
        conv_flops,
        0,
        (part_a, part_b),
    )
    for ahead, behind in zip(flips[1:], flips):
        got_a, got_b, grad_pages = hold((exchange(part_a, ahead), exchange(part_b, behind), grad_pages))
        part_a, part_b = add(part_a, got_a), add(part_b, got_b)
    got_a, got_b = hold((spread([part_a] * 4), exchange(part_b, flips[-1])))
    half_a, part_b = join(mine, *got_a), add(part_b, got_b)
    got_a, got_b = hold(([half_a, exchange(half_a, core_flip)], spread([part_b] * 4)))
    half_b = join(mine, *got_b)
    got_b = [half_b, exchange(half_b, core_flip)]
    factor = float(pixels * lax.axis_size("gy") * lax.axis_size("gx") * lax.axis_size("rep")) ** (-0.5)
    begun = finish(factor, 0, first, second, hid, channels, core, *got_a)
    win, wout, gk, g_scale, g_bout, g_gain, g_shift, g_bias, g_bin = finish(
        factor, first, second, second, hid, channels, core, *got_b, begun
    )
    return (
        result.reshape(pages.shape),
        grad_pages.reshape(pages.shape),
        gk,
        g_bias,
        g_gain,
        g_shift,
        win,
        g_bin,
        wout,
        g_bout,
        g_scale,
    )


def solution(mesh):
    split = P("rep", "gy", "gx", None)
    return jax.shard_map(
        shards,
        mesh=mesh,
        in_specs=(split, split) + (P(),) * 9,
        out_specs=(split, split) + (P(),) * 9,
        check_vma=False,
    )
```

```python
import functools
import math

import jax
import jax.numpy as jnp
from jax import lax
from jax.experimental import pallas as pl
from jax.experimental.pallas import tpu as pltpu
from jax.sharding import PartitionSpec as P

norm_epsilon = 1e-06
inv_root_two = 0.7071067811865476
inv_root_tau = 0.3989422804014327

LANES = 128
EDGE = 8
BAND = 32
AXES = ("gy", "gx", "rep")
f32 = jnp.float32
bf16 = jnp.bfloat16


def dot(a, b, dims):
    return lax.dot_general(a, b, (dims, ((), ())), preferred_element_type=f32)


NN = ((1,), (0,))
NT = ((1,), (1,))
TN = ((0,), (0,))


def pair_rounds(count):
    first = [(i, i + 1) for i in range(0, count - 1, 2)]
    second = [(i, i + 1) for i in range(1, count - 1, 2)]
    return [pairs + [(b, a) for a, b in pairs] for pairs in (first, second)]


def halo(tile, even_y, even_x):
    rows, cols, _ = tile.shape

    def swap_edges(low, high, axis, even):
        got = []
        for pairs, is_high in zip(pair_rounds(lax.axis_size(axis)), (even, ~even)):
            if pairs:
                got.append(lax.ppermute(jnp.where(is_high, high, low), axis, pairs))
            else:
                got.append(jnp.zeros_like(low))
        return jnp.where(even, got[1], got[0]), jnp.where(even, got[0], got[1])

    top, bottom = swap_edges(tile[:3], tile[rows - 3 :], "gy", even_y)
    column = [
        jnp.concatenate([part[:, at : at + 3] for part in (top, tile, bottom)], axis=0) for at in (0, cols - 3)
    ]
    left, right = swap_edges(*column, "gx", even_x)
    return top, bottom, left, right


def fill(pad, tile, top, bottom, left, right):
    rows, cols, channels = tile.shape
    for slab in range(channels // LANES):
        at = slice(slab * LANES, (slab + 1) * LANES)
        pad[slab, 0:3, EDGE : EDGE + cols, :] = top[:, :, at].astype(f32)
        pad[slab, 3 + rows :, EDGE : EDGE + cols, :] = bottom[:, :, at].astype(f32)
        pad[slab, :, EDGE - 3 : EDGE, :] = left[:, :, at].astype(f32)
        pad[slab, :, EDGE + cols : EDGE + cols + 3, :] = right[:, :, at].astype(f32)

        def body(row, _):
            pad[slab, row + 3, EDGE : EDGE + cols, :] = tile[row, :, at].astype(f32)
            return _

        lax.fori_loop(0, rows, body, 0, unroll=4)


def steps(rows, cols, channels, body):
    slabs, tiles, bands = channels // LANES, cols // 8, rows // BAND

    def step(i, _):
        slab = i // (tiles * bands)
        rest = i % (tiles * bands)
        body(slab, pl.multiple_of(rest // bands * 8, 8), rest % bands * BAND)
        return _

    lax.fori_loop(0, slabs * tiles * bands, step, 0)


def lanes(slab):
    return pl.ds(pl.multiple_of(slab * LANES, LANES), LANES)


def taps(pad, kernel, slab, col, row, flip):
    acc = [None] * BAND
    for b in range(7):
        scale = []
        for a in range(7):
            i, j = (6 - a, 6 - b) if flip else (a, b)
            scale.append(jnp.broadcast_to(kernel[i, j : j + 1, lanes(slab)], (8, LANES)))
        for r in range(BAND + 6):
            x = pad[slab, row + r, pl.ds(col + EDGE - 3 + b, 8), :]
            for a in range(7):
                i = r - a
                if 0 <= i < BAND:
                    acc[i] = x * scale[a] if acc[i] is None else acc[i] + x * scale[a]
    return acc


def line(ref, at=slice(None)):
    return ref[at].reshape(1, -1)


def conv_norm_kernel(
    tile, top, bottom, left, right, kernel, bias, gain, shift, normed_ref, inv_ref, ln_ref, pad, depth
):
    rows, cols, channels = tile.shape
    fill(pad, tile, top, bottom, left, right)

    def piece(slab, col, row):
        acc = taps(pad, kernel, slab, col, row, False)
        add = jnp.broadcast_to(line(bias, lanes(slab)), (8, LANES))
        for i in range(BAND):
            at = pl.ds(pl.multiple_of((row + i) * cols + col, 8), 8)
            depth[at, lanes(slab)] = acc[i] + add

    steps(rows, cols, channels, piece)
    block = 128

    def norm(i, _):
        at = pl.ds(pl.multiple_of(i * block, block), block)
        x = depth[at, :]
        centred = x - jnp.mean(x, axis=-1, keepdims=True)
        inv = lax.rsqrt(jnp.mean(centred * centred, axis=-1, keepdims=True) + norm_epsilon)
        normed = centred * inv
        normed_ref[at, :] = normed
        inv_ref[at, :] = jnp.broadcast_to(inv, (block, LANES))
        ln_ref[at, :] = (normed * line(gain) + line(shift)).astype(bf16)
        return _

    lax.fori_loop(0, rows * cols // block, norm, 0)


def gelu_pair(u):
    cdf = 0.5 * (1.0 + lax.erf(u * inv_root_two))
    pdf = jnp.exp(-0.5 * u * u) * inv_root_tau
    return u * cdf, cdf + u * pdf


def fold(x):
    return jnp.sum(x.reshape(-1, 8, x.shape[1]), axis=0)


def mlp(core, ln_ref, d_branch, w_in, w_out, b_in, base, width, hid_ref, dpre_ref, keep, send, gbin_ref):
    sub = 256
    count = width // sub
    channels = ln_ref.shape[1]
    ln = ln_ref[...]

    def products(s):
        at = pl.ds(base + s * sub, sub)
        return dot(ln, w_in[at, :], NT), dot(d_branch[...], w_out[:, at], NN)

    ahead = products(0)
    for s in range(count):
        pre, d_hidden = ahead
        if s + 1 < count:
            ahead = products(s + 1)
        act, slope = gelu_pair(pre + line(b_in, pl.ds(base + s * sub, sub)))
        d_pre = d_hidden * slope
        at = slice(s * sub, (s + 1) * sub)
        gbin_ref[:, at] = jnp.sum(d_pre, axis=0, keepdims=True)
        hid_ref[:, at] = act.astype(bf16)
        dpre_ref[:, at] = d_pre.astype(bf16)

    def store(first, second):
        for s in range(count):
            at = slice(s * sub, (s + 1) * sub)
            gwin = dot(dpre_ref[:, at], ln_ref[...], TN).astype(bf16)
            for j in range(channels // LANES):
                start = j * width + s * sub
                first[start : start + sub, :] = gwin[:, j * LANES : (j + 1) * LANES]
            gwout = dot(d_branch[...], hid_ref[:, at], TN).astype(bf16)
            for j in range(sub // LANES):
                start = (s * sub // LANES + j) * channels
                second[start : start + channels, :] = gwout[:, j * LANES : (j + 1) * LANES]

    pl.when(core[0] == 0)(lambda: store(keep, send))
    pl.when(core[0] != 0)(lambda: store(send, keep))


PIXELS = 256


def mlp_block(ln, d_branch, w_in, w_out, b_in, base, width, hid_ref, dpre_ref, gbin):
    sub = 256
    count = width // sub

    def products(s):
        at = pl.ds(base + s * sub, sub)
        return dot(ln, w_in[at, :], NT), dot(d_branch, w_out[:, at], NN)

    ahead = products(0)
    for s in range(count):
        pre, d_hidden = ahead
        if s + 1 < count:
            ahead = products(s + 1)
        act, slope = gelu_pair(pre + line(b_in, pl.ds(base + s * sub, sub)))
        d_pre = d_hidden * slope
        gbin[:, s * sub : (s + 1) * sub] += fold(d_pre)
        hid_ref[:, s * sub : (s + 1) * sub] = act.astype(bf16)
        dpre_ref[:, s * sub : (s + 1) * sub] = d_pre.astype(bf16)
    at = pl.ds(base, width)
    hidden, d_pre = hid_ref[...], dpre_ref[...]
    branch = dot(hidden, w_out[:, at], NT)
    d_norm = dot(d_pre, w_in[at, :], NN)
    return hidden, d_pre, branch, d_norm


def pack_grads(core, keep, send, gwin, gwout, gbin_ref, gbin):
    width, channels = gwin.shape

    def store(first, second):
        for j in range(channels // LANES):
            first[j * width : (j + 1) * width, :] = gwin[:, j * LANES : (j + 1) * LANES].astype(bf16)
        for j in range(width // LANES):
            second[j * channels : (j + 1) * channels, :] = gwout[
                :, j * LANES : (j + 1) * LANES
            ].astype(bf16)

    pl.when(core[0] == 0)(lambda: store(keep, send))
    pl.when(core[0] != 0)(lambda: store(send, keep))
    gbin_ref[...] = jnp.sum(gbin[...], axis=0, keepdims=True)


MLP_BLOCK = 512


def mlp_first_kernel(
    base, width, core, ln_ref, cot, w_in, w_out, b_in, scale, branch_ref, dnorm_ref, d_branch_ref, keep, send, gbin_ref,
    hid_ref, dpre_ref, gwin, gwout, gbin,
):
    gwin[...] = jnp.zeros_like(gwin)
    gwout[...] = jnp.zeros_like(gwout)
    gbin[...] = jnp.zeros_like(gbin)

    def step(i, _):
        at = pl.ds(pl.multiple_of(i * MLP_BLOCK, MLP_BLOCK), MLP_BLOCK)
        ln = ln_ref[at, :]
        d_branch = (line(scale) * cot[at, :].astype(f32)).astype(bf16)
        hidden, d_pre, branch, d_norm = mlp_block(
            ln, d_branch, w_in, w_out, b_in, base, width, hid_ref, dpre_ref, gbin
        )
        d_branch_ref[at, :] = d_branch
        branch_ref[at, :] = branch
        dnorm_ref[at, :] = d_norm
        gwin[...] += dot(d_pre, ln, TN)
        gwout[...] += dot(d_branch, hidden, TN)
        return _

    lax.fori_loop(0, ln_ref.shape[0] // MLP_BLOCK, step, 0)
    pack_grads(core, keep, send, gwin, gwout, gbin_ref, gbin)


def mlp_second_kernel(
    base, width, core, ln_ref, cot, w_in, w_out, b_in, scale, b_out, gain, page, normed_ref, inv_ref,
    branch_ref, dnorm_ref, d_branch_ref,
    result, d_depth_ref, keep, send, gbin_ref, sums_ref,
    hid_ref, dpre_ref, sums,
):
    sums[...] = jnp.zeros_like(sums)
    mlp(core, ln_ref, d_branch_ref, w_in, w_out, b_in, base, width, hid_ref, dpre_ref, keep, send, gbin_ref)
    units = pl.ds(base, width)

    def step(i, _):
        at = pl.ds(pl.multiple_of(i * PIXELS, PIXELS), PIXELS)
        cot32 = cot[at, :].astype(f32)
        branch = dot(hid_ref[at, :], w_out[:, units], NT) + branch_ref[at, :] + line(b_out)
        result[at, :] = (page[at, :].astype(f32) + line(scale) * branch).astype(bf16)
        d_norm = dot(dpre_ref[at, :], w_in[units, :], NN) + dnorm_ref[at, :]
        normed = normed_ref[at, :]
        inv = inv_ref[at, 0:1]
        weighted = d_norm * normed
        s = d_norm * line(gain)
        mean_s = jnp.mean(s, axis=-1, keepdims=True)
        mean_sn = jnp.mean(s * normed, axis=-1, keepdims=True)
        d_depth = (inv * (s - mean_s - normed * mean_sn)).astype(bf16)
        d_depth_ref[at, :] = d_depth
        sums[0] += fold(cot32 * branch)
        sums[1] += fold(line(scale) * cot32)
        sums[2] += fold(weighted)
        sums[3] += fold(d_norm)
        sums[4] += fold(d_depth.astype(f32))
        return _

    lax.fori_loop(0, ln_ref.shape[0] // PIXELS, step, 0)
    for j in range(5):
        sums_ref[j : j + 1, :] = jnp.sum(sums[j], axis=0, keepdims=True)


SMALL = 64


def kernel_grad_kernel(
    core, tile, top, bottom, left, right, d_depth, sums, gbin_a, gbin_b, keep, send, pad, d32, acc_ref
):
    rows, cols, channels = tile.shape
    fill(pad, tile, top, bottom, left, right)
    d32[...] = d_depth[...].astype(f32)
    acc_ref[...] = jnp.zeros_like(acc_ref)

    def piece(slab, col, row):
        grads = []
        for i in range(BAND):
            at = pl.ds(pl.multiple_of((row + i) * cols + col, 8), 8)
            grads.append(d32[at, lanes(slab)])
        for b in range(7):
            acc = [None] * 7
            for r in range(BAND + 6):
                x = pad[slab, row + r, pl.ds(col + EDGE - 3 + b, 8), :]
                for a in range(7):
                    i = r - a
                    if 0 <= i < BAND:
                        acc[a] = x * grads[i] if acc[a] is None else acc[a] + x * grads[i]
            for a in range(7):
                acc_ref[slab, a * 7 + b] += acc[a]

    steps(rows, cols, channels, piece)

    def store(first, second):
        slabs, half = channels // LANES, SMALL // 2
        for slab in range(slabs):
            at = slice(slab * LANES, (slab + 1) * LANES)
            part = [jnp.sum(acc_ref[slab], axis=1), sums[:5, at]]
            for j in range((gbin_a.shape[1] + gbin_b.shape[1]) // channels):
                lane = (j * slabs + slab) * LANES
                source = gbin_a if lane < gbin_a.shape[1] else gbin_b
                lane = lane if lane < gbin_a.shape[1] else lane - gbin_a.shape[1]
                part.append(source[:, lane : lane + LANES])
            part = jnp.concatenate(part)
            part = jnp.concatenate([part, jnp.zeros((SMALL - part.shape[0], LANES), f32)])
            first[slab * half : (slab + 1) * half, :] = part[:half].astype(bf16)
            second[slab * half : (slab + 1) * half, :] = part[half:].astype(bf16)
        for ref in (first, second):
            ref[slabs * half :, :] = jnp.zeros((ref.shape[0] - slabs * half, LANES), bf16)

    pl.when(core[0] == 0)(lambda: store(keep, send))
    pl.when(core[0] != 0)(lambda: store(send, keep))


def conv_grad_kernel(tile, top, bottom, left, right, kernel, cot, out, pad, total):
    rows, cols, channels = tile.shape
    fill(pad, tile, top, bottom, left, right)

    def piece(slab, col, row):
        acc = taps(pad, kernel, slab, col, row, True)
        for i in range(BAND):
            at = pl.ds(pl.multiple_of((row + i) * cols + col, 8), 8)
            total[at, lanes(slab)] = acc[i]

    steps(rows, cols, channels, piece)
    block = 128

    def finish(i, _):
        at = pl.ds(pl.multiple_of(i * block, block), block)
        out[at, :] = (cot[at, :].astype(f32) + total[at, :]).astype(bf16)
        return _

    lax.fori_loop(0, rows * cols // block, finish, 0)


def call(body, outs, scratch, args, flops, scalars=0, after=(), size=24 << 20):
    held = len(args)

    def kernel(*refs):
        body(*refs[:held], *refs[held + len(after) :])

    vmem = pl.BlockSpec(memory_space=pltpu.VMEM)
    smem = pl.BlockSpec(memory_space=pltpu.SMEM)
    return pl.pallas_call(
        kernel,
        out_shape=[jax.ShapeDtypeStruct(shape, dtype) for shape, dtype in outs],
        in_specs=[smem] * scalars
        + [vmem] * (held - scalars)
        + [pl.BlockSpec(memory_space=pl.ANY)] * len(after),
        out_specs=[vmem] * len(outs),
        scratch_shapes=[pltpu.VMEM(shape, dtype) for shape, dtype in scratch],
        compiler_params=pltpu.CompilerParams(vmem_limit_bytes=size),
        cost_estimate=pl.CostEstimate(flops=flops, bytes_accessed=flops >> 10, transcendentals=0),
    )(*args, *after)


def bits(axis):
    return [(axis, j) for j in range(max(lax.axis_size(axis).bit_length() - 1, 0))]


def plane():
    return [("gy", 1), ("gx", 0)]


def beyond():
    return bits("gy")[2:] + bits("gx")[1:] + bits("rep")


def exchange(x, flips):
    sizes = [lax.axis_size(axis) for axis in AXES]
    perm = []
    for i in range(math.prod(sizes)):
        at = {"gy": i // (sizes[1] * sizes[2]), "gx": i // sizes[2] % sizes[1], "rep": i % sizes[2]}
        for axis, bit in flips:
            at[axis] ^= 1 << bit
        perm.append((i, (at["gy"] * sizes[1] + at["gx"]) * sizes[2] + at["rep"]))
    return lax.ppermute(x, AXES, perm)


def spread(parts):
    flips = [[g for j, g in enumerate(plane()) if delta >> j & 1] for delta in range(1, 4)]
    return [parts[0]] + [exchange(x, flip) for x, flip in zip(parts[1:], flips)]


def hold(arrays):
    return lax.optimization_barrier(arrays)


def chunks(rows, body):
    size = max(n for n in (128, 64, 32, 16) if rows % n == 0)

    def step(i, _):
        body(pl.multiple_of(i * size, size), size)
        return _

    lax.fori_loop(0, rows // size, step, 0, unroll=2 if rows // size > 1 else 1)


def first_sum_kernel(has_small, mine, *refs):
    wide, outs = refs[:2], refs[4 if has_small else 2 :]
    rows = wide[0].shape[0] // len(outs)
    for delta, out in enumerate(outs):
        to = mine[0] ^ delta

        def add(at, size):
            part = pl.ds(pl.multiple_of(to * rows + at, 16), size)
            out[pl.ds(at, size), :] = (wide[0][part, :].astype(f32) + wide[1][part, :].astype(f32)).astype(bf16)

        chunks(rows, add)
        end = rows
        if has_small:
            small = refs[2:4]
            size = small[0].shape[0] // len(outs)
            part = pl.ds(pl.multiple_of(to * size, 16), size)
            out[end : end + size, :] = (small[0][part, :].astype(f32) + small[1][part, :].astype(f32)).astype(bf16)
            end += size
        if end < out.shape[0]:
            out[end:, :] = jnp.zeros((out.shape[0] - end, LANES), bf16)


def sum_kernel(*refs):
    ins, out = refs[:-1], refs[-1]

    def add(at, size):
        part = pl.ds(at, size)
        out[part, :] = sum(r[part, :].astype(f32) for r in ins).astype(bf16)

    chunks(out.shape[0], add)


def join_kernel(mine, *refs):
    out = refs[-1]
    rows = refs[0].shape[0]
    for delta, ref in enumerate(refs[:-1]):
        out[pl.ds(pl.multiple_of((mine[0] ^ delta) * rows, 16), rows), :] = ref[...]


SUM_FLOPS = 1 << 20


def add_halves(mine, keep, other, *small):
    rows = (keep.shape[0] + (small[0].shape[0] if small else 0)) // 4
    return call(
        functools.partial(first_sum_kernel, bool(small)),
        [((rows, LANES), bf16)] * 4,
        [],
        (mine, keep, other, *small),
        SUM_FLOPS,
        1,
    )


def add(*arrays):
    (x,) = call(sum_kernel, [(arrays[0].shape, bf16)], [], arrays, SUM_FLOPS)
    return x


def join(mine, *parts):
    (x,) = call(join_kernel, [((4 * parts[0].shape[0], LANES), bf16)], [], (mine, *parts), SUM_FLOPS, 1)
    return x


def finish_kernel(factor, width, core, own, other, win, wout, *smalls):
    channels, unit = wout.shape
    slabs = channels // LANES

    def rows(ref, at):
        part, block = ref.shape[0] // 4, width * slabs // 4
        start = at // block * part + at % block
        return ref[start : start + LANES, :].astype(f32) * factor

    def store(first, second, offset):
        for j in range(slabs):
            for i in range(0, unit, LANES):
                win[i : i + LANES, j * LANES : (j + 1) * LANES] = rows(first, j * width + offset + i)
        for j in range(unit // LANES):
            for i in range(0, channels, LANES):
                wout[i : i + LANES, j * LANES : (j + 1) * LANES] = rows(
                    second, (offset // LANES + j) * channels + i
                )

    def store_small(*halves):
        gk, scale, b_out, gain, shift, bias, b_in = smalls
        for slab in range(slabs):
            at = slice(slab * LANES, (slab + 1) * LANES)
            start = slab * (halves[0].shape[0] // 4) + width * slabs // 4
            values = jnp.concatenate([ref[start : start + SMALL // 2, :].astype(f32) for ref in halves]) * factor
            for j in range(7):
                gk[j, :, at] = values[7 * j : 7 * j + 7]
            for j, ref in enumerate((scale, b_out, gain, shift, bias)):
                ref[at] = values[49 + j]
            for j in range(b_in.shape[0] // channels):
                lane = (j * slabs + slab) * LANES
                b_in[lane : lane + LANES] = values[54 + j]

    is_first = core[0] == 0
    step = pl.program_id(0)
    for i in range(width // unit):
        here = step == i
        pl.when(here & is_first)(functools.partial(store, own, other, i * unit))
        pl.when(here & ~is_first)(functools.partial(store, other, own, i * unit))
    if smalls:
        pl.when(is_first)(lambda: store_small(own, other))
        pl.when(~is_first)(lambda: store_small(other, own))


def finish(factor, base, width, unit, hid, channels, core, own, other, whole=()):
    vmem = pl.BlockSpec(memory_space=pltpu.VMEM)
    start = base // unit
    outs = [(hid, channels), (channels, hid)]
    smalls = [(7, 7, channels)] + [(channels,)] * 5 + [(hid,)] if whole else []

    def kernel(core, own, other, *refs):
        finish_kernel(factor, width, core, own, other, *refs[len(whole) :])

    return pl.pallas_call(
        kernel,
        grid=(width // unit,),
        out_shape=[jax.ShapeDtypeStruct(shape, f32) for shape in outs + smalls],
        in_specs=[pl.BlockSpec(memory_space=pltpu.SMEM), vmem, vmem]
        + [pl.BlockSpec(memory_space=pl.ANY)] * len(whole),
        out_specs=[
            pl.BlockSpec((unit, channels), lambda i: (start + i, 0)),
            pl.BlockSpec((channels, unit), lambda i: (0, start + i)),
        ]
        + [vmem] * len(smalls),
        input_output_aliases={3: 0, 4: 1} if whole else {},
        compiler_params=pltpu.CompilerParams(vmem_limit_bytes=24 << 20),
    )(core, own, other, *whole)


def shards(
    pages,
    cotangent,
    conv_kernel,
    conv_bias,
    norm_gain,
    norm_bias,
    w_in,
    b_in,
    w_out,
    b_out,
    layer_scale,
):
    _, rows, cols, channels = pages.shape
    hid = w_in.shape[0]
    pixels = rows * cols
    tile = pages.reshape(rows, cols, channels)
    page = pages.reshape(pixels, channels)
    cot = cotangent.reshape(pixels, channels)
    pad = ((channels // LANES, rows + 6, EDGE + cols + 8, LANES), f32)
    full = (pixels, channels)

    even_y = lax.axis_index("gy") % 2 == 0
    even_x = lax.axis_index("gx") % 2 == 0
    core = (lax.axis_index("gy") % 2).astype(jnp.int32).reshape(1)
    mine = (lax.axis_index("gy") // 2 % 2 + lax.axis_index("gx") % 2 * 2).astype(jnp.int32).reshape(1)
    even_y, even_x, core, mine, tile = hold((even_y, even_x, core, mine, tile))
    around = halo(tile, even_y, even_x)
    conv_flops = 2 * 49 * pixels * channels * 60
    normed, inv, ln_out = call(
        conv_norm_kernel,
        [(full, f32), ((pixels, LANES), f32), (full, bf16)],
        [pad, (full, f32)],
        (tile, *around, conv_kernel, conv_bias, norm_gain, norm_bias),
        conv_flops,
    )
    acts = lambda width: [((pixels, width), bf16)] * 2
    packed = lambda width: [((width * channels // LANES, LANES), bf16)] * 2 + [((1, width), f32)]
    core_flip = [("gy", 0)]
    mlp_flops = 12 * pixels * channels * hid
    weights = (w_in, w_out, b_in, layer_scale)
    first, second = hid * 2 // 3, hid // 3
    branch, d_norm, d_branch, keep_a, send_a, gbin_a = call(
        functools.partial(mlp_first_kernel, 0, first),
        [(full, f32), (full, f32), (full, bf16)] + packed(first),
        [
            ((MLP_BLOCK, first), bf16),
            ((MLP_BLOCK, first), bf16),
            ((first, channels), f32),
            ((channels, first), f32),
            ((8, first), f32),
        ],
        (core, ln_out, cot, *weights),
        mlp_flops,
        1,
    )
    other_a = exchange(send_a, core_flip)
    result, d_depth, keep_b, send_b, gbin_b, sums = call(
        functools.partial(mlp_second_kernel, first, second),
        [(full, bf16), (full, bf16)] + packed(second) + [((8, channels), f32)],
        acts(second) + [((8, 8, channels), f32)],
        (core, ln_out, cot, *weights, b_out, norm_gain, page, normed, inv, branch, d_norm, d_branch),
        mlp_flops,
        1,
    )
    d_tile = d_depth.reshape(tile.shape)
    other_a, d_tile, keep_b, send_b = hold((other_a, d_tile, keep_b, send_b))
    parts_a = add_halves(mine, keep_a, other_a)
    got_a = spread(parts_a)
    other_b = exchange(send_b, core_flip)
    d_around = halo(d_tile, even_y, even_x)
    small_rows = ((2 * SMALL, LANES), bf16)
    keep_s, send_s = call(
        kernel_grad_kernel,
        [small_rows, small_rows],
        [pad, (full, f32), ((channels // LANES, 49, 8, LANES), f32)],
        (core, tile, *around, d_tile.reshape(full), sums, gbin_a, gbin_b),
        conv_flops,
        1,
        (parts_a[1],),
    )
    got_a, keep_s, send_s, other_b = hold((got_a, keep_s, send_s, other_b))
    other_s = exchange(send_s, core_flip)
    part_a = add(*got_a)
    parts_b = add_halves(mine, keep_b, other_b, keep_s, other_s)
    flips = [[bit] for bit in beyond()]
    got_a, got_b = exchange(part_a, flips[0]), spread(parts_b)
    got_a, got_b = hold((got_a, got_b))
    part_a, part_b = add(part_a, got_a), add(*got_b)
    (grad_pages,) = call(
        conv_grad_kernel,
        [(full, bf16)],
        [pad, (full, f32)],
        (d_tile, *d_around, conv_kernel, cot),
        conv_flops,
        0,
        (part_a, part_b),
    )
    for ahead, behind in zip(flips[1:], flips):
        got_a, got_b, grad_pages = hold((exchange(part_a, ahead), exchange(part_b, behind), grad_pages))
        part_a, part_b = add(part_a, got_a), add(part_b, got_b)
    got_a, got_b = hold((spread([part_a] * 4), exchange(part_b, flips[-1])))
    half_a, part_b = join(mine, *got_a), add(part_b, got_b)
    got_a, got_b = hold(([half_a, exchange(half_a, core_flip)], spread([part_b] * 4)))
    half_b = join(mine, *got_b)
    got_b = [half_b, exchange(half_b, core_flip)]
    factor = float(pixels * lax.axis_size("gy") * lax.axis_size("gx") * lax.axis_size("rep")) ** (-0.5)
    begun = finish(factor, 0, first, second, hid, channels, core, *got_a)
    win, wout, gk, g_scale, g_bout, g_gain, g_shift, g_bias, g_bin = finish(
        factor, first, second, second, hid, channels, core, *got_b, begun
    )
    return (
        result.reshape(pages.shape),
        grad_pages.reshape(pages.shape),
        gk,
        g_bias,
        g_gain,
        g_shift,
        win,
        g_bin,
        wout,
        g_bout,
        g_scale,
    )


def solution(mesh):
    split = P("rep", "gy", "gx", None)
    return jax.shard_map(
        shards,
        mesh=mesh,
        in_specs=(split, split) + (P(),) * 9,
        out_specs=(split, split) + (P(),) * 9,
        check_vma=False,
    )
```

```python
import functools
import math

import jax
import jax.numpy as jnp
from jax import lax
from jax.experimental import pallas as pl
from jax.experimental.pallas import tpu as pltpu
from jax.sharding import PartitionSpec as P

norm_epsilon = 1e-06
inv_root_two = 0.7071067811865476
inv_root_tau = 0.3989422804014327

LANES = 128
EDGE = 8
BAND = 32
AXES = ("gy", "gx", "rep")
f32 = jnp.float32
bf16 = jnp.bfloat16


def dot(a, b, dims):
    return lax.dot_general(a, b, (dims, ((), ())), preferred_element_type=f32)


NN = ((1,), (0,))
NT = ((1,), (1,))
TN = ((0,), (0,))


def pair_rounds(count):
    first = [(i, i + 1) for i in range(0, count - 1, 2)]
    second = [(i, i + 1) for i in range(1, count - 1, 2)]
    return [pairs + [(b, a) for a, b in pairs] for pairs in (first, second)]


def halo(tile, even_y, even_x):
    rows, cols, _ = tile.shape

    def swap_edges(low, high, axis, even):
        got = []
        for pairs, is_high in zip(pair_rounds(lax.axis_size(axis)), (even, ~even)):
            if pairs:
                got.append(lax.ppermute(jnp.where(is_high, high, low), axis, pairs))
            else:
                got.append(jnp.zeros_like(low))
        return jnp.where(even, got[1], got[0]), jnp.where(even, got[0], got[1])

    top, bottom = swap_edges(tile[:3], tile[rows - 3 :], "gy", even_y)
    column = [
        jnp.concatenate([part[:, at : at + 3] for part in (top, tile, bottom)], axis=0) for at in (0, cols - 3)
    ]
    left, right = swap_edges(*column, "gx", even_x)
    return top, bottom, left, right


def fill(pad, tile, top, bottom, left, right):
    rows, cols, channels = tile.shape
    for slab in range(channels // LANES):
        at = slice(slab * LANES, (slab + 1) * LANES)
        pad[slab, 0:3, EDGE : EDGE + cols, :] = top[:, :, at].astype(f32)
        pad[slab, 3 + rows :, EDGE : EDGE + cols, :] = bottom[:, :, at].astype(f32)
        pad[slab, :, EDGE - 3 : EDGE, :] = left[:, :, at].astype(f32)
        pad[slab, :, EDGE + cols : EDGE + cols + 3, :] = right[:, :, at].astype(f32)

        def body(row, _):
            pad[slab, row + 3, EDGE : EDGE + cols, :] = tile[row, :, at].astype(f32)
            return _

        lax.fori_loop(0, rows, body, 0, unroll=4)


def steps(rows, cols, channels, body):
    slabs, tiles, bands = channels // LANES, cols // 8, rows // BAND

    def step(i, _):
        slab = i // (tiles * bands)
        rest = i % (tiles * bands)
        body(slab, pl.multiple_of(rest // bands * 8, 8), rest % bands * BAND)
        return _

    lax.fori_loop(0, slabs * tiles * bands, step, 0)


def lanes(slab):
    return pl.ds(pl.multiple_of(slab * LANES, LANES), LANES)


def taps(pad, kernel, slab, col, row, flip):
    acc = [None] * BAND
    for b in range(7):
        scale = []
        for a in range(7):
            i, j = (6 - a, 6 - b) if flip else (a, b)
            scale.append(jnp.broadcast_to(kernel[i, j : j + 1, lanes(slab)], (8, LANES)))
        for r in range(BAND + 6):
            x = pad[slab, row + r, pl.ds(col + EDGE - 3 + b, 8), :]
            for a in range(7):
                i = r - a
                if 0 <= i < BAND:
                    acc[i] = x * scale[a] if acc[i] is None else acc[i] + x * scale[a]
    return acc


def line(ref, at=slice(None)):
    return ref[at].reshape(1, -1)


def conv_norm_kernel(
    tile, top, bottom, left, right, kernel, bias, gain, shift, normed_ref, inv_ref, ln_ref, pad, depth
):
    rows, cols, channels = tile.shape
    fill(pad, tile, top, bottom, left, right)

    def piece(slab, col, row):
        acc = taps(pad, kernel, slab, col, row, False)
        add = jnp.broadcast_to(line(bias, lanes(slab)), (8, LANES))
        for i in range(BAND):
            at = pl.ds(pl.multiple_of((row + i) * cols + col, 8), 8)
            depth[at, lanes(slab)] = acc[i] + add

    steps(rows, cols, channels, piece)
    block = 128

    def norm(i, _):
        at = pl.ds(pl.multiple_of(i * block, block), block)
        x = depth[at, :]
        centred = x - jnp.mean(x, axis=-1, keepdims=True)
        inv = lax.rsqrt(jnp.mean(centred * centred, axis=-1, keepdims=True) + norm_epsilon)
        normed = centred * inv
        normed_ref[at, :] = normed
        inv_ref[at, :] = jnp.broadcast_to(inv, (block, LANES))
        ln_ref[at, :] = (normed * line(gain) + line(shift)).astype(bf16)
        return _

    lax.fori_loop(0, rows * cols // block, norm, 0)


def gelu_pair(u):
    cdf = 0.5 * (1.0 + lax.erf(u * inv_root_two))
    pdf = jnp.exp(-0.5 * u * u) * inv_root_tau
    return u * cdf, cdf + u * pdf


def fold(x):
    return jnp.sum(x.reshape(-1, 8, x.shape[1]), axis=0)


def mlp(core, ln_ref, d_branch, w_in, w_out, b_in, base, width, hid_ref, dpre_ref, keep, send, gbin_ref):
    sub = 256
    count = width // sub
    channels = ln_ref.shape[1]
    ln = ln_ref[...]

    def products(s):
        at = pl.ds(base + s * sub, sub)
        return dot(ln, w_in[at, :], NT), dot(d_branch[...], w_out[:, at], NN)

    ahead = products(0)
    for s in range(count):
        pre, d_hidden = ahead
        if s + 1 < count:
            ahead = products(s + 1)
        act, slope = gelu_pair(pre + line(b_in, pl.ds(base + s * sub, sub)))
        d_pre = d_hidden * slope
        at = slice(s * sub, (s + 1) * sub)
        gbin_ref[:, at] = jnp.sum(d_pre, axis=0, keepdims=True)
        hid_ref[:, at] = act.astype(bf16)
        dpre_ref[:, at] = d_pre.astype(bf16)

    def store(first, second):
        for s in range(count):
            at = slice(s * sub, (s + 1) * sub)
            gwin = dot(dpre_ref[:, at], ln_ref[...], TN).astype(bf16)
            for j in range(channels // LANES):
                start = j * width + s * sub
                first[start : start + sub, :] = gwin[:, j * LANES : (j + 1) * LANES]
            gwout = dot(d_branch[...], hid_ref[:, at], TN).astype(bf16)
            for j in range(sub // LANES):
                start = (s * sub // LANES + j) * channels
                second[start : start + channels, :] = gwout[:, j * LANES : (j + 1) * LANES]

    pl.when(core[0] == 0)(lambda: store(keep, send))
    pl.when(core[0] != 0)(lambda: store(send, keep))


PIXELS = 512


def mlp_block(ln, d_branch, w_in, w_out, b_in, base, width, hid_ref, dpre_ref, gbin):
    sub = 256
    count = width // sub

    def products(s):
        at = pl.ds(base + s * sub, sub)
        return dot(ln, w_in[at, :], NT), dot(d_branch, w_out[:, at], NN)

    ahead = products(0)
    for s in range(count):
        pre, d_hidden = ahead
        if s + 1 < count:
            ahead = products(s + 1)
        act, slope = gelu_pair(pre + line(b_in, pl.ds(base + s * sub, sub)))
        d_pre = d_hidden * slope
        gbin[:, s * sub : (s + 1) * sub] += fold(d_pre)
        hid_ref[:, s * sub : (s + 1) * sub] = act.astype(bf16)
        dpre_ref[:, s * sub : (s + 1) * sub] = d_pre.astype(bf16)
    at = pl.ds(base, width)
    hidden, d_pre = hid_ref[...], dpre_ref[...]
    branch = dot(hidden, w_out[:, at], NT)
    d_norm = dot(d_pre, w_in[at, :], NN)
    return hidden, d_pre, branch, d_norm


def pack_grads(core, keep, send, gwin, gwout, gbin_ref, gbin):
    width, channels = gwin.shape

    def store(first, second):
        for j in range(channels // LANES):
            first[j * width : (j + 1) * width, :] = gwin[:, j * LANES : (j + 1) * LANES].astype(bf16)
        for j in range(width // LANES):
            second[j * channels : (j + 1) * channels, :] = gwout[
                :, j * LANES : (j + 1) * LANES
            ].astype(bf16)

    pl.when(core[0] == 0)(lambda: store(keep, send))
    pl.when(core[0] != 0)(lambda: store(send, keep))
    gbin_ref[...] = jnp.sum(gbin[...], axis=0, keepdims=True)


MLP_BLOCK = 512


def mlp_first_kernel(
    base, width, core, ln_ref, cot, w_in, w_out, b_in, scale, branch_ref, dnorm_ref, d_branch_ref, keep, send, gbin_ref,
    hid_ref, dpre_ref, gwin, gwout, gbin,
):
    gwin[...] = jnp.zeros_like(gwin)
    gwout[...] = jnp.zeros_like(gwout)
    gbin[...] = jnp.zeros_like(gbin)

    def step(i, _):
        at = pl.ds(pl.multiple_of(i * MLP_BLOCK, MLP_BLOCK), MLP_BLOCK)
        ln = ln_ref[at, :]
        d_branch = (line(scale) * cot[at, :].astype(f32)).astype(bf16)
        hidden, d_pre, branch, d_norm = mlp_block(
            ln, d_branch, w_in, w_out, b_in, base, width, hid_ref, dpre_ref, gbin
        )
        d_branch_ref[at, :] = d_branch
        branch_ref[at, :] = branch
        dnorm_ref[at, :] = d_norm
        gwin[...] += dot(d_pre, ln, TN)
        gwout[...] += dot(d_branch, hidden, TN)
        return _

    lax.fori_loop(0, ln_ref.shape[0] // MLP_BLOCK, step, 0)
    pack_grads(core, keep, send, gwin, gwout, gbin_ref, gbin)


def mlp_second_kernel(
    base, width, core, ln_ref, cot, w_in, w_out, b_in, scale, b_out, gain, page, normed_ref, inv_ref,
    branch_ref, dnorm_ref, d_branch_ref,
    result, d_depth_ref, keep, send, gbin_ref, sums_ref,
    hid_ref, dpre_ref, sums,
):
    sums[...] = jnp.zeros_like(sums)
    mlp(core, ln_ref, d_branch_ref, w_in, w_out, b_in, base, width, hid_ref, dpre_ref, keep, send, gbin_ref)
    units = pl.ds(base, width)

    def step(i, _):
        at = pl.ds(pl.multiple_of(i * PIXELS, PIXELS), PIXELS)
        cot32 = cot[at, :].astype(f32)
        branch = dot(hid_ref[at, :], w_out[:, units], NT) + branch_ref[at, :] + line(b_out)
        result[at, :] = (page[at, :].astype(f32) + line(scale) * branch).astype(bf16)
        d_norm = dot(dpre_ref[at, :], w_in[units, :], NN) + dnorm_ref[at, :]
        normed = normed_ref[at, :]
        inv = inv_ref[at, 0:1]
        weighted = d_norm * normed
        s = d_norm * line(gain)
        mean_s = jnp.mean(s, axis=-1, keepdims=True)
        mean_sn = jnp.mean(s * normed, axis=-1, keepdims=True)
        d_depth = (inv * (s - mean_s - normed * mean_sn)).astype(bf16)
        d_depth_ref[at, :] = d_depth
        sums[0] += fold(cot32 * branch)
        sums[1] += fold(line(scale) * cot32)
        sums[2] += fold(weighted)
        sums[3] += fold(d_norm)
        sums[4] += fold(d_depth.astype(f32))
        return _

    lax.fori_loop(0, ln_ref.shape[0] // PIXELS, step, 0)
    for j in range(5):
        sums_ref[j : j + 1, :] = jnp.sum(sums[j], axis=0, keepdims=True)


SMALL = 64


def kernel_grad_kernel(
    core, tile, top, bottom, left, right, d_depth, sums, gbin_a, gbin_b, keep, send, pad, d32, acc_ref
):
    rows, cols, channels = tile.shape
    fill(pad, tile, top, bottom, left, right)
    d32[...] = d_depth[...].astype(f32)
    acc_ref[...] = jnp.zeros_like(acc_ref)

    def piece(slab, col, row):
        grads = []
        for i in range(BAND):
            at = pl.ds(pl.multiple_of((row + i) * cols + col, 8), 8)
            grads.append(d32[at, lanes(slab)])
        for b in range(7):
            acc = [None] * 7
            for r in range(BAND + 6):
                x = pad[slab, row + r, pl.ds(col + EDGE - 3 + b, 8), :]
                for a in range(7):
                    i = r - a
                    if 0 <= i < BAND:
                        acc[a] = x * grads[i] if acc[a] is None else acc[a] + x * grads[i]
            for a in range(7):
                acc_ref[slab, a * 7 + b] += acc[a]

    steps(rows, cols, channels, piece)

    def store(first, second):
        slabs, half = channels // LANES, SMALL // 2
        for slab in range(slabs):
            at = slice(slab * LANES, (slab + 1) * LANES)
            part = [jnp.sum(acc_ref[slab], axis=1), sums[:5, at]]
            for j in range((gbin_a.shape[1] + gbin_b.shape[1]) // channels):
                lane = (j * slabs + slab) * LANES
                source = gbin_a if lane < gbin_a.shape[1] else gbin_b
                lane = lane if lane < gbin_a.shape[1] else lane - gbin_a.shape[1]
                part.append(source[:, lane : lane + LANES])
            part = jnp.concatenate(part)
            part = jnp.concatenate([part, jnp.zeros((SMALL - part.shape[0], LANES), f32)])
            first[slab * half : (slab + 1) * half, :] = part[:half].astype(bf16)
            second[slab * half : (slab + 1) * half, :] = part[half:].astype(bf16)
        for ref in (first, second):
            ref[slabs * half :, :] = jnp.zeros((ref.shape[0] - slabs * half, LANES), bf16)

    pl.when(core[0] == 0)(lambda: store(keep, send))
    pl.when(core[0] != 0)(lambda: store(send, keep))


def conv_grad_kernel(tile, top, bottom, left, right, kernel, cot, out, pad, total):
    rows, cols, channels = tile.shape
    fill(pad, tile, top, bottom, left, right)

    def piece(slab, col, row):
        acc = taps(pad, kernel, slab, col, row, True)
        for i in range(BAND):
            at = pl.ds(pl.multiple_of((row + i) * cols + col, 8), 8)
            total[at, lanes(slab)] = acc[i]

    steps(rows, cols, channels, piece)
    block = 128

    def finish(i, _):
        at = pl.ds(pl.multiple_of(i * block, block), block)
        out[at, :] = (cot[at, :].astype(f32) + total[at, :]).astype(bf16)
        return _

    lax.fori_loop(0, rows * cols // block, finish, 0)


def call(body, outs, scratch, args, flops, scalars=0, after=(), size=24 << 20):
    held = len(args)

    def kernel(*refs):
        body(*refs[:held], *refs[held + len(after) :])

    vmem = pl.BlockSpec(memory_space=pltpu.VMEM)
    smem = pl.BlockSpec(memory_space=pltpu.SMEM)
    return pl.pallas_call(
        kernel,
        out_shape=[jax.ShapeDtypeStruct(shape, dtype) for shape, dtype in outs],
        in_specs=[smem] * scalars
        + [vmem] * (held - scalars)
        + [pl.BlockSpec(memory_space=pl.ANY)] * len(after),
        out_specs=[vmem] * len(outs),
        scratch_shapes=[pltpu.VMEM(shape, dtype) for shape, dtype in scratch],
        compiler_params=pltpu.CompilerParams(vmem_limit_bytes=size),
        cost_estimate=pl.CostEstimate(flops=flops, bytes_accessed=flops >> 10, transcendentals=0),
    )(*args, *after)


def bits(axis):
    return [(axis, j) for j in range(max(lax.axis_size(axis).bit_length() - 1, 0))]


def plane():
    return [("gy", 1), ("gx", 0)]


def beyond():
    return bits("gy")[2:] + bits("gx")[1:] + bits("rep")


def exchange(x, flips):
    sizes = [lax.axis_size(axis) for axis in AXES]
    perm = []
    for i in range(math.prod(sizes)):
        at = {"gy": i // (sizes[1] * sizes[2]), "gx": i // sizes[2] % sizes[1], "rep": i % sizes[2]}
        for axis, bit in flips:
            at[axis] ^= 1 << bit
        perm.append((i, (at["gy"] * sizes[1] + at["gx"]) * sizes[2] + at["rep"]))
    return lax.ppermute(x, AXES, perm)


def spread(parts):
    flips = [[g for j, g in enumerate(plane()) if delta >> j & 1] for delta in range(1, 4)]
    return [parts[0]] + [exchange(x, flip) for x, flip in zip(parts[1:], flips)]


def hold(arrays):
    return lax.optimization_barrier(arrays)


def chunks(rows, body):
    size = max(n for n in (128, 64, 32, 16) if rows % n == 0)

    def step(i, _):
        body(pl.multiple_of(i * size, size), size)
        return _

    lax.fori_loop(0, rows // size, step, 0, unroll=2 if rows // size > 1 else 1)


def first_sum_kernel(has_small, mine, *refs):
    wide, outs = refs[:2], refs[4 if has_small else 2 :]
    rows = wide[0].shape[0] // len(outs)
    for delta, out in enumerate(outs):
        to = mine[0] ^ delta

        def add(at, size):
            part = pl.ds(pl.multiple_of(to * rows + at, 16), size)
            out[pl.ds(at, size), :] = (wide[0][part, :].astype(f32) + wide[1][part, :].astype(f32)).astype(bf16)

        chunks(rows, add)
        end = rows
        if has_small:
            small = refs[2:4]
            size = small[0].shape[0] // len(outs)
            part = pl.ds(pl.multiple_of(to * size, 16), size)
            out[end : end + size, :] = (small[0][part, :].astype(f32) + small[1][part, :].astype(f32)).astype(bf16)
            end += size
        if end < out.shape[0]:
            out[end:, :] = jnp.zeros((out.shape[0] - end, LANES), bf16)


def sum_kernel(*refs):
    ins, out = refs[:-1], refs[-1]

    def add(at, size):
        part = pl.ds(at, size)
        out[part, :] = sum(r[part, :].astype(f32) for r in ins).astype(bf16)

    chunks(out.shape[0], add)


def join_kernel(mine, *refs):
    out = refs[-1]
    rows = refs[0].shape[0]
    for delta, ref in enumerate(refs[:-1]):
        out[pl.ds(pl.multiple_of((mine[0] ^ delta) * rows, 16), rows), :] = ref[...]


SUM_FLOPS = 1 << 20


def add_halves(mine, keep, other, *small):
    rows = (keep.shape[0] + (small[0].shape[0] if small else 0)) // 4
    return call(
        functools.partial(first_sum_kernel, bool(small)),
        [((rows, LANES), bf16)] * 4,
        [],
        (mine, keep, other, *small),
        SUM_FLOPS,
        1,
    )


def add(*arrays):
    (x,) = call(sum_kernel, [(arrays[0].shape, bf16)], [], arrays, SUM_FLOPS)
    return x


def join(mine, *parts):
    (x,) = call(join_kernel, [((4 * parts[0].shape[0], LANES), bf16)], [], (mine, *parts), SUM_FLOPS, 1)
    return x


def finish_kernel(factor, width, core, own, other, win, wout, *smalls):
    channels, unit = wout.shape
    slabs = channels // LANES

    def rows(ref, at):
        part, block = ref.shape[0] // 4, width * slabs // 4
        start = at // block * part + at % block
        return ref[start : start + LANES, :].astype(f32) * factor

    def store(first, second, offset):
        for j in range(slabs):
            for i in range(0, unit, LANES):
                win[i : i + LANES, j * LANES : (j + 1) * LANES] = rows(first, j * width + offset + i)
        for j in range(unit // LANES):
            for i in range(0, channels, LANES):
                wout[i : i + LANES, j * LANES : (j + 1) * LANES] = rows(
                    second, (offset // LANES + j) * channels + i
                )

    def store_small(*halves):
        gk, scale, b_out, gain, shift, bias, b_in = smalls
        for slab in range(slabs):
            at = slice(slab * LANES, (slab + 1) * LANES)
            start = slab * (halves[0].shape[0] // 4) + width * slabs // 4
            values = jnp.concatenate([ref[start : start + SMALL // 2, :].astype(f32) for ref in halves]) * factor
            for j in range(7):
                gk[j, :, at] = values[7 * j : 7 * j + 7]
            for j, ref in enumerate((scale, b_out, gain, shift, bias)):
                ref[at] = values[49 + j]
            for j in range(b_in.shape[0] // channels):
                lane = (j * slabs + slab) * LANES
                b_in[lane : lane + LANES] = values[54 + j]

    is_first = core[0] == 0
    step = pl.program_id(0)
    for i in range(width // unit):
        here = step == i
        pl.when(here & is_first)(functools.partial(store, own, other, i * unit))
        pl.when(here & ~is_first)(functools.partial(store, other, own, i * unit))
    if smalls:
        pl.when(is_first)(lambda: store_small(own, other))
        pl.when(~is_first)(lambda: store_small(other, own))


def finish(factor, base, width, unit, hid, channels, core, own, other, whole=()):
    vmem = pl.BlockSpec(memory_space=pltpu.VMEM)
    start = base // unit
    outs = [(hid, channels), (channels, hid)]
    smalls = [(7, 7, channels)] + [(channels,)] * 5 + [(hid,)] if whole else []

    def kernel(core, own, other, *refs):
        finish_kernel(factor, width, core, own, other, *refs[len(whole) :])

    return pl.pallas_call(
        kernel,
        grid=(width // unit,),
        out_shape=[jax.ShapeDtypeStruct(shape, f32) for shape in outs + smalls],
        in_specs=[pl.BlockSpec(memory_space=pltpu.SMEM), vmem, vmem]
        + [pl.BlockSpec(memory_space=pl.ANY)] * len(whole),
        out_specs=[
            pl.BlockSpec((unit, channels), lambda i: (start + i, 0)),
            pl.BlockSpec((channels, unit), lambda i: (0, start + i)),
        ]
        + [vmem] * len(smalls),
        input_output_aliases={3: 0, 4: 1} if whole else {},
        compiler_params=pltpu.CompilerParams(vmem_limit_bytes=24 << 20),
    )(core, own, other, *whole)


def shards(
    pages,
    cotangent,
    conv_kernel,
    conv_bias,
    norm_gain,
    norm_bias,
    w_in,
    b_in,
    w_out,
    b_out,
    layer_scale,
):
    _, rows, cols, channels = pages.shape
    hid = w_in.shape[0]
    pixels = rows * cols
    tile = pages.reshape(rows, cols, channels)
    page = pages.reshape(pixels, channels)
    cot = cotangent.reshape(pixels, channels)
    pad = ((channels // LANES, rows + 6, EDGE + cols + 8, LANES), f32)
    full = (pixels, channels)

    even_y = lax.axis_index("gy") % 2 == 0
    even_x = lax.axis_index("gx") % 2 == 0
    core = (lax.axis_index("gy") % 2).astype(jnp.int32).reshape(1)
    mine = (lax.axis_index("gy") // 2 % 2 + lax.axis_index("gx") % 2 * 2).astype(jnp.int32).reshape(1)
    even_y, even_x, core, mine, tile = hold((even_y, even_x, core, mine, tile))
    around = halo(tile, even_y, even_x)
    conv_flops = 2 * 49 * pixels * channels * 60
    normed, inv, ln_out = call(
        conv_norm_kernel,
        [(full, f32), ((pixels, LANES), f32), (full, bf16)],
        [pad, (full, f32)],
        (tile, *around, conv_kernel, conv_bias, norm_gain, norm_bias),
        conv_flops,
    )
    acts = lambda width: [((pixels, width), bf16)] * 2
    packed = lambda width: [((width * channels // LANES, LANES), bf16)] * 2 + [((1, width), f32)]
    core_flip = [("gy", 0)]
    mlp_flops = 12 * pixels * channels * hid
    weights = (w_in, w_out, b_in, layer_scale)
    first, second = hid * 2 // 3, hid // 3
    branch, d_norm, d_branch, keep_a, send_a, gbin_a = call(
        functools.partial(mlp_first_kernel, 0, first),
        [(full, f32), (full, f32), (full, bf16)] + packed(first),
        [
            ((MLP_BLOCK, first), bf16),
            ((MLP_BLOCK, first), bf16),
            ((first, channels), f32),
            ((channels, first), f32),
            ((8, first), f32),
        ],
        (core, ln_out, cot, *weights),
        mlp_flops,
        1,
    )
    other_a = exchange(send_a, core_flip)
    result, d_depth, keep_b, send_b, gbin_b, sums = call(
        functools.partial(mlp_second_kernel, first, second),
        [(full, bf16), (full, bf16)] + packed(second) + [((8, channels), f32)],
        acts(second) + [((8, 8, channels), f32)],
        (core, ln_out, cot, *weights, b_out, norm_gain, page, normed, inv, branch, d_norm, d_branch),
        mlp_flops,
        1,
    )
    d_tile = d_depth.reshape(tile.shape)
    other_a, d_tile, keep_b, send_b = hold((other_a, d_tile, keep_b, send_b))
    parts_a = add_halves(mine, keep_a, other_a)
    got_a = spread(parts_a)
    other_b = exchange(send_b, core_flip)
    d_around = halo(d_tile, even_y, even_x)
    small_rows = ((2 * SMALL, LANES), bf16)
    keep_s, send_s = call(
        kernel_grad_kernel,
        [small_rows, small_rows],
        [pad, (full, f32), ((channels // LANES, 49, 8, LANES), f32)],
        (core, tile, *around, d_tile.reshape(full), sums, gbin_a, gbin_b),
        conv_flops,
        1,
        (parts_a[1],),
    )
    got_a, keep_s, send_s, other_b = hold((got_a, keep_s, send_s, other_b))
    other_s = exchange(send_s, core_flip)
    part_a = add(*got_a)
    parts_b = add_halves(mine, keep_b, other_b, keep_s, other_s)
    flips = [[bit] for bit in beyond()]
    got_a, got_b = exchange(part_a, flips[0]), spread(parts_b)
    got_a, got_b = hold((got_a, got_b))
    part_a, part_b = add(part_a, got_a), add(*got_b)
    (grad_pages,) = call(
        conv_grad_kernel,
        [(full, bf16)],
        [pad, (full, f32)],
        (d_tile, *d_around, conv_kernel, cot),
        conv_flops,
        0,
        (part_a, part_b),
    )
    for ahead, behind in zip(flips[1:], flips):
        got_a, got_b, grad_pages = hold((exchange(part_a, ahead), exchange(part_b, behind), grad_pages))
        part_a, part_b = add(part_a, got_a), add(part_b, got_b)
    got_a, got_b = hold((spread([part_a] * 4), exchange(part_b, flips[-1])))
    half_a, part_b = join(mine, *got_a), add(part_b, got_b)
    got_a, got_b = hold(([half_a, exchange(half_a, core_flip)], spread([part_b] * 4)))
    half_b = join(mine, *got_b)
    got_b = [half_b, exchange(half_b, core_flip)]
    factor = float(pixels * lax.axis_size("gy") * lax.axis_size("gx") * lax.axis_size("rep")) ** (-0.5)
    begun = finish(factor, 0, first, second, hid, channels, core, *got_a)
    win, wout, gk, g_scale, g_bout, g_gain, g_shift, g_bias, g_bin = finish(
        factor, first, second, second, hid, channels, core, *got_b, begun
    )
    return (
        result.reshape(pages.shape),
        grad_pages.reshape(pages.shape),
        gk,
        g_bias,
        g_gain,
        g_shift,
        win,
        g_bin,
        wout,
        g_bout,
        g_scale,
    )


def solution(mesh):
    split = P("rep", "gy", "gx", None)
    return jax.shard_map(
        shards,
        mesh=mesh,
        in_specs=(split, split) + (P(),) * 9,
        out_specs=(split, split) + (P(),) * 9,
        check_vma=False,
    )
```
